128 devices in a mesh: gx: 8 (over y, core), gy: 8 (over x, z_hi), sa: 2 (over z_lo).
Axes of the slice: x: 4, y: 4, z: 4 (z_hi: 2, z_lo: 2; z = z_hi * 2 + z_lo), core: 2. Of those that a mesh axis runs over, the one named last changes fastest.
Arguments:
- fields: float32 [2, 7, 32, 64, 512], P('sa', None, 'gx', 'gy'), may hold values from -6 to 6
- sources: float32 [2, 7, 32, 64, 512], P('sa', None, 'gx', 'gy'), may hold values from -5 to 5
- diagonal: float32 [7, 32, 64, 512], P(None, 'gx', 'gy'), may hold values from 0.25 to 2
- block_inverse: float32 [7, 7, 32, 64, 512], P(None, None, 'gx', 'gy'), may hold values from -0.035 to 0.14
- coupling: float32 [7], replicated, may hold values from 0.25 to 0.75
- donors: int32 [64, 3], replicated, may hold values from 0 to 895, as said below
- returns: int32 [8, 896], P('gy'), may hold values from 0 to 63
Outputs:
- fields_out: float32 [2, 7, 32, 64, 512], P('sa', None, 'gx', 'gy')
The draws below stay inside these ranges and needn't reach their ends.
Inputs may be any that keep to these rules, and one draw needn't show every extreme that they name: `donors`: column 0 is a gy position, column 1 a block index on that position's exit face, column 2 the inflow slot filled; column 2 is a permutation of 0 to 63.
All inputs are finite; a program needn't handle non-finite values.
Results may differ from the reference program's by a relative error of at most 0.00002.
Values sent between devices are 32-bit elements; how exact they have to be, the bound alone decides.
No kernel may reach another device: no remote copies, remote signals or barrier semaphores. Data moves between devices by JAX's collectives and lax.ppermute only.
A program may use at most 128 MiB of HBM per device.

```python
import math
import jax
import jax.numpy as jnp

STATES = 7
SWEEPS = 4
BLK = 32
CX = 4
CY = 8
NX = 32
NY = 64
NZ = 512
SLOTS = 1
EXIT_FACE_BLOCKS = 896
INFLOW_SLOTS = 64
N_GX = 8
N_GY = 8


def draw_donors(key, part):
    key = jax.random.fold_in(key, 5)
    key_source, key_block, key_target = jax.random.split(key, 3)
    slot_total = N_GX * N_GY * SLOTS
    anchor = jax.random.randint(key_source, (slot_total,), 0, N_GY, dtype=jnp.int32)
    blocks = jax.random.randint(key_block, (slot_total,), 0, EXIT_FACE_BLOCKS, dtype=jnp.int32).at[0].set(EXIT_FACE_BLOCKS - 1)
    targets = jax.random.permutation(key_target, slot_total).astype(jnp.int32)
    return jnp.stack([anchor, blocks, targets], axis=1).astype(jnp.int32)


def draw_block_inverse(key, part):
    key = jax.random.fold_in(key, 7)
    diagonal_key, key_off = jax.random.split(key)
    full_shape = (STATES, STATES, NX, NY, NZ)
    identity = jnp.eye(STATES, dtype=jnp.float32)[:, :, None, None, None]
    leading = jax.random.uniform(diagonal_key, full_shape, jnp.float32, 0.1, 0.14)
    coupled = jnp.clip(0.012 * jax.random.normal(key_off, full_shape, jnp.float32), -0.035, 0.035)
    return identity * leading + (1.0 - identity) * coupled


def draw_sources(key, part):
    key = jax.random.fold_in(key, 9)
    full_shape = (2, STATES, NX, NY, NZ)
    return jnp.clip(jax.random.normal(key, full_shape, jnp.float32), -5.0, 5.0)


def place_ends(values, stream_key, low, top_value):
    shape = values.shape
    place = [jax.random.randint(jax.random.fold_in(stream_key, axis), (), 0, shape[axis]) for axis in range(len(shape))]
    values = values.at[tuple(place)].set(low)
    longest = shape.index(max(shape))
    place[longest] = (place[longest] + 1) % shape[longest]
    return values.at[tuple(place)].set(top_value)


def block_levels(key, shape, cuts, low, high):
    level = 1.0
    for position, parts in cuts:
        steps = jax.random.uniform(jax.random.fold_in(jax.random.fold_in(key, 6), position), (parts,), jnp.float32, low / len(cuts), high / len(cuts))
        level = level * jnp.repeat(jnp.exp(steps), shape[position] // parts).reshape((-1,) + (1,) * (len(shape) - 1 - position))
    return level


def noise(key, shape, width, most, cuts=(), kind=jnp.bfloat16):
    entries = jax.random.normal(key, shape, jnp.float32) * width
    if len(cuts) > 0:
        entries = block_levels(key, shape, cuts, -0.22, 0.18) * entries
    return jnp.clip(entries, min=-most, max=most).astype(kind)


def setup_inputs(seed: int = 0) -> dict:
    streams_of = jax.random.split(jax.random.key(seed), 8)
    fields = noise(streams_of[0], (2, STATES, NX, NY, NZ), 1.0, 6.0, ((0, 2), (2, 8), (3, 8)), jnp.float32)
    sources = draw_sources(jax.random.fold_in(streams_of[7], 71), 0)
    diagonal = jnp.clip(0.25 + 1.75 * jax.random.uniform(streams_of[2], (STATES, NX, NY, NZ), jnp.float32) ** block_levels(streams_of[2], (STATES, NX, NY, NZ), ((1, 8), (2, 8)), -0.2, 0.2), 0.25, 2.0)
    block_inverse = draw_block_inverse(jax.random.fold_in(streams_of[7], 71), 0)
    coupling = jnp.clip(jnp.exp(jax.random.uniform(streams_of[4], (STATES,), jnp.float32, math.log(0.25), math.log(0.75))), 0.25, 0.75)
    donors = draw_donors(jax.random.fold_in(streams_of[7], 71), 0)
    returns = place_ends(jax.random.randint(streams_of[6], (N_GY, EXIT_FACE_BLOCKS), 0, INFLOW_SLOTS), jax.random.fold_in(streams_of[6], 1), 0, INFLOW_SLOTS - 1).astype(jnp.int32)
    return dict(fields=fields, sources=sources, diagonal=diagonal, block_inverse=block_inverse, coupling=coupling, donors=donors, returns=returns)


def z_terms_combustor(values):
    blank_cap = jnp.zeros_like(values[:1, :, :, :1])
    upper_cap = jnp.concatenate([values[1:, :, :, :1], blank_cap], axis=0)
    lower_cap = jnp.concatenate([blank_cap, values[:-1, :, :, -1:]], axis=0)
    upper_terms = jnp.concatenate([values[:, :, :, 1:], upper_cap], axis=3)
    lower_terms = jnp.concatenate([lower_cap, values[:, :, :, :-1]], axis=3)
    return upper_terms, lower_terms


def z_terms_turbine(values, inflow):
    upper_cap = jnp.zeros_like(values[:, :, :, :1])
    lower_cap = jnp.concatenate([inflow[None, :, :, None], values[1:, :, :, :1]], axis=0)
    upper_terms = jnp.concatenate([values[:, :, :, 1:], upper_cap], axis=3)
    lower_terms = jnp.concatenate([lower_cap, values[:, :, :, :-1]], axis=3)
    return upper_terms, lower_terms


def neighbour_sum(padded, upper_terms, lower_terms):
    summed = padded[:, 2:, 1:-1] + padded[:, :-2, 1:-1]
    summed = summed + padded[:, 1:-1, 2:] + padded[:, 1:-1, :-2]
    return summed + upper_terms + lower_terms


def apply_inverse(block_inverse, driving):
    result = block_inverse[:, 0] * driving[0]
    for column in range(1, driving.shape[0]):
        result = result + block_inverse[:, column] * driving[column]
    return result


def reference(fields, sources, diagonal, block_inverse, coupling, donors, returns):
    combustor = fields[0]
    turbine = fields[1]
    slot_total = N_GX * N_GY * SLOTS
    inlet_blocks = turbine[0, :, :, 0].reshape(N_GX, CX, N_GY, CY).transpose(0, 2, 1, 3).reshape(slot_total, BLK)
    exit_blocks = combustor[:, NX - 1].reshape(STATES, N_GY, CY, NZ).transpose(1, 0, 2, 3).reshape(N_GY, EXIT_FACE_BLOCKS, BLK)
    filled = jnp.zeros((slot_total, BLK), jnp.float32).at[donors[:, 2]].set(exit_blocks[donors[:, 0], donors[:, 1]])
    inflow = filled.reshape(N_GX, N_GY, CX, CY).transpose(0, 2, 1, 3).reshape(NX, NY)
    pressure_back = inlet_blocks[returns].reshape(N_GY, STATES, CY, NZ).transpose(1, 0, 2, 3).reshape(STATES, NY, NZ)
    parity = (jnp.arange(NX)[:, None, None] + jnp.arange(NY)[None, :, None] + jnp.arange(NZ)[None, None, :]) % 2
    divisor = 6.0 + diagonal
    weights = coupling[:, None, None, None]
    widths = ((0, 0), (1, 1), (1, 1), (0, 0))
    for sweep_index in range(SWEEPS):
        for colour in (0, 1):
            padded = jnp.pad(combustor, widths)
            padded = padded.at[:, -1, 1:-1, :].set(pressure_back)
            upper_terms, lower_terms = z_terms_combustor(combustor)
            updated = (sources[0] + neighbour_sum(padded, upper_terms, lower_terms)) / divisor
            combustor = jnp.where(parity == colour, updated, combustor)
            padded = jnp.pad(turbine, widths)
            upper_terms, lower_terms = z_terms_turbine(turbine, inflow)
            driving = sources[1] + weights * neighbour_sum(padded, upper_terms, lower_terms)
            updated = apply_inverse(block_inverse, driving)
            turbine = jnp.where(parity == colour, updated, turbine)
    return jnp.stack([combustor, turbine])
```

```python
import functools
import jax
import jax.numpy as jnp
import numpy as np
from jax import lax
from jax.experimental import pallas as pl
from jax.experimental.pallas import tpu as pltpu
from jax.sharding import PartitionSpec as P

SWEEPS = 4
BLK = 32
T = 7
CX = 4
CY = 8
NZ = 512
ZT = 128
VAL = T * NZ
MSG = VAL + T * ZT
COEF = T * T + T
BULK = COEF // 4
F32 = jnp.float32


def iotas(width):
    sub = lax.broadcasted_iota(jnp.int32, (8, width), 0)
    lane = lax.broadcasted_iota(jnp.int32, (8, width), 1)
    return sub, lane


def even_mask(width):
    sub, lane = iotas(width)
    return (sub + lane) % 2 == 0


def roll(array, shift, axis):
    size = array.shape[axis]
    shift = shift % size
    return array if shift == 0 else pltpu.roll(array, shift, axis)


def packed(pair_low, pair_high, even, colour):
    return jnp.where(even, pair_low, pair_high) if colour == 0 else jnp.where(even, pair_high, pair_low)


def store_message(ref, ones, zeros_first):
    for t in range(T):
        ref[:, t * NZ : (t + 1) * NZ] = ones(t)
        ref[:, VAL + t * ZT : VAL + (t + 1) * ZT] = zeros_first(t)


def first_kernel(place, fields, m1, m2):
    odd = place[1]
    even, even_z = even_mask(NZ), even_mask(ZT)
    for ref, pair in ((m1, 1 - odd), (m2, odd)):
        store_message(
            ref,
            lambda t: packed(fields[t, 2 * pair], fields[t, 2 * pair + 1], even, 1),
            lambda t: packed(fields[t, 2 * pair, :, :ZT], fields[t, 2 * pair + 1, :, :ZT], even_z, 0),
        )


def coefficient(section, sources, diagonal, inverse, index, plane):
    if index >= T * T:
        return sources[index - T * T, plane]
    raw = inverse[index // T, index % T, plane]
    return jnp.where(section == 0, diagonal[index, plane], raw) if index < T else raw


def bulk_kernel(place, sources, diagonal, inverse, x1, x2, low, high):
    section, odd = place[0], place[1]
    even = even_mask(NZ)
    sub, _ = iotas(NZ)
    for index in range(COEF):
        x1[index] = coefficient(section, sources, diagonal, inverse, index, (1 - odd) * (CX - 1))
        x2[index] = coefficient(section, sources, diagonal, inverse, index, odd * (CX - 1))
    for tile in range(BULK):
        rows_low = jnp.zeros((8, NZ), F32)
        rows_high = jnp.zeros((8, NZ), F32)
        for j in range(4):
            index = 4 * tile + j
            for k in (0, 1):
                plane = packed(
                    coefficient(section, sources, diagonal, inverse, index, 2 * k),
                    coefficient(section, sources, diagonal, inverse, index, 2 * k + 1),
                    even,
                    0,
                )
                here = sub == 2 * j + k
                rows_low = jnp.where(here, roll(plane, 2 * j + k, 0), rows_low)
                rows_high = jnp.where(here, roll(plane, 2 * j + k - 7, 0), rows_high)
        low[:, tile * NZ : (tile + 1) * NZ] = rows_low
        high[:, tile * NZ : (tile + 1) * NZ] = rows_high


def corner_kernel(with_bulk, place, m1, m2, r1, r2, *rest):
    odd_x, odd_y = place[1] == 1, place[2] == 1
    if with_bulk:
        low, high, marks_low, marks_high, y1, y2 = rest
    else:
        y1, y2 = rest
    sub, _ = iotas(ZT)
    for tile in range(MSG // ZT):
        at = slice(tile * ZT, (tile + 1) * ZT)
        a, b, c, d = m1[:, at], m2[:, at], r1[:, at], r2[:, at]
        own_low, own_high = jnp.where(odd_x, a, b), jnp.where(odd_x, b, a)
        from_low, from_high = jnp.where(odd_x, c, d), jnp.where(odd_x, d, c)

        def rows(start):
            parts = [from_low, own_low, own_high, from_high]
            shifted = [roll(part, 2 * p - start, 0) for p, part in enumerate(parts)]
            halves = [jnp.where(sub < 2, shifted[0], shifted[1]), jnp.where(sub < 6, shifted[2], shifted[3])]
            return jnp.where(sub < 4, halves[0], halves[1])

        down, up = rows(0), rows(6)
        y1[:, at] = jnp.where(odd_y, down, up)
        y2[:, at] = jnp.where(odd_y, up, down)
    if with_bulk:
        for tile in range(BULK * NZ // ZT):
            at = slice(tile * ZT, (tile + 1) * ZT)
            to = slice(MSG + tile * ZT, MSG + (tile + 1) * ZT)
            down, up = low[:, at], high[:, at]
            y1[:, to] = jnp.where(odd_y, down, up)
            y2[:, to] = jnp.where(odd_y, up, down)
        end = MSG + BULK * NZ
        y1[:, end:] = jnp.where(odd_y, marks_low[...], marks_high[...])
        y2[:, end:] = jnp.where(odd_y, marks_high[...], marks_low[...])


def interface_kernel(place, blocks, marks, marks1, marks2, chosen, back, inflow):
    odd_y = place[2] == 1
    exit_side = place[3] == 1
    back[...] = jnp.zeros_like(back)
    total = jnp.sum(blocks[...], axis=0, keepdims=True)
    for row in range(16):
        at = slice(8 * row, 8 * row + 8)
        inflow[at, :] = jnp.broadcast_to(jnp.sum(chosen[at, :] * total, axis=1, keepdims=True), (8, ZT))

    @pl.when(exit_side)
    def _():
        table = blocks[:, :ZT]
        first = jnp.where(odd_y, marks2[...], marks1[...])
        second = jnp.where(odd_y, marks1[...], marks2[...])
        _, lane_blocks = iotas(ZT)
        column = lax.broadcasted_iota(jnp.int32, table.shape, 1)
        spots = [
            jnp.where(column // BLK == q, roll(table, q * BLK, 1), 0.0) for q in range(ZT // BLK)
        ]
        wanted = [marks[t] for t in range(T)] + [first, second]
        for group, want in enumerate(wanted):
            for tile in range(NZ // ZT):
                laid = jnp.zeros((8, ZT), F32)
                for q in range(ZT // BLK):
                    block = tile * (ZT // BLK) + q
                    match = want[:, block : block + 1] * 2.0 + 1.0 == lane_blocks.astype(F32)
                    laid = laid + jnp.dot(
                        match.astype(F32), spots[q], precision=lax.Precision.HIGHEST, preferred_element_type=F32
                    )
                at = slice(tile * ZT, (tile + 1) * ZT)
                if group < T:
                    back[group, 0:8, at] = laid
                else:
                    row = 8 if group == T else 15
                    for t in range(T):
                        back[t, row : row + 1, at] = laid[t : t + 1, :]


def sweep_kernel(
    place, coupling, fields, sources, diagonal, inverse, r1, r2, x1, x2, y1, y2, yb, zb, back, inflow, out, m1, m2, u0, u1
):
    section = place[0]
    odd_x, odd_y = place[1], place[2]
    exit_side = place[3] == 1
    even, even_z = even_mask(NZ), even_mask(ZT)
    sub, lane = iotas(NZ)
    sub_z, _ = iotas(ZT)
    colours = (u0, u1)
    own, edge = slice(0, 8), slice(8, 16)

    for t in range(T):
        for k in (0, 1):
            u1[t, k + 1, own] = packed(fields[t, 2 * k], fields[t, 2 * k + 1], even, 1)
            u0[t, k + 1, own] = packed(fields[t, 2 * k], fields[t, 2 * k + 1], even, 0)
        for ref, at, width in (
            (u1, slice(t * NZ, (t + 1) * NZ), NZ),
            (u0, slice(VAL + t * ZT, VAL + (t + 1) * ZT), ZT),
        ):
            low, high = jnp.where(odd_x == 1, r1[:, at], r2[:, at]), jnp.where(odd_x == 1, r2[:, at], r1[:, at])
            ref[t, 0, own, :width] = low
            ref[t, 3, own, :width] = high
            low, high = jnp.where(odd_y == 1, y1[:, at], y2[:, at]), jnp.where(odd_y == 1, y2[:, at], y1[:, at])
            rows = lax.broadcasted_iota(jnp.int32, (8, width), 0)
            for p in range(4):
                ref[t, p, edge, :width] = jnp.where(rows < 2, roll(high, -2 * p, 0), roll(low, 6 - 2 * p, 0))

    @pl.when(exit_side)
    def _():
        for t in range(T):
            u0[t, 3] = back[t]
            u1[t, 3] = back[t]

    def around(centre, beyond):
        up = roll(jnp.where(sub == 0, beyond, centre), -1, 0)
        down = roll(jnp.where(sub == 7, beyond, centre), 1, 0)
        return up + down

    def planes(colour, unit, t):
        old, new = colours[colour], colours[1 - colour]
        if unit == "ring":
            centre = jnp.where(even, new[t, 0, own], new[t, 3, own])
            beyond = jnp.where(even, new[t, 0, edge], new[t, 3, edge])
            x_sum = jnp.where(even, new[t, 3, own] + new[t, 2, own], new[t, 0, own] + new[t, 1, own])
            return centre, beyond, x_sum, jnp.where(even, old[t, 3, own], old[t, 0, own])
        p, rows = unit
        here, other = (own, edge) if rows == 0 else (edge, own)
        centre, beyond = new[t, p, here], new[t, p, other]
        below, above = new[t, p - 1, here], new[t, p + 1, here]
        x_sum = centre + (jnp.where(even, below, above) if colour == 0 else jnp.where(even, above, below))
        return centre, beyond, x_sum, old[t, p, here]

    def inflow_of(colour, unit):
        base = 64 * colour
        if unit == "ring":
            values = jnp.where(even_z, inflow[base + 48 : base + 56], inflow[base : base + 8])
        else:
            start = base + 16 * unit[0] + 8 * unit[1]
            values = inflow[start : start + 8]
        return jnp.concatenate([values] * (NZ // ZT), axis=1)

    ring_mask = (sub + lane + odd_x) % 2 == 0
    edge_mask = jnp.where(sub == 7, 1, 0) == odd_y

    def taken(colour, unit, index, raw):
        if unit == "ring":
            return jnp.where(ring_mask, x1[index], x2[index])
        p, rows = unit
        if rows == 0:
            return packed(raw[2 * p - 2], raw[2 * p - 1], even, colour)
        at = slice((index // 4) * NZ, (index // 4 + 1) * NZ)
        row = 2 * (index % 4) + p - 1
        return jnp.where(edge_mask, yb[row : row + 1, at], zb[row : row + 1, at])

    def put(colour, unit, t, value):
        ref = colours[colour]
        if unit == "ring":
            ref[t, 0, own] = value
            ref[t, 3, own] = jnp.where(exit_side, back[t, own], value)
        else:
            ref[t, unit[0], own if unit[1] == 0 else edge] = value

    def valid(unit):
        if unit == "ring":
            return jnp.where(even, place[5], place[4])
        if unit[1] == 0:
            return None
        return jnp.where(sub == 7, place[6], place[7])

    def turbine(colour, unit):
        driving = []
        for t in range(T):
            centre, beyond, x_sum, kept = planes(colour, unit, t)
            start = inflow_of(colour, unit) if t == 0 else kept
            ahead = jnp.where(lane == NZ - 1, 0.0, roll(centre, -1, 1))
            behind = jnp.where(lane == 0, start, roll(centre, 1, 1))
            total = x_sum + around(centre, beyond) + ahead + behind
            source = taken(colour, unit, T * T + t, sources.at[t])
            driving.append(source + coupling[t] * total)
        for s in range(T):
            value = taken(colour, unit, T * s, inverse.at[s, 0]) * driving[0]
            for t in range(1, T):
                value = value + taken(colour, unit, T * s + t, inverse.at[s, t]) * driving[t]
            put(colour, unit, s, value)

    def combustor(colour, unit):
        before = None
        current = planes(colour, unit, 0)
        flag = valid(unit)
        for t in range(T):
            after = planes(colour, unit, t + 1) if t + 1 < T else None
            centre, beyond, x_sum, _ = current
            edge_ahead = 0.0 if after is None else roll(after[0], -1, 1)
            edge_behind = 0.0 if before is None else roll(before, 1, 1)
            ahead = jnp.where(lane == NZ - 1, edge_ahead, roll(centre, -1, 1))
            behind = jnp.where(lane == 0, edge_behind, roll(centre, 1, 1))
            total = x_sum + around(centre, beyond) + ahead + behind
            source = taken(colour, unit, T * T + t, sources.at[t])
            value = (source + total) / (6.0 + taken(colour, unit, t, diagonal.at[t]))
            if flag is not None:
                value = jnp.where(flag == 1, value, 0.0)
            put(colour, unit, t, value)
            before, current = centre, after

    def both(step):
        for unit in ((1, 0), (2, 0), (1, 1), (2, 1), "ring"):
            step(0, unit)
        for unit in ((1, 0), (2, 0)):
            step(1, unit)

    pl.when(section == 0)(functools.partial(both, combustor))
    pl.when(section != 0)(functools.partial(both, turbine))

    for t in range(T):
        for k in (0, 1):
            a, b = u0[t, k + 1, own], u1[t, k + 1, own]
            out[t, 2 * k] = jnp.where(even, a, b)
            out[t, 2 * k + 1] = jnp.where(even, b, a)
    for ref, pair in ((m1, 2 - odd_x), (m2, 1 + odd_x)):
        store_message(ref, lambda t: u1[t, pair, own], lambda t: u0[t, pair, own, :ZT])


def shape(*dims):
    return jax.ShapeDtypeStruct(dims, F32)


def call(kernel, outs, scalars, arrays, scratch=(), limit=24, cost=None):
    smem, vmem = (pl.BlockSpec(memory_space=pltpu.SMEM), pl.BlockSpec(memory_space=pltpu.VMEM))
    return pl.pallas_call(
        kernel,
        out_shape=outs,
        in_specs=[smem] * len(scalars) + [vmem] * len(arrays),
        out_specs=[vmem] * len(outs),
        scratch_shapes=list(scratch),
        compiler_params=pltpu.CompilerParams(vmem_limit_bytes=limit << 20),
        cost_estimate=cost,
    )(*scalars, *arrays)


def swaps(axis, first, second):
    peers = lax.axis_size(axis)
    inner = [(i, i ^ 1) for i in range(peers)]
    outer = [(i, (i + 1 ^ 1) - 1) for i in range(1, peers - 1)]
    return lax.ppermute(first, axis, inner), lax.ppermute(second, axis, outer)


def chosen_slots():
    table = np.zeros((128, 2 * ZT), np.float32)
    for c in range(2):
        for p in range(4):
            for r in range(16):
                y = r if r < 12 else r - 16
                x = 2 * (p - 1) + (c if r % 2 == 0 else 1 - c)
                block = None
                if 0 <= x < CX and 0 <= y < CY:
                    block = (0, x, y)
                elif x == -1 and 0 <= y < CY:
                    block = (1, CX - 1, y)
                elif x == CX and 0 <= y < CY:
                    block = (2, 0, y)
                elif 0 <= x < CX and y == -1:
                    block = (3, x, CY - 1)
                elif 0 <= x < CX and y == CY:
                    block = (4, x, 0)
                if block is not None:
                    table[64 * c + 16 * p + r, BLK * block[0] + CY * block[1] + block[2]] = 1.0
    return table


def shards(fields, sources, diagonal, block_inverse, coupling, donors, returns):
    values = fields[0]
    source = sources[0]
    rows_x, rows_y = lax.axis_size("gx"), lax.axis_size("gy")
    cells = rows_x * rows_y
    section, place_x, place_y = (lax.axis_index(axis) for axis in ("sa", "gx", "gy"))
    exit_side = (section == 0) & (place_x == rows_x - 1)
    place = jnp.stack(
        [
            section,
            place_x % 2,
            place_y % 2,
            exit_side.astype(jnp.int32),
            (place_x > 0).astype(jnp.int32),
            (place_x < rows_x - 1).astype(jnp.int32),
            (place_y > 0).astype(jnp.int32),
            (place_y < rows_y - 1).astype(jnp.int32),
        ]
    ).astype(jnp.int32)

    m1, m2 = call(first_kernel, [shape(8, MSG)] * 2, [place], [values])
    r1, r2 = swaps("gx", m1, m2)

    x1, x2, low, high = call(
        bulk_kernel,
        [shape(COEF, 8, NZ)] * 2 + [shape(8, BULK * NZ)] * 2,
        [place],
        [source, diagonal, block_inverse],
    )
    x1, x2 = swaps("gx", x1, x2)

    marks = returns[0].astype(F32).reshape(T, CY, NZ // BLK)
    marks = jnp.pad(marks, ((0, 0), (0, 0), (0, ZT - NZ // BLK)))
    marks_low, marks_high = (jnp.pad(marks[:, row], ((0, 1), (0, 0))) for row in (0, CY - 1))
    full = MSG + BULK * NZ + ZT
    y1, y2 = call(
        functools.partial(corner_kernel, True),
        [shape(8, full)] * 2,
        [place],
        [m1, m2, r1, r2, low, high, marks_low, marks_high],
    )
    y1, y2 = swaps("gy", y1, y2)

    matches = donors[None, :, 2] == jnp.arange(cells, dtype=jnp.int32)[:, None]
    slot_source = jnp.sum(jnp.where(matches, donors[None, :, 0], 0), axis=1)
    slot_block = jnp.sum(jnp.where(matches, donors[None, :, 1], 0), axis=1)
    exit_face = values[:, CX - 1].reshape(-1, BLK)
    sending = exit_side & (slot_source == place_y)
    downward = jnp.where(sending[:, None], jnp.take(exit_face, slot_block, axis=0), 0.0)
    downward = jnp.pad(downward.reshape(rows_x, rows_y, BLK), ((1, 1), (1, 1), (0, 0)))
    five = [downward[1:-1, 1:-1], downward[:-2, 1:-1], downward[2:, 1:-1], downward[1:-1, :-2], downward[1:-1, 2:]]
    downward = jnp.pad(jnp.concatenate(five, axis=2).reshape(cells, 5 * BLK), ((0, 0), (0, 2 * ZT - 5 * BLK)))
    inlet = jnp.where(section == 1, values[0, :, :, 0].reshape(1, BLK), 0.0)
    upward = jnp.broadcast_to(jnp.pad(inlet, ((0, 0), (0, 2 * ZT - BLK))), (cells, 2 * ZT))
    outgoing = jnp.stack([upward, downward], axis=1).reshape(2 * cells, 2 * ZT)
    blocks = lax.all_to_all(outgoing, ("gx", "gy", "sa"), split_axis=0, concat_axis=0, tiled=True)
    if blocks.shape[0] < ZT:
        blocks = jnp.pad(blocks, ((0, ZT - blocks.shape[0]), (0, 0)))
    end = MSG + BULK * NZ
    back, inflow = call(
        interface_kernel,
        [shape(T, 16, NZ), shape(128, ZT)],
        [place],
        [blocks, marks, y1[:, end:], y2[:, end:], jnp.asarray(chosen_slots())],
    )

    yb, zb = y1[:, MSG:end], y2[:, MSG:end]
    y1, y2 = y1[:, :MSG], y2[:, :MSG]
    for sweep in range(SWEEPS):
        if sweep > 0:
            r1, r2 = swaps("gx", m1, m2)
            y1, y2 = call(functools.partial(corner_kernel, False), [shape(8, MSG)] * 2, [place], [m1, m2, r1, r2])
            y1, y2 = swaps("gy", y1, y2)
        values, m1, m2 = call(
            sweep_kernel,
            [shape(T, CX, CY, NZ), shape(8, MSG), shape(8, MSG)],
            [place, coupling],
            [values, source, diagonal, block_inverse, r1, r2, x1, x2, y1, y2, yb, zb, back, inflow],
            [pltpu.VMEM((T, 4, 16, NZ), F32)] * 2,
            40,
        )
    return values[None]


def solution(mesh):
    return jax.shard_map(
        shards,
        mesh=mesh,
        in_specs=(
            P("sa", None, "gx", "gy", None),
            P("sa", None, "gx", "gy", None),
            P(None, "gx", "gy", None),
            P(None, None, "gx", "gy", None),
            P(),
            P(),
            P("gy", None),
        ),
        out_specs=P("sa", None, "gx", "gy", None),
        check_vma=False,
    )
```

```python
import functools
import jax
import jax.numpy as jnp
import numpy as np
from jax import lax
from jax.experimental import pallas as pl
from jax.experimental.pallas import tpu as pltpu
from jax.sharding import PartitionSpec as P

SWEEPS = 4
BLK = 32
T = 7
CX = 4
CY = 8
NZ = 512
ZT = 128
VAL = T + 2
COEF = T * T + T
XBULK = COEF // 2
YVAL = 5
YHEAD = YVAL + 4
YBULK = T * T // 4 + 1
F32 = jnp.float32


def iotas(width):
    sub = lax.broadcasted_iota(jnp.int32, (8, width), 0)
    lane = lax.broadcasted_iota(jnp.int32, (8, width), 1)
    return sub, lane


def even_mask(width):
    sub, lane = iotas(width)
    return (sub + lane) % 2 == 0


def roll(array, shift, axis):
    size = array.shape[axis]
    shift = shift % size
    return array if shift == 0 else pltpu.roll(array, shift, axis)


def packed(pair_low, pair_high, even, colour):
    return jnp.where(even, pair_low, pair_high) if colour == 0 else jnp.where(even, pair_high, pair_low)


def store_message(ref, ones, zeros_first):
    for t in range(T):
        ref[t] = ones(t)
        ref[T + t // 4, :, (t % 4) * ZT : (t % 4 + 1) * ZT] = zeros_first(t)
    ref[T + 1, :, 3 * ZT :] = jnp.zeros((8, ZT), F32)


def wait_for(copies):
    for copy in copies:
        copy.wait()


def lines(ref, index, row):
    found = [ref[pl.ds(128 * index + 8 * z + row, 8, stride=32), :] for z in range(NZ // ZT)]
    return jnp.concatenate(found, axis=1)


def second_half(array):
    return roll(array, 4, 0)


def row_of_colour_0(raw, row, lane):
    return jnp.where((lane + row) % 2 == 0, raw, roll(raw, -1, 0))


def interleaved(first, second, sub):
    return jnp.where(sub % 2 == 0, first, roll(second, 1, 0))


def opening_kernel(
    place, donors, fields, sources, diagonal, inverse, m1, m2, b1, b2, payload, blocks, coef, inv, sems
):
    section, odd, place_y, odd_y = place[0], place[1], place[9], place[2] == 1
    exit_side = place[3] == 1
    loads = [
        pltpu.make_async_copy(sources, coef.at[0], sems.at[0]),
        pltpu.make_async_copy(diagonal, coef.at[1], sems.at[1]),
        pltpu.make_async_copy(inverse, inv, sems.at[2]),
    ]
    for load in loads:
        load.start()
    even, even_z = even_mask(NZ), even_mask(ZT)
    for ref, pair in ((m1, 1 - odd), (m2, odd)):
        store_message(
            ref,
            lambda t: packed(fields[t, 2 * pair], fields[t, 2 * pair + 1], even, 1),
            lambda t: packed(fields[t, 2 * pair, :, :ZT], fields[t, 2 * pair + 1, :, :ZT], even_z, 0),
        )

    sub, lane = iotas(ZT)
    payload[...] = jnp.zeros_like(payload)
    cells = blocks.shape[0]

    @pl.when(exit_side)
    def _():
        for entry in range(cells):
            gy, block, slot = donors[3 * entry], donors[3 * entry + 1], donors[3 * entry + 2]
            piece, row, column = block // 128, block % 128 // 16, block % 16
            start = pl.multiple_of(column // 4 * ZT, ZT)
            found = fields[piece, CX - 1, :, pl.ds(start, ZT)]
            found = pltpu.roll(pltpu.roll(found, (8 - row) % 8, 0), (ZT - column % 4 * BLK) % ZT, 1)
            blocks[pl.ds(slot, 1), :] = jnp.where((lane < BLK) & (gy == place_y), found, 0.0)[:1]
        tiles = cells // 8
        zero = jnp.zeros((8, ZT), F32)
        for tile in range(tiles):
            here = blocks[8 * tile : 8 * tile + 8]
            below = blocks[8 * tile - 8 : 8 * tile] if tile > 0 else zero
            above = blocks[8 * tile + 8 : 8 * tile + 16] if tile + 1 < tiles else zero
            left = jnp.where(sub == 0, 0.0, roll(here, 1, 0))
            right = jnp.where(sub == 7, 0.0, roll(here, -1, 0))
            wide = here + roll(below, BLK, 1) + roll(above, 2 * BLK, 1) + roll(left, 3 * BLK, 1)
            payload[pl.ds(2 * cells + 16 * tile, 8, stride=2), :] = wide
            payload[pl.ds(2 * cells + 16 * tile + 1, 8, stride=2), :] = right

    @pl.when(section == 1)
    def _():
        inlet = jnp.zeros((8, ZT), F32)
        for x in range(CX):
            column = jnp.broadcast_to(fields[0, x, :, 0:1], (8, ZT))
            inlet = inlet + jnp.where(lane == CY * x + sub, column, 0.0)
        inlet = jnp.broadcast_to(jnp.sum(inlet, axis=0, keepdims=True), (8, ZT))
        for tile in range(cells // 8):
            payload[pl.ds(16 * tile, 8, stride=2), :] = inlet

    wait_for(loads)
    sub, lane = iotas(NZ)

    def plane_of(ref, index, plane):
        at = [pl.multiple_of(8 * (4 * (CX * index + plane) + z), 8) for z in range(NZ // ZT)]
        return jnp.concatenate([ref[pl.ds(start, 8), :] for start in at], axis=1)

    def coefficient(index, plane):
        if index >= T * T:
            return plane_of(coef.at[0], index - T * T, plane)
        raw = plane_of(inv, index, plane)
        return jnp.where(section == 0, plane_of(coef.at[1], index, plane), raw) if index < T else raw

    for ref, far in ((m1, 1 - odd), (m2, odd)):
        wanted = (sub + lane + far) % 2 == 0
        plane = far * (CX - 1)
        for tile in range(XBULK):
            first, second = coefficient(2 * tile, plane), coefficient(2 * tile + 1, plane)
            ref[VAL + tile] = jnp.where(wanted, first, roll(second, 1, 0))

    for tile in range(YBULK):
        sides = []
        for row in (0, CY - 1):
            if tile + 1 < YBULK:
                first, second = (row_of_colour_0(lines(inv, 4 * tile + 2 * n, row), row, lane) for n in (0, 1))
                sides.append(interleaved(first, second, sub))
            else:
                sides.append(row_of_colour_0(second_half(lines(inv, T * T - 2, row)), row, lane))
        down, up = sides
        b1[tile] = jnp.where(odd_y, down, up)
        b2[tile] = jnp.where(odd_y, up, down)


def corner_values(place, m1, m2, r1, r2, y1, y2):
    odd_x, odd_y = place[1] == 1, place[2] == 1
    sub, lane = iotas(NZ)
    even = even_mask(NZ)
    tiles = {}
    for t in range(VAL):
        a, b = m1[t], m2[t]
        own = jnp.where(odd_x, a, b), jnp.where(odd_x, b, a)
        for start in (0, 6):
            if t < T:
                base = 4 * (t % 2)
                rows = [roll(own[k], base + 2 * k - start, 0) for k in (0, 1)]
                both = jnp.where(sub < base + 2, rows[0], rows[1])
                tiles[start, t] = both
                c, d = r1[t], r2[t]
                from_low, from_high = jnp.where(odd_x, c, d), jnp.where(odd_x, d, c)
                ring = jnp.where(even, from_low, from_high)
                tiles[start, "ring", t] = roll(ring, t - (0 if start == 0 else CY - 1), 0)
            else:
                row = 0 if start == 0 else CY - 1
                rows = [roll(own[k], 4 + 2 * k + t - T - row, 0) for k in (0, 1)]
                tiles[start, t] = jnp.where(sub < 6, rows[0], rows[1])
    for tile in range(YVAL):
        sides = []
        for start in (0, 6):
            if tile < 3:
                sides.append(jnp.where(sub < 4, tiles[start, 2 * tile], tiles[start, 2 * tile + 1]))
            elif tile == 3:
                firsts = jnp.where(sub % 2 == 0, tiles[start, T], tiles[start, T + 1])
                sides.append(jnp.where(sub < 4, tiles[start, T - 1], firsts))
            else:
                laid = tiles[start, "ring", 0]
                for t in range(1, T):
                    laid = jnp.where(sub == t, tiles[start, "ring", t], laid)
                sides.append(laid)
        down, up = sides
        y1[tile] = jnp.where(odd_y, down, up)
        y2[tile] = jnp.where(odd_y, up, down)


def corner_kernel(place, m1, m2, r1, r2, y1, y2):
    corner_values(place, m1, m2, r1, r2, y1, y2)


def first_corner_kernel(place, m1, m2, r1, r2, returns, sources, diagonal, y1, y2, heads, sems):
    odd_y = place[2] == 1
    copies = [
        pltpu.make_async_copy(ref.at[:VAL], heads.at[n], sems.at[n]) for n, ref in enumerate((m1, m2, r1, r2))
    ]
    for copy in copies:
        copy.start()
    sub, lane = iotas(NZ)

    def pair(index, row):
        if index + 1 < T:
            return lines(sources, index, row)
        if index + 1 == T:
            halves = second_half(lines(sources, index - 1, row)), second_half(lines(diagonal, 0, row))
            return jnp.where(sub < 4, halves[0], halves[1])
        return lines(diagonal, index - T, row)

    small, _ = iotas(ZT)
    marks = jnp.zeros((8, ZT), F32)
    for t in range(T):
        line = jnp.broadcast_to(returns[0:1, t * ZT : (t + 1) * ZT], (8, ZT))
        marks = jnp.where(small == t, line.astype(F32), marks)
    for tile in range(4):
        sides = []
        for row in (0, CY - 1):
            first = row_of_colour_0(pair(4 * tile, row), row, lane)
            if tile < 3:
                second = row_of_colour_0(pair(4 * tile + 2, row), row, lane)
                sides.append(interleaved(first, second, sub))
            else:
                sides.append(first)
        down, up = sides
        y1[YVAL + tile] = jnp.where(odd_y, down, up)
        y2[YVAL + tile] = jnp.where(odd_y, up, down)
    turned = roll(marks, NZ // BLK, 1)
    for ref, value in ((y1, jnp.where(odd_y, marks, turned)), (y2, jnp.where(odd_y, turned, marks))):
        for t in range(T):
            row = 2 * (t % 4) + 1
            ref[YVAL + 3, row : row + 1, t // 4 * ZT : (t // 4 + 1) * ZT] = value[t : t + 1]
    wait_for(copies)
    corner_values(place, *[heads.at[n] for n in range(4)], y1, y2)


def interface_kernel(place, blocks, returns, y1, y2, chosen, back, inflow, beside, sems):
    odd_y = place[2] == 1
    exit_side = place[3] == 1
    back[...] = jnp.zeros_like(back)
    copies = [pltpu.make_async_copy(ref.at[YHEAD - 1], beside.at[n], sems.at[n]) for n, ref in enumerate((y1, y2))]
    for copy in copies:
        copy.start()
    half = blocks.shape[0] // 2
    total = blocks[0:8]
    for tile in range(1, half // 8):
        total = total + blocks[8 * tile : 8 * tile + 8]
    total = total + roll(total, 4, 0)
    total = total + roll(total, 2, 0)
    first, second = (jnp.broadcast_to(total[row : row + 1], (8, ZT)) for row in (0, 1))
    for row in range(16):
        at = slice(8 * row, 8 * row + 8)
        found = chosen[at, :ZT] * first + chosen[at, ZT:] * second
        inflow[at, :] = jnp.broadcast_to(jnp.sum(found, axis=1, keepdims=True), (8, ZT))
    wait_for(copies)

    @pl.when(exit_side)
    def _():
        cells = half // 2
        table = blocks[pl.ds(half, cells, stride=2), :]
        sub, _ = iotas(ZT)

        def marks_of(n):
            laid = jnp.zeros((8, ZT), F32)
            for t in range(T):
                row, at = 2 * (t % 4) + 1, slice(t // 4 * ZT, (t // 4 + 1) * ZT)
                laid = jnp.where(sub == t, jnp.broadcast_to(beside[n, row : row + 1, at], (8, ZT)), laid)
            return laid

        first, second = marks_of(0), marks_of(1)
        high, low = jnp.where(odd_y, second, first), jnp.where(odd_y, first, second)
        slots = lax.broadcasted_iota(jnp.int32, (8, cells), 1).astype(F32)
        column = lax.broadcasted_iota(jnp.int32, table.shape, 1)
        spots = [jnp.where(column // BLK == q, roll(table, q * BLK, 1), 0.0) for q in range(ZT // BLK)]
        wanted = []
        for t in range(T):
            line = jnp.broadcast_to(returns[0:1, t * ZT : (t + 1) * ZT], (8, ZT))
            spread = line
            for y in range(1, CY):
                spread = jnp.where(sub == y, roll(line, -y * (NZ // BLK), 1), spread)
            wanted.append(spread.astype(F32))
        wanted += [high, low]
        for tile in range(NZ // ZT):
            laid = jnp.zeros((8 * len(wanted), ZT), F32)
            for q in range(ZT // BLK):
                block = tile * (ZT // BLK) + q
                match = jnp.concatenate([want[:, block : block + 1] == slots for want in wanted], axis=0)
                laid = laid + jnp.dot(
                    match.astype(F32), spots[q], precision=lax.Precision.HIGHEST, preferred_element_type=F32
                )
            at = slice(tile * ZT, (tile + 1) * ZT)
            for t in range(T):
                back[t, 0:8, at] = laid[8 * t : 8 * t + 8]
                back[t, 8:9, at] = laid[8 * T + t : 8 * T + t + 1]
                back[t, 15:16, at] = laid[8 * T + 8 + t : 8 * T + 9 + t]


def sweep_kernel(
    place, coupling, fields, sources, diagonal, inverse, x1, x2, ya, za, yb, zb, back, inflow, *rest
):
    r1, r2, y1, y2 = rest[:4] if len(rest) == 9 else (x1, x2, ya, za)
    out, m1, m2, u0, u1 = rest[-5:]
    section = place[0]
    odd_x, odd_y = place[1], place[2]
    exit_side = place[3] == 1
    even, even_z = even_mask(NZ), even_mask(ZT)
    sub, lane = iotas(NZ)
    sub_z, _ = iotas(ZT)
    colours = (u0, u1)
    own, edge = slice(0, 8), slice(8, 16)

    for t in range(T):
        for k in (0, 1):
            u1[t, k + 1, own] = packed(fields[t, 2 * k], fields[t, 2 * k + 1], even, 1)
            u0[t, k + 1, own] = packed(fields[t, 2 * k], fields[t, 2 * k + 1], even, 0)
        for ref, tile, at, width in (
            (u1, t, slice(0, NZ), NZ),
            (u0, T + t // 4, slice(t % 4 * ZT, (t % 4 + 1) * ZT), ZT),
        ):
            low = jnp.where(odd_x == 1, r1[tile, :, at], r2[tile, :, at])
            high = jnp.where(odd_x == 1, r2[tile, :, at], r1[tile, :, at])
            ref[t, 0, own, :width] = low
            ref[t, 3, own, :width] = high
    own_rows, own_rows_z = (lax.broadcasted_iota(jnp.int32, (8, width), 0) for width in (NZ, ZT))

    def beside(tile, rows, at):
        first, second = y1[tile, rows, at], y2[tile, rows, at]
        low, high = jnp.where(odd_y == 1, first, second), jnp.where(odd_y == 1, second, first)
        return low, high

    whole = slice(0, NZ)
    for t in range(T):
        low, high = beside(t // 2, slice(0, 8), whole)
        for k in (0, 1):
            base = 4 * (t % 2) + 2 * k
            u1[t, k + 1, edge] = jnp.where(own_rows < 2, roll(high, -base, 0), roll(low, 6 - base, 0))
            row, at = 4 + 2 * k + t // 4, slice(t % 4 * ZT, (t % 4 + 1) * ZT)
            first, last = beside(3, slice(row, row + 1), at)
            u0[t, k + 1, edge, :ZT] = jnp.where(own_rows_z < 4, last, first)
        first, last = beside(4, slice(t, t + 1), whole)
        corner = jnp.where(own_rows < 4, last, first)
        u1[t, 0, edge] = corner
        u1[t, 3, edge] = corner

    @pl.when(exit_side)
    def _():
        for t in range(T):
            u0[t, 3] = back[t]
            u1[t, 3] = back[t]

    def around(centre, beyond):
        up = roll(jnp.where(sub == 0, beyond, centre), -1, 0)
        down = roll(jnp.where(sub == 7, beyond, centre), 1, 0)
        return up + down

    def planes(colour, unit, t):
        old, new = colours[colour], colours[1 - colour]
        if unit == "ring":
            centre = jnp.where(even, new[t, 0, own], new[t, 3, own])
            beyond = jnp.where(even, new[t, 0, edge], new[t, 3, edge])
            x_sum = jnp.where(even, new[t, 3, own] + new[t, 2, own], new[t, 0, own] + new[t, 1, own])
            return centre, beyond, x_sum, jnp.where(even, old[t, 3, own], old[t, 0, own])
        p, rows = unit
        here, other = (own, edge) if rows == 0 else (edge, own)
        centre, beyond = new[t, p, here], new[t, p, other]
        below, above = new[t, p - 1, here], new[t, p + 1, here]
        x_sum = centre + (jnp.where(even, below, above) if colour == 0 else jnp.where(even, above, below))
        return centre, beyond, x_sum, old[t, p, here]

    def inflow_of(colour, unit):
        base = 64 * colour
        if unit == "ring":
            values = jnp.where(even_z, inflow[base + 48 : base + 56], inflow[base : base + 8])
        else:
            start = base + 16 * unit[0] + 8 * unit[1]
            values = inflow[start : start + 8]
        return jnp.concatenate([values] * (NZ // ZT), axis=1)

    ring_mask = (sub + lane + odd_x) % 2 == 0
    edge_mask = jnp.where(sub == 7, 1, 0) == odd_y

    def of_ring(index):
        tile = VAL + index // 2
        if index % 2 == 0:
            return jnp.where(ring_mask, x1[tile], x2[tile])
        return roll(jnp.where(ring_mask, x2[tile], x1[tile]), -1, 0)

    def of_edge(first, second, tile, index, p):
        tile, row = tile + index // 4, 4 * (index % 2) + 2 * (p - 1) + index % 4 // 2
        return jnp.where(edge_mask, first[tile, row : row + 1], second[tile, row : row + 1])

    def taken(colour, unit, kind, index):
        if unit == "ring":
            return of_ring(T * T + index if kind == "source" else index)
        p, rows = unit
        if rows == 0:
            if kind == "inverse":
                raw = inverse.at[index // T, index % T]
            else:
                raw = (sources if kind == "source" else diagonal).at[index]
            return packed(raw[2 * p - 2], raw[2 * p - 1], even, colour)
        if kind == "inverse":
            return of_edge(yb, zb, 0, index, p)
        return of_edge(ya, za, YVAL, index if kind == "source" else T + index, p)

    def put(colour, unit, t, value):
        ref = colours[colour]
        if unit == "ring":
            ref[t, 0, own] = value
            ref[t, 3, own] = jnp.where(exit_side, back[t, own], value)
        else:
            ref[t, unit[0], own if unit[1] == 0 else edge] = value

    def valid(unit):
        if unit == "ring":
            return jnp.where(even, place[5], place[4])
        if unit[1] == 0:
            return None
        return jnp.where(sub == 7, place[6], place[7])

    def turbine(colour, unit):
        driving = []
        for t in range(T):
            centre, beyond, x_sum, kept = planes(colour, unit, t)
            start = inflow_of(colour, unit) if t == 0 else kept
            ahead = jnp.where(lane == NZ - 1, 0.0, roll(centre, -1, 1))
            behind = jnp.where(lane == 0, start, roll(centre, 1, 1))
            total = x_sum + around(centre, beyond) + ahead + behind
            source = taken(colour, unit, "source", t)
            driving.append(source + coupling[t] * total)
        for s in range(T):
            value = taken(colour, unit, "inverse", T * s) * driving[0]
            for t in range(1, T):
                value = value + taken(colour, unit, "inverse", T * s + t) * driving[t]
            put(colour, unit, s, value)

    def combustor(colour, unit):
        before = None
        current = planes(colour, unit, 0)
        flag = valid(unit)
        for t in range(T):
            after = planes(colour, unit, t + 1) if t + 1 < T else None
            centre, beyond, x_sum, _ = current
            edge_ahead = 0.0 if after is None else roll(after[0], -1, 1)
            edge_behind = 0.0 if before is None else roll(before, 1, 1)
            ahead = jnp.where(lane == NZ - 1, edge_ahead, roll(centre, -1, 1))
            behind = jnp.where(lane == 0, edge_behind, roll(centre, 1, 1))
            total = x_sum + around(centre, beyond) + ahead + behind
            source = taken(colour, unit, "source", t)
            value = (source + total) / (6.0 + taken(colour, unit, "diagonal", t))
            if flag is not None:
                value = jnp.where(flag == 1, value, 0.0)
            put(colour, unit, t, value)
            before, current = centre, after

    def both(step):
        for unit in ((1, 0), (2, 0), (1, 1), (2, 1), "ring"):
            step(0, unit)
        for unit in ((1, 0), (2, 0)):
            step(1, unit)

    pl.when(section == 0)(functools.partial(both, combustor))
    pl.when(section != 0)(functools.partial(both, turbine))

    for t in range(T):
        for k in (0, 1):
            a, b = u0[t, k + 1, own], u1[t, k + 1, own]
            out[t, 2 * k] = jnp.where(even, a, b)
            out[t, 2 * k + 1] = jnp.where(even, b, a)
    for ref, pair in ((m1, 2 - odd_x), (m2, 1 + odd_x)):
        store_message(ref, lambda t: u1[t, pair, own], lambda t: u0[t, pair, own, :ZT])


def shape(*dims):
    return jax.ShapeDtypeStruct(dims, F32)


SMEM = pl.BlockSpec(memory_space=pltpu.SMEM)
VMEM = pl.BlockSpec(memory_space=pltpu.VMEM)
ANY = pl.BlockSpec(memory_space=pl.ANY)


def call(kernel, outs, operands, out_specs=None, scratch=(), limit=24):
    return pl.pallas_call(
        kernel,
        out_shape=outs,
        in_specs=[spec for spec, _ in operands],
        out_specs=out_specs or [VMEM] * len(outs),
        scratch_shapes=list(scratch),
        compiler_params=pltpu.CompilerParams(vmem_limit_bytes=limit << 20),
    )(*[operand for _, operand in operands])


def swaps(axis, first, second, turbine_only=False):
    peers = lax.axis_size(axis)
    inner = [(i, i ^ 1) for i in range(peers)]
    outer = [(i, (i + 1 ^ 1) - 1) for i in range(1, peers - 1)]
    if turbine_only:
        inner, outer = ([(2 * i + 1, 2 * j + 1) for i, j in pairs] for pairs in (inner, outer))
        axis = (axis, "sa")
    second = lax.ppermute(second, axis, outer)
    return lax.ppermute(first, axis, inner), second


def chosen_slots():
    table = np.zeros((128, 2 * ZT), np.float32)
    for c in range(2):
        for p in range(4):
            for r in range(16):
                y = r if r < 12 else r - 16
                x = 2 * (p - 1) + (c if r % 2 == 0 else 1 - c)
                block = None
                if 0 <= x < CX and 0 <= y < CY:
                    block = (0, x, y)
                elif x == -1 and 0 <= y < CY:
                    block = (1, CX - 1, y)
                elif x == CX and 0 <= y < CY:
                    block = (2, 0, y)
                elif 0 <= x < CX and y == -1:
                    block = (3, x, CY - 1)
                elif 0 <= x < CX and y == CY:
                    block = (4, x, 0)
                if block is not None:
                    table[64 * c + 16 * p + r, BLK * block[0] + CY * block[1] + block[2]] = 1.0
    return table


def shards(fields, sources, diagonal, block_inverse, coupling, donors, returns):
    values = fields[0]
    source = sources[0]
    rows_x, rows_y = lax.axis_size("gx"), lax.axis_size("gy")
    cells = rows_x * rows_y
    section, place_x, place_y = (lax.axis_index(axis) for axis in ("sa", "gx", "gy"))
    exit_side = (section == 0) & (place_x == rows_x - 1)
    place = jnp.stack(
        [
            section,
            place_x % 2,
            place_y % 2,
            exit_side.astype(jnp.int32),
            (place_x > 0).astype(jnp.int32),
            (place_x < rows_x - 1).astype(jnp.int32),
            (place_y > 0).astype(jnp.int32),
            (place_y < rows_y - 1).astype(jnp.int32),
            place_x,
            place_y,
        ]
    ).astype(jnp.int32)

    flat = [
        array.reshape(-1, CY, NZ // ZT, ZT).transpose(0, 2, 1, 3).reshape(-1, ZT)
        for array in (source, diagonal, block_inverse)
    ]
    m1, m2, yb, zb, payload = call(
        opening_kernel,
        [shape(VAL + XBULK, 8, NZ)] * 2 + [shape(YBULK, 8, NZ)] * 2 + [shape(4 * cells, ZT)],
        [(SMEM, place), (SMEM, donors.reshape(-1)), (VMEM, values)] + [(ANY, array) for array in flat],
        scratch=[
            pltpu.VMEM((cells, ZT), F32),
            pltpu.VMEM((2, *flat[0].shape), F32),
            pltpu.VMEM(flat[2].shape, F32),
            pltpu.SemaphoreType.DMA((3,)),
        ],
        limit=60,
    )
    x1, x2 = swaps("gx", m1, m2)
    yb, zb = swaps("gy", yb, zb, turbine_only=True)
    ya, za = call(
        first_corner_kernel,
        [shape(YHEAD, 8, NZ)] * 2,
        [(SMEM, place)] + [(ANY, array) for array in (m1, m2, x1, x2)] + [(VMEM, array) for array in (returns, *flat[:2])],
        scratch=[pltpu.VMEM((4, VAL, 8, NZ), F32), pltpu.SemaphoreType.DMA((4,))],
    )
    ya, za = swaps("gy", ya, za)
    arrived = lax.all_to_all(
        payload.reshape(2 * cells, 1, 2 * ZT), ("sa", "gx", "gy"), split_axis=0, concat_axis=0, tiled=True
    ).reshape(4 * cells, ZT)
    back, inflow = call(
        interface_kernel,
        [shape(T, 16, NZ), shape(128, ZT)],
        [(SMEM, place), (VMEM, arrived), (VMEM, returns), (ANY, ya), (ANY, za), (VMEM, jnp.asarray(chosen_slots()))],
        scratch=[pltpu.VMEM((2, 8, NZ), F32), pltpu.SemaphoreType.DMA((2,))],
    )

    for sweep in range(SWEEPS):
        received = []
        if sweep > 0:
            r1, r2 = swaps("gx", m1, m2)
            y1, y2 = call(
                corner_kernel,
                [shape(YVAL, 8, NZ)] * 2,
                [(SMEM, place)] + [(VMEM, array) for array in (m1, m2, r1, r2)],
            )
            received = [r1, r2, *swaps("gy", y1, y2)]
        values, m1, m2 = call(
            sweep_kernel,
            [shape(T, CX, CY, NZ), shape(VAL, 8, NZ), shape(VAL, 8, NZ)],
            [(SMEM, place), (SMEM, coupling)]
            + [(VMEM, array) for array in (values, source, diagonal, block_inverse)]
            + [(VMEM, array) for array in (x1, x2, ya, za, yb, zb, back, inflow, *received)],
            scratch=[pltpu.VMEM((T, 4, 16, NZ), F32)] * 2,
            limit=40,
        )
    return values[None]


def solution(mesh):
    return jax.shard_map(
        shards,
        mesh=mesh,
        in_specs=(
            P("sa", None, "gx", "gy", None),
            P("sa", None, "gx", "gy", None),
            P(None, "gx", "gy", None),
            P(None, None, "gx", "gy", None),
            P(),
            P(),
            P("gy", None),
        ),
        out_specs=P("sa", None, "gx", "gy", None),
        check_vma=False,
    )
```

```python
import functools
import jax
import jax.numpy as jnp
from jax import lax
from jax.experimental import pallas as pl
from jax.experimental.pallas import tpu as pltpu
from jax.sharding import PartitionSpec as P

SWEEPS = 4
BLK = 32
T = 7
CX = 4
CY = 8
NZ = 512
ZT = 128
VAL = T + 2
COEF = T * T + T
XBULK = COEF // 2
MARKS = NZ // BLK
YVAL = 5
YHEAD = YVAL + 4
YBULK = T * T // 4 + 1
F32 = jnp.float32


def iotas(width):
    sub = lax.broadcasted_iota(jnp.int32, (8, width), 0)
    lane = lax.broadcasted_iota(jnp.int32, (8, width), 1)
    return sub, lane


def even_mask(width):
    sub, lane = iotas(width)
    return (sub + lane) % 2 == 0


def roll(array, shift, axis):
    size = array.shape[axis]
    shift = shift % size
    return array if shift == 0 else pltpu.roll(array, shift, axis)


def packed(pair_low, pair_high, even, colour):
    return jnp.where(even, pair_low, pair_high) if colour == 0 else jnp.where(even, pair_high, pair_low)


class Place:
    def __init__(self):
        self.rows_x = lax.axis_size("gx")
        self.section, self.x, self.y = (lax.axis_index(axis) for axis in ("sa", "gx", "gy"))
        self.rows_y = lax.axis_size("gy")
        self.odd_x, self.odd_y = lax.rem(self.x, 2), lax.rem(self.y, 2)
        self.exit_side = (self.section == 0) & (self.x == self.rows_x - 1)


def store_message(ref, ones, zeros_first):
    for t in range(T):
        ref[t] = ones(t)
        ref[T + t // 4, :, (t % 4) * ZT : (t % 4 + 1) * ZT] = zeros_first(t)
    ref[T + 1, :, 3 * ZT :] = jnp.zeros((8, ZT), F32)


def wait_for(copies):
    for copy in copies:
        copy.wait()


def lines(ref, index, row):
    found = [ref[pl.ds(128 * index + 8 * z + row, 8, stride=32), :] for z in range(NZ // ZT)]
    return jnp.concatenate(found, axis=1)


def second_half(array):
    return roll(array, 4, 0)


def row_of_colour_0(raw, row, lane):
    return jnp.where((lane + row) % 2 == 0, raw, roll(raw, -1, 0))


def interleaved(first, second, sub):
    return jnp.where(sub % 2 == 0, first, roll(second, 1, 0))


def fill_payload(place, donors, returns, fields, payload, blocks):
    sub, lane = iotas(ZT)
    payload[...] = jnp.zeros_like(payload)
    cells = blocks.shape[0]

    @pl.when(place.exit_side)
    def _():
        for entry in range(cells):
            gy, block, slot = donors[0, entry], donors[1, entry], donors[2, entry]
            piece, row, column = block // 128, block % 128 // 16, block % 16
            start = pl.multiple_of(column // 4 * ZT, ZT)
            found = fields[piece, CX - 1, :, pl.ds(start, ZT)]
            found = pltpu.roll(pltpu.roll(found, (8 - row) % 8, 0), (ZT - column % 4 * BLK) % ZT, 1)
            blocks[pl.ds(slot, 1), :] = jnp.where((lane < BLK) & (gy == place.y), found, 0.0)[:1]
        marks = [jnp.zeros((8, ZT), F32)] * 2
        for t in range(T):
            line = jnp.broadcast_to(returns[0:1, t * ZT : (t + 1) * ZT], (8, ZT)).astype(F32)
            for n, row in enumerate((CY - 1, 0)):
                turned = roll(line, MARKS * (t - row), 1)
                marks[n] = jnp.where(lane // MARKS == t, turned, marks[n])
        both = jnp.where(sub % 2 == 0, marks[0], marks[1])
        for tile in range(2 * cells // 8):
            payload[8 * tile : 8 * tile + 8, :] = both
        tiles = cells // 8
        zero = jnp.zeros((8, ZT), F32)
        for tile in range(tiles):
            here = blocks[8 * tile : 8 * tile + 8]
            below = blocks[8 * tile - 8 : 8 * tile] if tile > 0 else zero
            above = blocks[8 * tile + 8 : 8 * tile + 16] if tile + 1 < tiles else zero
            left = jnp.where(sub == 0, 0.0, roll(here, 1, 0))
            right = jnp.where(sub == 7, 0.0, roll(here, -1, 0))
            wide = here + roll(below, BLK, 1) + roll(above, 2 * BLK, 1) + roll(left, 3 * BLK, 1)
            payload[pl.ds(2 * cells + 16 * tile, 8, stride=2), :] = wide
            payload[pl.ds(2 * cells + 16 * tile + 1, 8, stride=2), :] = right

    @pl.when(place.section == 1)
    def _():
        inlet = jnp.zeros((8, ZT), F32)
        for x in range(CX):
            column = jnp.broadcast_to(fields[0, x, :, 0:1], (8, ZT))
            inlet = inlet + jnp.where(lane == CY * x + sub, column, 0.0)
        inlet = jnp.broadcast_to(jnp.sum(inlet, axis=0, keepdims=True), (8, ZT))
        for tile in range(cells // 8):
            payload[pl.ds(16 * tile, 8, stride=2), :] = inlet


def lines(ref, index, row):
    found = [ref[pl.ds(128 * index + 8 * z + row, 8, stride=32), :] for z in range(NZ // ZT)]
    return jnp.concatenate(found, axis=1)


def second_half(array):
    return roll(array, 4, 0)


def row_of_colour_0(raw, row, lane):
    return jnp.where((lane + row) % 2 == 0, raw, roll(raw, -1, 0))


def interleaved(first, second, sub):
    return jnp.where(sub % 2 == 0, first, roll(second, 1, 0))


def opening_kernel(
    donors,
    returns_far,
    fields_far,
    sources_far,
    diagonal_far,
    inverse_far,
    m1,
    m2,
    b1,
    b2,
    s1,
    s2,
    payload,
    returns,
    fields,
    sources,
    diagonal,
    inverse,
    blocks,
    sems,
):
    pairs = (
        (returns_far, returns),
        (fields_far, fields),
        (sources_far, sources),
        (diagonal_far, diagonal),
        (inverse_far, inverse),
    )
    loads = [pltpu.make_async_copy(far, near, sems.at[n]) for n, (far, near) in enumerate(pairs)]
    for load in loads:
        load.start()
    wait_for(loads[:2])
    place = Place()
    section, odd, odd_y = place.section, place.odd_x, place.odd_y == 1
    even, even_z = even_mask(NZ), even_mask(ZT)
    for ref, pair in ((m1, 1 - odd), (m2, odd)):
        store_message(
            ref,
            lambda t: packed(fields[t, 2 * pair], fields[t, 2 * pair + 1], even, 1),
            lambda t: packed(fields[t, 2 * pair, :, :ZT], fields[t, 2 * pair + 1, :, :ZT], even_z, 0),
        )
    fill_payload(place, donors, returns, fields, payload, blocks)
    wait_for(loads[2:])
    sub, lane = iotas(NZ)

    def plane_of(ref, index, plane):
        at = [pl.multiple_of(8 * (4 * (CX * index + plane) + z), 8) for z in range(NZ // ZT)]
        return jnp.concatenate([ref[pl.ds(start, 8), :] for start in at], axis=1)

    def coefficient(index, plane):
        if index >= T * T:
            return plane_of(sources, index - T * T, plane)
        raw = plane_of(inverse, index, plane)
        return jnp.where(section == 0, plane_of(diagonal, index, plane), raw) if index < T else raw

    for ref, far in ((m1, 1 - odd), (m2, odd)):
        wanted = (sub + lane + far) % 2 == 0
        plane = far * (CX - 1)
        for tile in range(XBULK):
            first, second = coefficient(2 * tile, plane), coefficient(2 * tile + 1, plane)
            ref[VAL + tile] = jnp.where(wanted, first, roll(second, 1, 0))

    def inverse_rows(tile, row):
        if tile + 1 == YBULK:
            return row_of_colour_0(second_half(lines(inverse, T * T - 2, row)), row, lane)
        first, second = (row_of_colour_0(lines(inverse, 4 * tile + 2 * n, row), row, lane) for n in (0, 1))
        return interleaved(first, second, sub)

    def pair(index, row):
        if index + 1 < T:
            return lines(sources, index, row)
        if index + 1 == T:
            halves = second_half(lines(sources, index - 1, row)), second_half(lines(diagonal, 0, row))
            return jnp.where(sub < 4, halves[0], halves[1])
        return lines(diagonal, index - T, row)

    def other_rows(tile, row):
        first = row_of_colour_0(pair(4 * tile, row), row, lane)
        if tile == 3:
            return first
        return interleaved(first, row_of_colour_0(pair(4 * tile + 2, row), row, lane), sub)

    for first, second, rows_of, tiles in ((b1, b2, inverse_rows, YBULK), (s1, s2, other_rows, 4)):
        for tile in range(tiles):
            down, up = rows_of(tile, 0), rows_of(tile, CY - 1)
            first[tile] = jnp.where(odd_y, down, up)
            second[tile] = jnp.where(odd_y, up, down)


def corner_values(m1, m2, r1, r2, y1, y2):
    place = Place()
    odd_x, odd_y = place.odd_x == 1, place.odd_y == 1
    sub, lane = iotas(NZ)
    even = even_mask(NZ)
    tiles = {}
    for t in range(VAL):
        a, b = m1[t], m2[t]
        own = jnp.where(odd_x, a, b), jnp.where(odd_x, b, a)
        for start in (0, 6):
            if t < T:
                base = 4 * (t % 2)
                rows = [roll(own[k], base + 2 * k - start, 0) for k in (0, 1)]
                both = jnp.where(sub < base + 2, rows[0], rows[1])
                tiles[start, t] = both
                c, d = r1[t], r2[t]
                from_low, from_high = jnp.where(odd_x, c, d), jnp.where(odd_x, d, c)
                ring = jnp.where(even, from_low, from_high)
                tiles[start, "ring", t] = roll(ring, t - (0 if start == 0 else CY - 1), 0)
            else:
                row = 0 if start == 0 else CY - 1
                rows = [roll(own[k], 4 + 2 * k + t - T - row, 0) for k in (0, 1)]
                tiles[start, t] = jnp.where(sub < 6, rows[0], rows[1])
    for tile in range(YVAL):
        sides = []
        for start in (0, 6):
            if tile < 3:
                sides.append(jnp.where(sub < 4, tiles[start, 2 * tile], tiles[start, 2 * tile + 1]))
            elif tile == 3:
                firsts = jnp.where(sub % 2 == 0, tiles[start, T], tiles[start, T + 1])
                sides.append(jnp.where(sub < 4, tiles[start, T - 1], firsts))
            else:
                laid = tiles[start, "ring", 0]
                for t in range(1, T):
                    laid = jnp.where(sub == t, tiles[start, "ring", t], laid)
                sides.append(laid)
        down, up = sides
        y1[tile] = jnp.where(odd_y, down, up)
        y2[tile] = jnp.where(odd_y, up, down)


def corner_kernel(m1, m2, r1, r2, y1, y2):
    corner_values(m1, m2, r1, r2, y1, y2)


def first_corner_kernel(m1, m2, r1, r2, s1, s2, y1, y2, heads, sems):
    pairs = [(ref.at[:VAL], heads.at[n]) for n, ref in enumerate((m1, m2, r1, r2))]
    pairs += [(s1, y1.at[YVAL:YHEAD]), (s2, y2.at[YVAL:YHEAD])]
    copies = [pltpu.make_async_copy(far, near, sems.at[n]) for n, (far, near) in enumerate(pairs)]
    for copy in copies:
        copy.start()
    wait_for(copies)
    corner_values(*[heads.at[n] for n in range(4)], y1, y2)


def interface_kernel(blocks, coupling, returns_far, *refs):
    count = (len(refs) - 5) // 2
    back, inflow, weights = refs[count : count + 3]
    returns, sems = refs[-2:]
    pairs = [(returns_far, returns), *zip(refs[:count], refs[count + 3 : -2])]
    copies = [pltpu.make_async_copy(far, near, sems.at[n]) for n, (far, near) in enumerate(pairs)]
    for copy in copies:
        copy.start()
    place = Place()
    back[...] = jnp.zeros_like(back)
    half = blocks.shape[0] // 2
    total = blocks[0:8]
    for tile in range(1, half // 8):
        total = total + blocks[8 * tile : 8 * tile + 8]
    total = total + roll(total, 4, 0)
    total = total + roll(total, 2, 0)
    first, second = (jnp.broadcast_to(total[row : row + 1], (8, ZT)) for row in (0, 1))
    sub, lane = iotas(ZT)
    weight = jnp.zeros((8, ZT), F32)
    for t in range(T):
        weight = jnp.where(sub == t, coupling[t], weight)
    weights[...] = weight
    for row in range(16):
        found = jnp.full((8, ZT), -1, jnp.int32)
        for r, target in enumerate(chosen_places(row)):
            found = jnp.where(sub == r, target, found)
        parts = jnp.where(lane == found, first, 0.0) + jnp.where(lane + ZT == found, second, 0.0)
        inflow[8 * row : 8 * row + 8, :] = jnp.broadcast_to(jnp.sum(parts, axis=1, keepdims=True), (8, ZT))

    copies[0].wait()

    @pl.when(place.exit_side)
    def _():
        cells = half // 2
        table = blocks[pl.ds(half, cells, stride=2), :]
        sub, lane = iotas(ZT)

        def marks_of(row):
            first = half - 2 * place.rows_y
            line = jnp.zeros((8, ZT), F32)
            for tile in range(2 * place.rows_y // 8):
                at = first + 8 * tile
                line = line + jnp.where(sub + 8 * tile == row, blocks[at : at + 8], 0.0)
            line = jnp.broadcast_to(jnp.sum(line, axis=0, keepdims=True), (8, ZT))
            laid = line
            for t in range(1, T):
                laid = jnp.where(sub == t, roll(line, -MARKS * t, 1), laid)
            return laid

        high, low = marks_of(2 * place.y + 3), marks_of(2 * place.y - 2)
        slots = lax.broadcasted_iota(jnp.int32, (8, cells), 1).astype(F32)
        column = lax.broadcasted_iota(jnp.int32, table.shape, 1)
        spots = [jnp.where(column // BLK == q, roll(table, q * BLK, 1), 0.0) for q in range(ZT // BLK)]
        wanted = []
        for t in range(T):
            line = jnp.broadcast_to(returns[0:1, t * ZT : (t + 1) * ZT], (8, ZT))
            spread = line
            for y in range(1, CY):
                spread = jnp.where(sub == y, roll(line, -y * MARKS, 1), spread)
            wanted.append(spread.astype(F32))
        wanted += [high, low]
        for tile in range(NZ // ZT):
            laid = jnp.zeros((8 * len(wanted), ZT), F32)
            for q in range(ZT // BLK):
                block = tile * (ZT // BLK) + q
                match = jnp.concatenate([want[:, block : block + 1] == slots for want in wanted], axis=0)
                laid = laid + jnp.dot(
                    match.astype(F32), spots[q], precision=lax.Precision.HIGHEST, preferred_element_type=F32
                )
            at = slice(tile * ZT, (tile + 1) * ZT)
            for t in range(T):
                back[t, 0:8, at] = laid[8 * t : 8 * t + 8]
                back[t, 8:9, at] = laid[8 * T + t : 8 * T + t + 1]
                back[t, 15:16, at] = laid[8 * T + 8 + t : 8 * T + 9 + t]

    wait_for(copies[1:])


def sweep_kernel(
    last, weights, fields, sources, diagonal, inverse, x1, x2, ya, za, yb, zb, back, inflow, *rest
):
    r1, r2, y1, y2 = rest[:4] if len(rest) > 5 else (x1, x2, ya, za)
    u0, u1 = rest[-2:]
    place = Place()
    section, odd_x, odd_y, exit_side = place.section, place.odd_x, place.odd_y, place.exit_side
    even, even_z = even_mask(NZ), even_mask(ZT)
    sub, lane = iotas(NZ)
    sub_z, _ = iotas(ZT)
    colours = (u0, u1)
    own, edge = slice(0, 8), slice(8, 16)

    for t in range(T):
        for k in (0, 1):
            u1[t, k + 1, own] = packed(fields[t, 2 * k], fields[t, 2 * k + 1], even, 1)
            u0[t, k + 1, own] = packed(fields[t, 2 * k], fields[t, 2 * k + 1], even, 0)
        for ref, tile, at, width in (
            (u1, t, slice(0, NZ), NZ),
            (u0, T + t // 4, slice(t % 4 * ZT, (t % 4 + 1) * ZT), ZT),
        ):
            low = jnp.where(odd_x == 1, r1[tile, :, at], r2[tile, :, at])
            high = jnp.where(odd_x == 1, r2[tile, :, at], r1[tile, :, at])
            ref[t, 0, own, :width] = low
            ref[t, 3, own, :width] = high
    own_rows, own_rows_z = (lax.broadcasted_iota(jnp.int32, (8, width), 0) for width in (NZ, ZT))

    def beside(tile, rows, at):
        first, second = y1[tile, rows, at], y2[tile, rows, at]
        low, high = jnp.where(odd_y == 1, first, second), jnp.where(odd_y == 1, second, first)
        return low, high

    whole = slice(0, NZ)
    for t in range(T):
        low, high = beside(t // 2, slice(0, 8), whole)
        for k in (0, 1):
            base = 4 * (t % 2) + 2 * k
            u1[t, k + 1, edge] = jnp.where(own_rows < 2, roll(high, -base, 0), roll(low, 6 - base, 0))
            row, at = 4 + 2 * k + t // 4, slice(t % 4 * ZT, (t % 4 + 1) * ZT)
            above, below = beside(3, slice(row, row + 1), at)
            u0[t, k + 1, edge, :ZT] = jnp.where(own_rows_z < 4, below, above)
        above, below = beside(4, slice(t, t + 1), whole)
        corner = jnp.where(own_rows < 4, below, above)
        u1[t, 0, edge] = corner
        u1[t, 3, edge] = corner

    @pl.when(exit_side)
    def _():
        for t in range(T):
            u0[t, 3] = back[t]
            u1[t, 3] = back[t]

    def around(centre, beyond):
        up = roll(jnp.where(sub == 0, beyond, centre), -1, 0)
        down = roll(jnp.where(sub == 7, beyond, centre), 1, 0)
        return up + down

    def planes(colour, unit, t):
        old, new = colours[colour], colours[1 - colour]
        if unit == "ring":
            centre = jnp.where(even, new[t, 0, own], new[t, 3, own])
            beyond = jnp.where(even, new[t, 0, edge], new[t, 3, edge])
            x_sum = jnp.where(even, new[t, 3, own] + new[t, 2, own], new[t, 0, own] + new[t, 1, own])
            return centre, beyond, x_sum, jnp.where(even, old[t, 3, own], old[t, 0, own])
        p, rows = unit
        here, other = (own, edge) if rows == 0 else (edge, own)
        centre, beyond = new[t, p, here], new[t, p, other]
        below, above = new[t, p - 1, here], new[t, p + 1, here]
        x_sum = centre + (jnp.where(even, below, above) if colour == 0 else jnp.where(even, above, below))
        return centre, beyond, x_sum, old[t, p, here]

    def inflow_of(colour, unit):
        base = 64 * colour
        if unit == "ring":
            values = jnp.where(even_z, inflow[base + 48 : base + 56], inflow[base : base + 8])
        else:
            start = base + 16 * unit[0] + 8 * unit[1]
            values = inflow[start : start + 8]
        return jnp.concatenate([values] * (NZ // ZT), axis=1)

    ring_mask = (sub + lane + odd_x) % 2 == 0
    edge_mask = jnp.where(sub == 7, 1, 0) == odd_y

    def of_ring(index):
        tile = VAL + index // 2
        if index % 2 == 0:
            return jnp.where(ring_mask, x1[tile], x2[tile])
        return roll(jnp.where(ring_mask, x2[tile], x1[tile]), -1, 0)

    def of_edge(first, second, tile, index, p):
        tile, row = tile + index // 4, 4 * (index % 2) + 2 * (p - 1) + index % 4 // 2
        return jnp.where(edge_mask, first[tile, row : row + 1], second[tile, row : row + 1])

    def taken(colour, unit, kind, index):
        if unit == "ring":
            return of_ring(T * T + index if kind == "source" else index)
        p, rows = unit
        if rows == 0:
            if kind == "inverse":
                raw = inverse.at[index // T, index % T]
            else:
                raw = (sources if kind == "source" else diagonal).at[index]
            return packed(raw[2 * p - 2], raw[2 * p - 1], even, colour)
        if kind == "inverse":
            return of_edge(yb, zb, 0, index, p)
        return of_edge(ya, za, YVAL, index if kind == "source" else T + index, p)

    def put(colour, unit, t, value):
        ref = colours[colour]
        if unit == "ring":
            ref[t, 0, own] = value
            ref[t, 3, own] = jnp.where(exit_side, back[t, own], value)
        else:
            ref[t, unit[0], own if unit[1] == 0 else edge] = value

    def valid(unit):
        if unit == "ring":
            return jnp.where(even, place.rows_x - 1 - place.x, place.x) > 0
        if unit[1] == 0:
            return None
        return jnp.where(sub == 7, place.y, place.rows_y - 1 - place.y) > 0

    def turbine(colour, unit):
        driving = []
        for t in range(T):
            centre, beyond, x_sum, kept = planes(colour, unit, t)
            start = inflow_of(colour, unit) if t == 0 else kept
            ahead = jnp.where(lane == NZ - 1, 0.0, roll(centre, -1, 1))
            behind = jnp.where(lane == 0, start, roll(centre, 1, 1))
            total = x_sum + around(centre, beyond) + ahead + behind
            source = taken(colour, unit, "source", t)
            weight = jnp.concatenate([jnp.broadcast_to(weights[t : t + 1], (8, ZT))] * (NZ // ZT), axis=1)
            driving.append(source + weight * total)
        for s in range(T):
            value = taken(colour, unit, "inverse", T * s) * driving[0]
            for t in range(1, T):
                value = value + taken(colour, unit, "inverse", T * s + t) * driving[t]
            put(colour, unit, s, value)

    def combustor(colour, unit):
        before = None
        current = planes(colour, unit, 0)
        flag = valid(unit)
        for t in range(T):
            after = planes(colour, unit, t + 1) if t + 1 < T else None
            centre, beyond, x_sum, _ = current
            edge_ahead = 0.0 if after is None else roll(after[0], -1, 1)
            edge_behind = 0.0 if before is None else roll(before, 1, 1)
            ahead = jnp.where(lane == NZ - 1, edge_ahead, roll(centre, -1, 1))
            behind = jnp.where(lane == 0, edge_behind, roll(centre, 1, 1))
            total = x_sum + around(centre, beyond) + ahead + behind
            source = taken(colour, unit, "source", t)
            value = (source + total) / (6.0 + taken(colour, unit, "diagonal", t))
            if flag is not None:
                value = jnp.where(flag, value, 0.0)
            put(colour, unit, t, value)
            before, current = centre, after

    def both(step):
        for unit in ((1, 0), (2, 0), (1, 1), (2, 1), "ring"):
            step(0, unit)
        for unit in ((1, 0), (2, 0)):
            step(1, unit)

    pl.when(section == 0)(functools.partial(both, combustor))
    pl.when(section != 0)(functools.partial(both, turbine))

    out = rest[-3] if last else rest[-5]
    for t in range(T):
        for k in (0, 1):
            a, b = u0[t, k + 1, own], u1[t, k + 1, own]
            out[t, 2 * k] = jnp.where(even, a, b)
            out[t, 2 * k + 1] = jnp.where(even, b, a)
    if last:
        return
    for ref, pair in ((rest[-4], 2 - odd_x), (rest[-3], 1 + odd_x)):
        store_message(ref, lambda t: u1[t, pair, own], lambda t: u0[t, pair, own, :ZT])


def shape(*dims):
    return jax.ShapeDtypeStruct(dims, F32)


SMEM = pl.BlockSpec(memory_space=pltpu.SMEM)
VMEM = pl.BlockSpec(memory_space=pltpu.VMEM)
ANY = pl.BlockSpec(memory_space=pl.ANY)
HBM = pl.BlockSpec(memory_space=pltpu.HBM)


def call(kernel, outs, operands, out_specs=None, scratch=(), limit=24):
    return pl.pallas_call(
        kernel,
        out_shape=outs,
        in_specs=[spec for spec, _ in operands],
        out_specs=out_specs or [VMEM] * len(outs),
        scratch_shapes=list(scratch),
        compiler_params=pltpu.CompilerParams(vmem_limit_bytes=limit << 20),
    )(*[operand for _, operand in operands])


def far(array):
    return HBM, pltpu.with_memory_space_constraint(array, pltpu.HBM)


def swaps(axis, first, second, turbine_only=False):
    peers = lax.axis_size(axis)
    inner = [(i, i ^ 1) for i in range(peers)]
    outer = [(i, (i + 1 ^ 1) - 1) for i in range(1, peers - 1)]
    if turbine_only:
        inner, outer = ([(2 * i + 1, 2 * j + 1) for i, j in pairs] for pairs in (inner, outer))
        axis = (axis, "sa")
    second = lax.ppermute(second, axis, outer)
    return lax.ppermute(first, axis, inner), second


def chosen_places(tile):
    places = []
    for index in range(8 * tile, 8 * tile + 8):
        c, p, r = index // 64, index // 16 % 4, index % 16
        y = r if r < 12 else r - 16
        x = 2 * (p - 1) + (c if r % 2 == 0 else 1 - c)
        block = None
        if 0 <= x < CX and 0 <= y < CY:
            block = (0, x, y)
        elif x == -1 and 0 <= y < CY:
            block = (1, CX - 1, y)
        elif x == CX and 0 <= y < CY:
            block = (2, 0, y)
        elif 0 <= x < CX and y == -1:
            block = (3, x, CY - 1)
        elif 0 <= x < CX and y == CY:
            block = (4, x, 0)
        places.append(-1 if block is None else BLK * block[0] + CY * block[1] + block[2])
    return places


def shards(fields, sources, diagonal, block_inverse, coupling, donors, returns):
    values = fields[0]
    source = sources[0]
    rows_x, rows_y = lax.axis_size("gx"), lax.axis_size("gy")
    cells = rows_x * rows_y
    flat = [
        array.reshape(-1, CY, NZ // ZT, ZT).transpose(0, 2, 1, 3).reshape(-1, ZT)
        for array in (source, diagonal, block_inverse)
    ]
    near = (returns, values, *flat)
    m1, m2, yb, zb, s1, s2, payload = call(
        opening_kernel,
        [pltpu.HBM((tiles, 8, NZ), F32) for tiles in [VAL + XBULK] * 2 + [YBULK] * 2 + [4] * 2]
        + [shape(4 * cells, ZT)],
        [(SMEM, pltpu.with_memory_space_constraint(donors.T, pltpu.HBM))] + [far(array) for array in near],
        scratch=[pltpu.VMEM(array.shape, array.dtype) for array in near]
        + [pltpu.VMEM((cells, ZT), F32), pltpu.SemaphoreType.DMA((len(near),))],
    )
    x1, x2 = swaps("gx", m1, m2)
    yb, zb = swaps("gy", yb, zb, turbine_only=True)
    arrived = lax.all_to_all(
        payload.reshape(2 * cells, 1, 2 * ZT), ("sa", "gx", "gy"), split_axis=0, concat_axis=0, tiled=True
    ).reshape(4 * cells, ZT)
    arrived, x1, x2 = lax.optimization_barrier((arrived, x1, x2))
    ya, za = call(
        first_corner_kernel,
        [shape(YHEAD, 8, NZ)] * 2,
        [far(m1), far(m2), (ANY, x1), (ANY, x2), far(s1), far(s2)],
        scratch=[pltpu.VMEM((4, VAL, 8, NZ), F32), pltpu.SemaphoreType.DMA((6,))],
    )
    ya, za = swaps("gy", ya, za)
    distant = (values, source, diagonal, block_inverse)
    made = call(
        interface_kernel,
        [shape(T, 16, NZ), shape(128, ZT), shape(8, ZT)] + [pltpu.VMEM(array.shape, array.dtype) for array in distant],
        [(VMEM, arrived), (SMEM, pltpu.with_memory_space_constraint(coupling, pltpu.HBM)), far(returns)]
        + [far(array) for array in distant],
        scratch=[pltpu.VMEM(returns.shape, returns.dtype), pltpu.SemaphoreType.DMA((len(distant) + 1,))],
    )
    back, inflow, weights, values, source, diagonal, block_inverse = made

    for sweep in range(SWEEPS):
        received = []
        if sweep > 0:
            r1, r2 = swaps("gx", m1, m2)
            y1, y2 = call(
                corner_kernel, [shape(YVAL, 8, NZ)] * 2, [(VMEM, array) for array in (m1, m2, r1, r2)]
            )
            received = [r1, r2, *swaps("gy", y1, y2)]
        last = sweep == SWEEPS - 1
        results = call(
            functools.partial(sweep_kernel, last),
            [shape(T, CX, CY, NZ)] + [shape(VAL, 8, NZ)] * (0 if last else 2),
            [(VMEM, array) for array in (weights, values, source, diagonal, block_inverse)]
            + [(VMEM, array) for array in (x1, x2, ya, za, yb, zb, back, inflow, *received)],
            scratch=[pltpu.VMEM((T, 4, 16, NZ), F32)] * 2,
            limit=40,
        )
        values, m1, m2 = results if not last else (results[0], None, None)
    return values[None]


def solution(mesh):
    return jax.shard_map(
        shards,
        mesh=mesh,
        in_specs=(
            P("sa", None, "gx", "gy", None),
            P("sa", None, "gx", "gy", None),
            P(None, "gx", "gy", None),
            P(None, None, "gx", "gy", None),
            P(),
            P(),
            P("gy", None),
        ),
        out_specs=P("sa", None, "gx", "gy", None),
        check_vma=False,
    )
```

```python
import functools
import jax
import jax.numpy as jnp
from jax import lax
from jax.experimental import pallas as pl
from jax.experimental.pallas import tpu as pltpu
from jax.sharding import PartitionSpec as P

SWEEPS = 4
BLK = 32
T = 7
CX = 4
CY = 8
NZ = 512
ZT = 128
VAL = T + 2
COEF = T * T + T
XBULK = COEF // 2
MARKS = NZ // BLK
CHUNK = 2
YVAL = 5
YHEAD = YVAL + 4
YBULK = T * T // 4 + 1
F32 = jnp.float32


def iotas(width):
    sub = lax.broadcasted_iota(jnp.int32, (8, width), 0)
    lane = lax.broadcasted_iota(jnp.int32, (8, width), 1)
    return sub, lane


def even_mask(width):
    sub, lane = iotas(width)
    return (sub + lane) % 2 == 0


def roll(array, shift, axis):
    size = array.shape[axis]
    shift = shift % size
    return array if shift == 0 else pltpu.roll(array, shift, axis)


def packed(pair_low, pair_high, even, colour):
    return jnp.where(even, pair_low, pair_high) if colour == 0 else jnp.where(even, pair_high, pair_low)


class Place:
    def __init__(self):
        self.rows_x = lax.axis_size("gx")
        self.section, self.x, self.y = (lax.axis_index(axis) for axis in ("sa", "gx", "gy"))
        self.rows_y = lax.axis_size("gy")
        self.odd_x, self.odd_y = lax.rem(self.x, 2), lax.rem(self.y, 2)
        self.exit_side = (self.section == 0) & (self.x == self.rows_x - 1)


def store_message(ref, ones, zeros_first):
    for t in range(T):
        ref[t] = ones(t)
        ref[T + t // 4, :, (t % 4) * ZT : (t % 4 + 1) * ZT] = zeros_first(t)
    ref[T + 1, :, 3 * ZT :] = jnp.zeros((8, ZT), F32)


def wait_for(copies):
    for copy in copies:
        copy.wait()


def lines(ref, index, row):
    found = [ref[pl.ds(128 * index + 8 * z + row, 8, stride=32), :] for z in range(NZ // ZT)]
    return jnp.concatenate(found, axis=1)


def second_half(array):
    return roll(array, 4, 0)


def row_of_colour_0(raw, row, lane):
    return jnp.where((lane + row) % 2 == 0, raw, roll(raw, -1, 0))


def interleaved(first, second, sub):
    return jnp.where(sub % 2 == 0, first, roll(second, 1, 0))


def fill_payload(place, donors, returns, fields, payload, blocks):
    sub, lane = iotas(ZT)
    payload[...] = jnp.zeros_like(payload)
    cells = blocks.shape[0]

    @pl.when(place.exit_side)
    def _():
        for entry in range(cells):
            gy, block, slot = donors[0, entry], donors[1, entry], donors[2, entry]
            piece, row, column = block // 128, block % 128 // 16, block % 16
            start = pl.multiple_of(column // 4 * ZT, ZT)
            found = fields[piece, CX - 1, :, pl.ds(start, ZT)]
            found = pltpu.roll(pltpu.roll(found, (8 - row) % 8, 0), (ZT - column % 4 * BLK) % ZT, 1)
            blocks[pl.ds(slot, 1), :] = jnp.where((lane < BLK) & (gy == place.y), found, 0.0)[:1]
        marks = [jnp.zeros((8, ZT), F32)] * 2
        for t in range(T):
            line = jnp.broadcast_to(returns[0:1, t * ZT : (t + 1) * ZT], (8, ZT)).astype(F32)
            for n, row in enumerate((CY - 1, 0)):
                turned = roll(line, MARKS * (t - row), 1)
                marks[n] = jnp.where(lane // MARKS == t, turned, marks[n])
        for tile in range(cells // 8):
            for n in (0, 1):
                payload[pl.ds(8 * CHUNK * tile + n, 8, stride=CHUNK), :] = marks[n]
        tiles = cells // 8
        zero = jnp.zeros((8, ZT), F32)
        for tile in range(tiles):
            here = blocks[8 * tile : 8 * tile + 8]
            below = blocks[8 * tile - 8 : 8 * tile] if tile > 0 else zero
            above = blocks[8 * tile + 8 : 8 * tile + 16] if tile + 1 < tiles else zero
            left = jnp.where(sub == 0, 0.0, roll(here, 1, 0))
            right = jnp.where(sub == 7, 0.0, roll(here, -1, 0))
            wide = here + roll(below, BLK, 1) + roll(above, 2 * BLK, 1) + roll(left, 3 * BLK, 1)
            payload[pl.ds(CHUNK * (cells + 8 * tile), 8, stride=CHUNK), :] = wide
            payload[pl.ds(CHUNK * (cells + 8 * tile) + 1, 8, stride=CHUNK), :] = right

    @pl.when(place.section == 1)
    def _():
        inlet = jnp.zeros((8, ZT), F32)
        for x in range(CX):
            column = jnp.broadcast_to(fields[0, x, :, 0:1], (8, ZT))
            inlet = inlet + jnp.where(lane == CY * x + sub, column, 0.0)
        inlet = jnp.broadcast_to(jnp.sum(inlet, axis=0, keepdims=True), (8, ZT))
        for tile in range(cells // 8):
            payload[pl.ds(8 * CHUNK * tile, 8, stride=CHUNK), :] = inlet


def lines(ref, index, row):
    found = [ref[pl.ds(128 * index + 8 * z + row, 8, stride=32), :] for z in range(NZ // ZT)]
    return jnp.concatenate(found, axis=1)


def second_half(array):
    return roll(array, 4, 0)


def row_of_colour_0(raw, row, lane):
    return jnp.where((lane + row) % 2 == 0, raw, roll(raw, -1, 0))


def interleaved(first, second, sub):
    return jnp.where(sub % 2 == 0, first, roll(second, 1, 0))


def opening_kernel(
    donors_far,
    returns_far,
    fields_far,
    sources_far,
    diagonal_far,
    inverse_far,
    m1_far,
    m2_far,
    b1_far,
    b2_far,
    s1_far,
    s2_far,
    payload_far,
    donors,
    returns,
    fields,
    sources,
    diagonal,
    inverse,
    m1,
    m2,
    b1,
    b2,
    s1,
    s2,
    payload,
    blocks,
    sems,
    out_sems,
):
    pairs = (
        (donors_far, donors),
        (returns_far, returns),
        (fields_far, fields),
        (sources_far, sources),
        (diagonal_far, diagonal),
    )
    bounds = [0, 12, 24, 36, T * T]
    pieces = [slice(CX * NZ // ZT * CY * a, CX * NZ // ZT * CY * b) for a, b in zip(bounds, bounds[1:])]
    pairs += tuple((inverse_far.at[piece], inverse.at[piece]) for piece in pieces)
    loads = [pltpu.make_async_copy(far, near, sems.at[n]) for n, (far, near) in enumerate(pairs)]
    for load in loads:
        load.start()
    place = Place()
    sends = []

    def send(*refs):
        for near, far, at in refs:
            copy = pltpu.make_async_copy(near.at[at], far.at[at], out_sems.at[len(sends)])
            copy.start()
            sends.append(copy)

    wait_for(loads[:3])
    section, odd, odd_y = place.section, place.odd_x, place.odd_y == 1
    even, even_z = even_mask(NZ), even_mask(ZT)
    for ref, pair in ((m1, 1 - odd), (m2, odd)):
        store_message(
            ref,
            lambda t: packed(fields[t, 2 * pair], fields[t, 2 * pair + 1], even, 1),
            lambda t: packed(fields[t, 2 * pair, :, :ZT], fields[t, 2 * pair + 1, :, :ZT], even_z, 0),
        )
    send((m1, m1_far, slice(0, VAL)), (m2, m2_far, slice(0, VAL)))
    fill_payload(place, donors, returns, fields, payload, blocks)
    send((payload, payload_far, slice(None)))
    wait_for(loads[3:5])
    sub, lane = iotas(NZ)

    def plane_of(ref, index, plane):
        at = [pl.multiple_of(8 * (4 * (CX * index + plane) + z), 8) for z in range(NZ // ZT)]
        return jnp.concatenate([ref[pl.ds(start, 8), :] for start in at], axis=1)

    def coefficient(index, plane):
        if index >= T * T:
            return plane_of(sources, index - T * T, plane)
        raw = plane_of(inverse, index, plane)
        return jnp.where(section == 0, plane_of(diagonal, index, plane), raw) if index < T else raw

    def x_tiles(begin, end):
        for ref, far in ((m1, 1 - odd), (m2, odd)):
            wanted = (sub + lane + far) % 2 == 0
            plane = far * (CX - 1)
            for tile in range(begin, end):
                first, second = coefficient(2 * tile, plane), coefficient(2 * tile + 1, plane)
                ref[VAL + tile] = jnp.where(wanted, first, roll(second, 1, 0))
        at = slice(VAL + begin, VAL + end)
        send((m1, m1_far, at), (m2, m2_far, at))

    def inverse_rows(tile, row):
        if tile + 1 == YBULK:
            return row_of_colour_0(second_half(lines(inverse, T * T - 2, row)), row, lane)
        first, second = (row_of_colour_0(lines(inverse, 4 * tile + 2 * n, row), row, lane) for n in (0, 1))
        return interleaved(first, second, sub)

    def pair(index, row):
        if index + 1 < T:
            return lines(sources, index, row)
        if index + 1 == T:
            halves = second_half(lines(sources, index - 1, row)), second_half(lines(diagonal, 0, row))
            return jnp.where(sub < 4, halves[0], halves[1])
        return lines(diagonal, index - T, row)

    def other_rows(tile, row):
        first = row_of_colour_0(pair(4 * tile, row), row, lane)
        if tile == 3:
            return first
        return interleaved(first, row_of_colour_0(pair(4 * tile + 2, row), row, lane), sub)

    def y_tiles(refs, rows_of, begin, end):
        first, second, first_far, second_far = refs
        for tile in range(begin, end):
            down, up = rows_of(tile, 0), rows_of(tile, CY - 1)
            first[tile] = jnp.where(odd_y, down, up)
            second[tile] = jnp.where(odd_y, up, down)
        at = slice(begin, end)
        send((first, first_far, at), (second, second_far, at))

    y_tiles((s1, s2, s1_far, s2_far), other_rows, 0, 4)
    for n, (begin, end) in enumerate(zip(bounds, bounds[1:])):
        loads[5 + n].wait()
        last = end == T * T
        x_tiles(begin // 2, XBULK if last else end // 2)
        y_tiles((b1, b2, b1_far, b2_far), inverse_rows, begin // 4, YBULK if last else end // 4)
    wait_for(sends)


def corner_values(m1, m2, r1, r2, y1, y2):
    place = Place()
    odd_x, odd_y = place.odd_x == 1, place.odd_y == 1
    sub, lane = iotas(NZ)
    even = even_mask(NZ)
    tiles = {}
    for t in range(VAL):
        a, b = m1[t], m2[t]
        own = jnp.where(odd_x, a, b), jnp.where(odd_x, b, a)
        for start in (0, 6):
            if t < T:
                base = 4 * (t % 2)
                rows = [roll(own[k], base + 2 * k - start, 0) for k in (0, 1)]
                both = jnp.where(sub < base + 2, rows[0], rows[1])
                tiles[start, t] = both
                c, d = r1[t], r2[t]
                from_low, from_high = jnp.where(odd_x, c, d), jnp.where(odd_x, d, c)
                ring = jnp.where(even, from_low, from_high)
                tiles[start, "ring", t] = roll(ring, t - (0 if start == 0 else CY - 1), 0)
            else:
                row = 0 if start == 0 else CY - 1
                rows = [roll(own[k], 4 + 2 * k + t - T - row, 0) for k in (0, 1)]
                tiles[start, t] = jnp.where(sub < 6, rows[0], rows[1])
    for tile in range(YVAL):
        sides = []
        for start in (0, 6):
            if tile < 3:
                sides.append(jnp.where(sub < 4, tiles[start, 2 * tile], tiles[start, 2 * tile + 1]))
            elif tile == 3:
                firsts = jnp.where(sub % 2 == 0, tiles[start, T], tiles[start, T + 1])
                sides.append(jnp.where(sub < 4, tiles[start, T - 1], firsts))
            else:
                laid = tiles[start, "ring", 0]
                for t in range(1, T):
                    laid = jnp.where(sub == t, tiles[start, "ring", t], laid)
                sides.append(laid)
        down, up = sides
        y1[tile] = jnp.where(odd_y, down, up)
        y2[tile] = jnp.where(odd_y, up, down)


def corner_kernel(m1, m2, r2, r1, y1, y2):
    corner_values(m1, m2, r1, r2, y1, y2)


def first_corner_kernel(m1, m2, r2, r1, s1, s2, y1, y2, heads, sems):
    pairs = [(ref.at[:VAL], heads.at[n]) for n, ref in enumerate((m1, m2, r1, r2))]
    pairs += [(s1, y1.at[YVAL:YHEAD]), (s2, y2.at[YVAL:YHEAD])]
    copies = [pltpu.make_async_copy(far, near, sems.at[n]) for n, (far, near) in enumerate(pairs)]
    for copy in copies:
        copy.start()
    wait_for(copies)
    corner_values(*[heads.at[n] for n in range(4)], y1, y2)


def interface_kernel(blocks, coupling, returns_far, *refs):
    count = (len(refs) - 5) // 2
    back, inflow, weights = refs[count : count + 3]
    returns, sems = refs[-2:]
    pairs = [(returns_far, returns), *zip(refs[:count], refs[count + 3 : -2])]
    copies = [pltpu.make_async_copy(far, near, sems.at[n]) for n, (far, near) in enumerate(pairs)]
    for copy in copies:
        copy.start()
    place = Place()
    back[...] = jnp.zeros_like(back)
    cells = blocks.shape[0] // (2 * CHUNK)

    def summed(n):
        total = jnp.zeros((8, ZT), F32)
        for tile in range(cells // 8):
            total = total + blocks[pl.ds(8 * CHUNK * tile + n, 8, stride=CHUNK), :]
        return jnp.broadcast_to(jnp.sum(total, axis=0, keepdims=True), (8, ZT))

    first, second = summed(0), summed(1)
    sub, lane = iotas(ZT)
    weight = jnp.zeros((8, ZT), F32)
    for t in range(T):
        weight = jnp.where(sub == t, coupling[t], weight)
    weights[...] = weight
    for row in range(16):
        found = jnp.full((8, ZT), -1, jnp.int32)
        for r, target in enumerate(chosen_places(row)):
            found = jnp.where(sub == r, target, found)
        parts = jnp.where(lane == found, first, 0.0) + jnp.where(lane + ZT == found, second, 0.0)
        inflow[8 * row : 8 * row + 8, :] = jnp.broadcast_to(jnp.sum(parts, axis=1, keepdims=True), (8, ZT))

    copies[0].wait()

    @pl.when(place.exit_side)
    def _():
        table = blocks[pl.ds(CHUNK * cells, cells, stride=CHUNK), :]
        sub, lane = iotas(ZT)

        def marks_of(y, n):
            line = jnp.zeros((8, ZT), F32)
            for tile in range(place.rows_y // 8):
                at = CHUNK * (cells - place.rows_y + 8 * tile) + n
                line = line + jnp.where(sub + 8 * tile == y, blocks[pl.ds(at, 8, stride=CHUNK), :], 0.0)
            line = jnp.broadcast_to(jnp.sum(line, axis=0, keepdims=True), (8, ZT))
            laid = line
            for t in range(1, T):
                laid = jnp.where(sub == t, roll(line, -MARKS * t, 1), laid)
            return laid

        high, low = marks_of(place.y + 1, 1), marks_of(place.y - 1, 0)
        slots = lax.broadcasted_iota(jnp.int32, (8, cells), 1).astype(F32)
        column = lax.broadcasted_iota(jnp.int32, table.shape, 1)
        spots = [jnp.where(column // BLK == q, roll(table, q * BLK, 1), 0.0) for q in range(ZT // BLK)]
        wanted = []
        for t in range(T):
            line = jnp.broadcast_to(returns[0:1, t * ZT : (t + 1) * ZT], (8, ZT))
            spread = line
            for y in range(1, CY):
                spread = jnp.where(sub == y, roll(line, -y * MARKS, 1), spread)
            wanted.append(spread.astype(F32))
        wanted += [high, low]
        for tile in range(NZ // ZT):
            laid = jnp.zeros((8 * len(wanted), ZT), F32)
            for q in range(ZT // BLK):
                block = tile * (ZT // BLK) + q
                match = jnp.concatenate([want[:, block : block + 1] == slots for want in wanted], axis=0)
                laid = laid + jnp.dot(
                    match.astype(F32), spots[q], precision=lax.Precision.HIGHEST, preferred_element_type=F32
                )
            at = slice(tile * ZT, (tile + 1) * ZT)
            for t in range(T):
                back[t, 0:8, at] = laid[8 * t : 8 * t + 8]
                back[t, 8:9, at] = laid[8 * T + t : 8 * T + t + 1]
                back[t, 15:16, at] = laid[8 * T + 8 + t : 8 * T + 9 + t]

    wait_for(copies[1:])


def sweep_kernel(
    last, weights, fields, sources, diagonal, inverse, x2, x1, za, ya, zb, yb, back, inflow, *rest
):
    r2, r1, y2, y1 = rest[:4] if len(rest) > 5 else (x2, x1, za, ya)
    u0, u1 = rest[-2:]
    place = Place()
    section, odd_x, odd_y, exit_side = place.section, place.odd_x, place.odd_y, place.exit_side
    even, even_z = even_mask(NZ), even_mask(ZT)
    sub, lane = iotas(NZ)
    sub_z, _ = iotas(ZT)
    colours = (u0, u1)
    own, edge = slice(0, 8), slice(8, 16)

    for t in range(T):
        for k in (0, 1):
            u1[t, k + 1, own] = packed(fields[t, 2 * k], fields[t, 2 * k + 1], even, 1)
            u0[t, k + 1, own] = packed(fields[t, 2 * k], fields[t, 2 * k + 1], even, 0)
        for ref, tile, at, width in (
            (u1, t, slice(0, NZ), NZ),
            (u0, T + t // 4, slice(t % 4 * ZT, (t % 4 + 1) * ZT), ZT),
        ):
            low = jnp.where(odd_x == 1, r1[tile, :, at], r2[tile, :, at])
            high = jnp.where(odd_x == 1, r2[tile, :, at], r1[tile, :, at])
            ref[t, 0, own, :width] = low
            ref[t, 3, own, :width] = high
    own_rows, own_rows_z = (lax.broadcasted_iota(jnp.int32, (8, width), 0) for width in (NZ, ZT))

    def beside(tile, rows, at):
        first, second = y1[tile, rows, at], y2[tile, rows, at]
        low, high = jnp.where(odd_y == 1, first, second), jnp.where(odd_y == 1, second, first)
        return low, high

    whole = slice(0, NZ)
    for t in range(T):
        low, high = beside(t // 2, slice(0, 8), whole)
        for k in (0, 1):
            base = 4 * (t % 2) + 2 * k
            u1[t, k + 1, edge] = jnp.where(own_rows < 2, roll(high, -base, 0), roll(low, 6 - base, 0))
            row, at = 4 + 2 * k + t // 4, slice(t % 4 * ZT, (t % 4 + 1) * ZT)
            above, below = beside(3, slice(row, row + 1), at)
            u0[t, k + 1, edge, :ZT] = jnp.where(own_rows_z < 4, below, above)
        above, below = beside(4, slice(t, t + 1), whole)
        corner = jnp.where(own_rows < 4, below, above)
        u1[t, 0, edge] = corner
        u1[t, 3, edge] = corner

    @pl.when(exit_side)
    def _():
        for t in range(T):
            u0[t, 3] = back[t]
            u1[t, 3] = back[t]

    def around(centre, beyond):
        up = roll(jnp.where(sub == 0, beyond, centre), -1, 0)
        down = roll(jnp.where(sub == 7, beyond, centre), 1, 0)
        return up + down

    def planes(colour, unit, t):
        old, new = colours[colour], colours[1 - colour]
        if unit == "ring":
            centre = jnp.where(even, new[t, 0, own], new[t, 3, own])
            beyond = jnp.where(even, new[t, 0, edge], new[t, 3, edge])
            x_sum = jnp.where(even, new[t, 3, own] + new[t, 2, own], new[t, 0, own] + new[t, 1, own])
            return centre, beyond, x_sum, jnp.where(even, old[t, 3, own], old[t, 0, own])
        p, rows = unit
        here, other = (own, edge) if rows == 0 else (edge, own)
        centre, beyond = new[t, p, here], new[t, p, other]
        below, above = new[t, p - 1, here], new[t, p + 1, here]
        x_sum = centre + (jnp.where(even, below, above) if colour == 0 else jnp.where(even, above, below))
        return centre, beyond, x_sum, old[t, p, here]

    def inflow_of(colour, unit):
        base = 64 * colour
        if unit == "ring":
            values = jnp.where(even_z, inflow[base + 48 : base + 56], inflow[base : base + 8])
        else:
            start = base + 16 * unit[0] + 8 * unit[1]
            values = inflow[start : start + 8]
        return jnp.concatenate([values] * (NZ // ZT), axis=1)

    ring_mask = (sub + lane + odd_x) % 2 == 0
    edge_mask = jnp.where(sub == 7, 1, 0) == odd_y

    def of_ring(index):
        tile = VAL + index // 2
        if index % 2 == 0:
            return jnp.where(ring_mask, x1[tile], x2[tile])
        return roll(jnp.where(ring_mask, x2[tile], x1[tile]), -1, 0)

    def of_edge(first, second, tile, index, p):
        tile, row = tile + index // 4, 4 * (index % 2) + 2 * (p - 1) + index % 4 // 2
        return jnp.where(edge_mask, first[tile, row : row + 1], second[tile, row : row + 1])

    def taken(colour, unit, kind, index):
        if unit == "ring":
            return of_ring(T * T + index if kind == "source" else index)
        p, rows = unit
        if rows == 0:
            if kind == "inverse":
                raw = inverse.at[index // T, index % T]
            else:
                raw = (sources if kind == "source" else diagonal).at[index]
            return packed(raw[2 * p - 2], raw[2 * p - 1], even, colour)
        if kind == "inverse":
            return of_edge(yb, zb, 0, index, p)
        return of_edge(ya, za, YVAL, index if kind == "source" else T + index, p)

    def put(colour, unit, t, value):
        ref = colours[colour]
        if unit == "ring":
            ref[t, 0, own] = value
            ref[t, 3, own] = jnp.where(exit_side, back[t, own], value)
        else:
            ref[t, unit[0], own if unit[1] == 0 else edge] = value

    def valid(unit):
        if unit == "ring":
            return jnp.where(even, place.rows_x - 1 - place.x, place.x) > 0
        if unit[1] == 0:
            return None
        return jnp.where(sub == 7, place.y, place.rows_y - 1 - place.y) > 0

    def turbine(colour, unit):
        driving = []
        for t in range(T):
            centre, beyond, x_sum, kept = planes(colour, unit, t)
            start = inflow_of(colour, unit) if t == 0 else kept
            ahead = jnp.where(lane == NZ - 1, 0.0, roll(centre, -1, 1))
            behind = jnp.where(lane == 0, start, roll(centre, 1, 1))
            total = x_sum + around(centre, beyond) + ahead + behind
            source = taken(colour, unit, "source", t)
            weight = jnp.concatenate([jnp.broadcast_to(weights[t : t + 1], (8, ZT))] * (NZ // ZT), axis=1)
            driving.append(source + weight * total)
        for s in range(T):
            value = taken(colour, unit, "inverse", T * s) * driving[0]
            for t in range(1, T):
                value = value + taken(colour, unit, "inverse", T * s + t) * driving[t]
            put(colour, unit, s, value)

    def combustor(colour, unit):
        before = None
        current = planes(colour, unit, 0)
        flag = valid(unit)
        for t in range(T):
            after = planes(colour, unit, t + 1) if t + 1 < T else None
            centre, beyond, x_sum, _ = current
            edge_ahead = 0.0 if after is None else roll(after[0], -1, 1)
            edge_behind = 0.0 if before is None else roll(before, 1, 1)
            ahead = jnp.where(lane == NZ - 1, edge_ahead, roll(centre, -1, 1))
            behind = jnp.where(lane == 0, edge_behind, roll(centre, 1, 1))
            total = x_sum + around(centre, beyond) + ahead + behind
            source = taken(colour, unit, "source", t)
            value = (source + total) / (6.0 + taken(colour, unit, "diagonal", t))
            if flag is not None:
                value = jnp.where(flag, value, 0.0)
            put(colour, unit, t, value)
            before, current = centre, after

    def both(step):
        for unit in ((1, 0), (2, 0), (1, 1), (2, 1), "ring"):
            step(0, unit)
        for unit in ((1, 0), (2, 0)):
            step(1, unit)

    pl.when(section == 0)(functools.partial(both, combustor))
    pl.when(section != 0)(functools.partial(both, turbine))

    out = rest[-3] if last else rest[-5]
    for t in range(T):
        for k in (0, 1):
            a, b = u0[t, k + 1, own], u1[t, k + 1, own]
            out[t, 2 * k] = jnp.where(even, a, b)
            out[t, 2 * k + 1] = jnp.where(even, b, a)
    if last:
        return
    for ref, pair in ((rest[-4], 2 - odd_x), (rest[-3], 1 + odd_x)):
        store_message(ref, lambda t: u1[t, pair, own], lambda t: u0[t, pair, own, :ZT])


def shape(*dims):
    return jax.ShapeDtypeStruct(dims, F32)


SMEM = pl.BlockSpec(memory_space=pltpu.SMEM)
VMEM = pl.BlockSpec(memory_space=pltpu.VMEM)
ANY = pl.BlockSpec(memory_space=pl.ANY)
HBM = pl.BlockSpec(memory_space=pltpu.HBM)


def call(kernel, outs, operands, out_specs=None, scratch=(), limit=24):
    return pl.pallas_call(
        kernel,
        out_shape=outs,
        in_specs=[spec for spec, _ in operands],
        out_specs=out_specs or [VMEM] * len(outs),
        scratch_shapes=list(scratch),
        compiler_params=pltpu.CompilerParams(vmem_limit_bytes=limit << 20),
    )(*[operand for _, operand in operands])


def far(array):
    return HBM, pltpu.with_memory_space_constraint(array, pltpu.HBM)


def swaps(axis, first, second, turbine_only=False):
    peers = lax.axis_size(axis)
    inner = [(i, i ^ 1) for i in range(peers)]
    outer = [(i, (i + 1 ^ 1) - 1) for i in range(1, peers - 1)]
    if turbine_only:
        inner, outer = ([(2 * i + 1, 2 * j + 1) for i, j in pairs] for pairs in (inner, outer))
        axis = (axis, "sa")
    second = lax.ppermute(second, axis, outer)
    return lax.ppermute(first, axis, inner), second


def chosen_places(tile):
    places = []
    for index in range(8 * tile, 8 * tile + 8):
        c, p, r = index // 64, index // 16 % 4, index % 16
        y = r if r < 12 else r - 16
        x = 2 * (p - 1) + (c if r % 2 == 0 else 1 - c)
        block = None
        if 0 <= x < CX and 0 <= y < CY:
            block = (0, x, y)
        elif x == -1 and 0 <= y < CY:
            block = (1, CX - 1, y)
        elif x == CX and 0 <= y < CY:
            block = (2, 0, y)
        elif 0 <= x < CX and y == -1:
            block = (3, x, CY - 1)
        elif 0 <= x < CX and y == CY:
            block = (4, x, 0)
        places.append(-1 if block is None else BLK * block[0] + CY * block[1] + block[2])
    return places


def shards(fields, sources, diagonal, block_inverse, coupling, donors, returns):
    values = fields[0]
    source = sources[0]
    rows_x, rows_y = lax.axis_size("gx"), lax.axis_size("gy")
    cells = rows_x * rows_y
    flat = [
        array.reshape(-1, CY, NZ // ZT, ZT).transpose(0, 2, 1, 3).reshape(-1, ZT)
        for array in (source, diagonal, block_inverse)
    ]
    near = (returns, values, *flat)
    messages = [(tiles, 8, NZ) for tiles in [VAL + XBULK] * 2 + [YBULK] * 2 + [4] * 2] + [(2 * CHUNK * cells, ZT)]
    m1, m2, yb, zb, s1, s2, payload = call(
        opening_kernel,
        [pltpu.HBM(dims, F32) for dims in messages],
        [far(array) for array in (donors.T, *near)],
        [HBM] * len(messages),
        [pltpu.SMEM(donors.T.shape, donors.dtype)]
        + [pltpu.VMEM(array.shape, array.dtype) for array in near]
        + [pltpu.VMEM(dims, F32) for dims in messages]
        + [pltpu.VMEM((cells, ZT), F32), pltpu.SemaphoreType.DMA((9,)), pltpu.SemaphoreType.DMA((21,))],
    )
    x1, x2 = swaps("gx", m1, m2)
    yb, zb = swaps("gy", yb, zb, turbine_only=True)
    arrived = lax.all_to_all(
        payload.reshape(2 * cells, 1, CHUNK * ZT), ("sa", "gx", "gy"), split_axis=0, concat_axis=0, tiled=True
    ).reshape(2 * CHUNK * cells, ZT)
    arrived, x1, x2 = lax.optimization_barrier((arrived, x1, x2))
    ya, za = call(
        first_corner_kernel,
        [shape(YHEAD, 8, NZ)] * 2,
        [far(m1), far(m2), (ANY, x2), (ANY, x1), far(s1), far(s2)],
        scratch=[pltpu.VMEM((4, VAL, 8, NZ), F32), pltpu.SemaphoreType.DMA((6,))],
    )
    ya, za = swaps("gy", ya, za)
    distant = (values, source, diagonal, block_inverse)
    made = call(
        interface_kernel,
        [shape(T, 16, NZ), shape(128, ZT), shape(8, ZT)] + [pltpu.VMEM(array.shape, array.dtype) for array in distant],
        [(VMEM, arrived), (SMEM, pltpu.with_memory_space_constraint(coupling, pltpu.HBM)), far(returns)]
        + [far(array) for array in distant],
        scratch=[pltpu.VMEM(returns.shape, returns.dtype), pltpu.SemaphoreType.DMA((len(distant) + 1,))],
    )
    back, inflow, weights, values, source, diagonal, block_inverse = made

    for sweep in range(SWEEPS):
        received = []
        if sweep > 0:
            r1, r2 = swaps("gx", m1, m2)
            y1, y2 = call(
                corner_kernel, [shape(YVAL, 8, NZ)] * 2, [(VMEM, array) for array in (m1, m2, r2, r1)]
            )
            received = [r2, r1, *swaps("gy", y1, y2)[::-1]]
        last = sweep == SWEEPS - 1
        results = call(
            functools.partial(sweep_kernel, last),
            [shape(T, CX, CY, NZ)] + [shape(VAL, 8, NZ)] * (0 if last else 2),
            [(VMEM, array) for array in (weights, values, source, diagonal, block_inverse)]
            + [(VMEM, array) for array in (x2, x1, za, ya, zb, yb, back, inflow, *received)],
            scratch=[pltpu.VMEM((T, 4, 16, NZ), F32)] * 2,
            limit=40,
        )
        values, m1, m2 = results if not last else (results[0], None, None)
    return values[None]


def solution(mesh):
    return jax.shard_map(
        shards,
        mesh=mesh,
        in_specs=(
            P("sa", None, "gx", "gy", None),
            P("sa", None, "gx", "gy", None),
            P(None, "gx", "gy", None),
            P(None, None, "gx", "gy", None),
            P(),
            P(),
            P("gy", None),
        ),
        out_specs=P("sa", None, "gx", "gy", None),
        check_vma=False,
    )
```

```python
import functools
import jax
import jax.numpy as jnp
from jax import lax
from jax.experimental import pallas as pl
from jax.experimental.pallas import tpu as pltpu
from jax.sharding import PartitionSpec as P

SWEEPS = 4
BLK = 32
T = 7
CX = 4
CY = 8
NZ = 512
ZT = 128
VAL = T + 2
COEF = T * T + T
XBULK = COEF // 2
MARKS = NZ // BLK
CHUNK = 2
YVAL = 5
YHEAD = YVAL + 4
YBULK = T * T // 4 + 1
F32 = jnp.float32


def iotas(width):
    sub = lax.broadcasted_iota(jnp.int32, (8, width), 0)
    lane = lax.broadcasted_iota(jnp.int32, (8, width), 1)
    return sub, lane


def even_mask(width):
    sub, lane = iotas(width)
    return (sub + lane) % 2 == 0


def roll(array, shift, axis):
    size = array.shape[axis]
    shift = shift % size
    return array if shift == 0 else pltpu.roll(array, shift, axis)


def packed(pair_low, pair_high, even, colour):
    return jnp.where(even, pair_low, pair_high) if colour == 0 else jnp.where(even, pair_high, pair_low)


class Place:
    def __init__(self):
        self.rows_x = lax.axis_size("gx")
        self.section, self.x, self.y = (lax.axis_index(axis) for axis in ("sa", "gx", "gy"))
        self.rows_y = lax.axis_size("gy")
        self.odd_x, self.odd_y = lax.rem(self.x, 2), lax.rem(self.y, 2)
        self.exit_side = (self.section == 0) & (self.x == self.rows_x - 1)


def store_message(ref, ones, zeros_first):
    for t in range(T):
        ref[t] = ones(t)
        ref[T + t // 4, :, (t % 4) * ZT : (t % 4 + 1) * ZT] = zeros_first(t)
    ref[T + 1, :, 3 * ZT :] = jnp.zeros((8, ZT), F32)


def wait_for(copies):
    for copy in copies:
        copy.wait()


def lines(ref, index, row):
    found = [ref[pl.ds(128 * index + 8 * z + row, 8, stride=32), :] for z in range(NZ // ZT)]
    return jnp.concatenate(found, axis=1)


def second_half(array):
    return roll(array, 4, 0)


def row_of_colour_0(raw, row, lane):
    return jnp.where((lane + row) % 2 == 0, raw, roll(raw, -1, 0))


def interleaved(first, second, sub):
    return jnp.where(sub % 2 == 0, first, roll(second, 1, 0))


def fill_payload(place, donors, returns, fields, payload, blocks):
    sub, lane = iotas(ZT)
    payload[...] = jnp.zeros_like(payload)
    cells = blocks.shape[0]

    @pl.when(place.exit_side)
    def _():
        for entry in range(cells):
            gy, block, slot = donors[0, entry], donors[1, entry], donors[2, entry]
            piece, row, column = block // 128, block % 128 // 16, block % 16
            start = pl.multiple_of(column // 4 * ZT, ZT)
            found = fields[piece, CX - 1, :, pl.ds(start, ZT)]
            found = pltpu.roll(pltpu.roll(found, (8 - row) % 8, 0), (ZT - column % 4 * BLK) % ZT, 1)
            blocks[pl.ds(slot, 1), :] = jnp.where((lane < BLK) & (gy == place.y), found, 0.0)[:1]
        marks = [jnp.zeros((8, ZT), F32)] * 2
        for t in range(T):
            line = jnp.broadcast_to(returns[0:1, t * ZT : (t + 1) * ZT], (8, ZT)).astype(F32)
            for n, row in enumerate((CY - 1, 0)):
                turned = roll(line, MARKS * (t - row), 1)
                marks[n] = jnp.where(lane // MARKS == t, turned, marks[n])
        for tile in range(cells // 8):
            for n in (0, 1):
                payload[pl.ds(8 * CHUNK * tile + n, 8, stride=CHUNK), :] = marks[n]
        tiles = cells // 8
        zero = jnp.zeros((8, ZT), F32)
        for tile in range(tiles):
            here = blocks[8 * tile : 8 * tile + 8]
            below = blocks[8 * tile - 8 : 8 * tile] if tile > 0 else zero
            above = blocks[8 * tile + 8 : 8 * tile + 16] if tile + 1 < tiles else zero
            left = jnp.where(sub == 0, 0.0, roll(here, 1, 0))
            right = jnp.where(sub == 7, 0.0, roll(here, -1, 0))
            wide = here + roll(below, BLK, 1) + roll(above, 2 * BLK, 1) + roll(left, 3 * BLK, 1)
            payload[pl.ds(CHUNK * (cells + 8 * tile), 8, stride=CHUNK), :] = wide
            payload[pl.ds(CHUNK * (cells + 8 * tile) + 1, 8, stride=CHUNK), :] = right

    @pl.when(place.section == 1)
    def _():
        inlet = jnp.zeros((8, ZT), F32)
        for x in range(CX):
            column = jnp.broadcast_to(fields[0, x, :, 0:1], (8, ZT))
            inlet = inlet + jnp.where(lane == CY * x + sub, column, 0.0)
        inlet = jnp.broadcast_to(jnp.sum(inlet, axis=0, keepdims=True), (8, ZT))
        for tile in range(cells // 8):
            payload[pl.ds(8 * CHUNK * tile, 8, stride=CHUNK), :] = inlet


def lines(ref, index, row):
    found = [ref[pl.ds(128 * index + 8 * z + row, 8, stride=32), :] for z in range(NZ // ZT)]
    return jnp.concatenate(found, axis=1)


def second_half(array):
    return roll(array, 4, 0)


def row_of_colour_0(raw, row, lane):
    return jnp.where((lane + row) % 2 == 0, raw, roll(raw, -1, 0))


def interleaved(first, second, sub):
    return jnp.where(sub % 2 == 0, first, roll(second, 1, 0))


def opening_kernel(
    donors_far,
    returns_far,
    fields_far,
    sources_far,
    diagonal_far,
    inverse_far,
    m1_far,
    m2_far,
    b1_far,
    b2_far,
    s1_far,
    s2_far,
    payload_far,
    donors,
    returns,
    fields,
    sources,
    diagonal,
    inverse,
    m1,
    m2,
    b1,
    b2,
    s1,
    s2,
    payload,
    blocks,
    sems,
    out_sems,
):
    pairs = (
        (donors_far, donors),
        (returns_far, returns),
        (fields_far, fields),
        (sources_far, sources),
        (diagonal_far, diagonal),
    )
    bounds = [0, 12, 24, 36, T * T]
    pieces = [slice(CX * NZ // ZT * CY * a, CX * NZ // ZT * CY * b) for a, b in zip(bounds, bounds[1:])]
    pairs += tuple((inverse_far.at[piece], inverse.at[piece]) for piece in pieces)
    loads = [pltpu.make_async_copy(far, near, sems.at[n]) for n, (far, near) in enumerate(pairs)]
    for load in loads:
        load.start()
    place = Place()
    sends = []

    def send(*refs):
        for near, far, at in refs:
            copy = pltpu.make_async_copy(near.at[at], far.at[at], out_sems.at[len(sends)])
            copy.start()
            sends.append(copy)

    wait_for(loads[:3])
    section, odd, odd_y = place.section, place.odd_x, place.odd_y == 1
    even, even_z = even_mask(NZ), even_mask(ZT)
    for ref, pair in ((m1, 1 - odd), (m2, odd)):
        store_message(
            ref,
            lambda t: packed(fields[t, 2 * pair], fields[t, 2 * pair + 1], even, 1),
            lambda t: packed(fields[t, 2 * pair, :, :ZT], fields[t, 2 * pair + 1, :, :ZT], even_z, 0),
        )
    send((m1, m1_far, slice(0, VAL)), (m2, m2_far, slice(0, VAL)))
    fill_payload(place, donors, returns, fields, payload, blocks)
    send((payload, payload_far, slice(None)))
    wait_for(loads[3:5])
    sub, lane = iotas(NZ)

    def plane_of(ref, index, plane):
        at = [pl.multiple_of(8 * (4 * (CX * index + plane) + z), 8) for z in range(NZ // ZT)]
        return jnp.concatenate([ref[pl.ds(start, 8), :] for start in at], axis=1)

    def coefficient(index, plane):
        if index >= T * T:
            return plane_of(sources, index - T * T, plane)
        raw = plane_of(inverse, index, plane)
        return jnp.where(section == 0, plane_of(diagonal, index, plane), raw) if index < T else raw

    def x_tiles(begin, end):
        for ref, far in ((m1, 1 - odd), (m2, odd)):
            wanted = (sub + lane + far) % 2 == 0
            plane = far * (CX - 1)
            for tile in range(begin, end):
                first, second = coefficient(2 * tile, plane), coefficient(2 * tile + 1, plane)
                ref[VAL + tile] = jnp.where(wanted, first, roll(second, 1, 0))
        at = slice(VAL + begin, VAL + end)
        send((m1, m1_far, at), (m2, m2_far, at))

    def inverse_rows(tile, row):
        if tile + 1 == YBULK:
            return row_of_colour_0(second_half(lines(inverse, T * T - 2, row)), row, lane)
        first, second = (row_of_colour_0(lines(inverse, 4 * tile + 2 * n, row), row, lane) for n in (0, 1))
        return interleaved(first, second, sub)

    def pair(index, row):
        if index + 1 < T:
            return lines(sources, index, row)
        if index + 1 == T:
            halves = second_half(lines(sources, index - 1, row)), second_half(lines(diagonal, 0, row))
            return jnp.where(sub < 4, halves[0], halves[1])
        return lines(diagonal, index - T, row)

    def other_rows(tile, row):
        first = row_of_colour_0(pair(4 * tile, row), row, lane)
        if tile == 3:
            return first
        return interleaved(first, row_of_colour_0(pair(4 * tile + 2, row), row, lane), sub)

    def y_tiles(refs, rows_of, begin, end):
        first, second, first_far, second_far = refs
        for tile in range(begin, end):
            down, up = rows_of(tile, 0), rows_of(tile, CY - 1)
            first[tile] = jnp.where(odd_y, down, up)
            second[tile] = jnp.where(odd_y, up, down)
        at = slice(begin, end)
        send((first, first_far, at), (second, second_far, at))

    y_tiles((s1, s2, s1_far, s2_far), other_rows, 0, 4)
    for n, (begin, end) in enumerate(zip(bounds, bounds[1:])):
        loads[5 + n].wait()
        last = end == T * T
        x_tiles(begin // 2, XBULK if last else end // 2)
        y_tiles((b1, b2, b1_far, b2_far), inverse_rows, begin // 4, YBULK if last else end // 4)
    wait_for(sends)


def corner_values(m1, m2, r1, r2, y1, y2):
    place = Place()
    odd_x, odd_y = place.odd_x == 1, place.odd_y == 1
    sub, lane = iotas(NZ)
    even = even_mask(NZ)
    tiles = {}
    for t in range(m1.shape[0]):
        a, b = m1[t], m2[t]
        own = jnp.where(odd_x, a, b), jnp.where(odd_x, b, a)
        for start in (0, 6):
            if t < T:
                base = 4 * (t % 2)
                rows = [roll(own[k], base + 2 * k - start, 0) for k in (0, 1)]
                both = jnp.where(sub < base + 2, rows[0], rows[1])
                tiles[start, t] = both
                c, d = r1[t], r2[t]
                from_low, from_high = jnp.where(odd_x, c, d), jnp.where(odd_x, d, c)
                ring = jnp.where(even, from_low, from_high)
                tiles[start, "ring", t] = roll(ring, t - (0 if start == 0 else CY - 1), 0)
            else:
                row = 0 if start == 0 else CY - 1
                rows = [roll(own[k], 4 + 2 * k + t - T - row, 0) for k in (0, 1)]
                tiles[start, t] = jnp.where(sub < 6, rows[0], rows[1])
    for tile in range(YVAL):
        sides = []
        for start in (0, 6):
            if tile < 3:
                sides.append(jnp.where(sub < 4, tiles[start, 2 * tile], tiles[start, 2 * tile + 1]))
            elif tile == 3:
                laid = tiles[start, T - 1]
                if m1.shape[0] > T:
                    firsts = jnp.where(sub % 2 == 0, tiles[start, T], tiles[start, T + 1])
                    laid = jnp.where(sub < 4, laid, firsts)
                sides.append(laid)
            else:
                laid = tiles[start, "ring", 0]
                for t in range(1, T):
                    laid = jnp.where(sub == t, tiles[start, "ring", t], laid)
                sides.append(laid)
        down, up = sides
        y1[tile] = jnp.where(odd_y, down, up)
        y2[tile] = jnp.where(odd_y, up, down)


def corner_kernel(m1, m2, r2, r1, y1, y2):
    corner_values(m1, m2, r1, r2, y1, y2)


def first_corner_kernel(m1, m2, r2, r1, s1, s2, y1, y2, heads, sems):
    pairs = [(ref.at[:VAL], heads.at[n]) for n, ref in enumerate((m1, m2, r1, r2))]
    pairs += [(s1, y1.at[YVAL:YHEAD]), (s2, y2.at[YVAL:YHEAD])]
    copies = [pltpu.make_async_copy(far, near, sems.at[n]) for n, (far, near) in enumerate(pairs)]
    for copy in copies:
        copy.start()
    wait_for(copies)
    corner_values(*[heads.at[n] for n in range(4)], y1, y2)


def interface_kernel(blocks, coupling, returns_far, *refs):
    count = (len(refs) - 5) // 2
    back, inflow, weights = refs[count : count + 3]
    returns, sems = refs[-2:]
    pairs = [(returns_far, returns), *zip(refs[:count], refs[count + 3 : -2])]
    copies = [pltpu.make_async_copy(far, near, sems.at[n]) for n, (far, near) in enumerate(pairs)]
    for copy in copies:
        copy.start()
    place = Place()
    back[...] = jnp.zeros_like(back)
    cells = blocks.shape[0] // (2 * CHUNK)

    def summed(n):
        total = jnp.zeros((8, ZT), F32)
        for tile in range(cells // 8):
            total = total + blocks[pl.ds(8 * CHUNK * tile + n, 8, stride=CHUNK), :]
        return jnp.broadcast_to(jnp.sum(total, axis=0, keepdims=True), (8, ZT))

    first, second = summed(0), summed(1)
    sub, lane = iotas(ZT)
    weight = jnp.zeros((8, ZT), F32)
    for t in range(T):
        weight = jnp.where(sub == t, coupling[t], weight)
    weights[...] = weight
    for row in range(16):
        found = jnp.full((8, ZT), -1, jnp.int32)
        for r, target in enumerate(chosen_places(row)):
            found = jnp.where(sub == r, target, found)
        parts = jnp.where(lane == found, first, 0.0) + jnp.where(lane + ZT == found, second, 0.0)
        inflow[8 * row : 8 * row + 8, :] = jnp.broadcast_to(jnp.sum(parts, axis=1, keepdims=True), (8, ZT))

    copies[0].wait()

    @pl.when(place.exit_side)
    def _():
        table = blocks[pl.ds(CHUNK * cells, cells, stride=CHUNK), :]
        sub, lane = iotas(ZT)

        def marks_of(y, n):
            line = jnp.zeros((8, ZT), F32)
            for tile in range(place.rows_y // 8):
                at = CHUNK * (cells - place.rows_y + 8 * tile) + n
                line = line + jnp.where(sub + 8 * tile == y, blocks[pl.ds(at, 8, stride=CHUNK), :], 0.0)
            line = jnp.broadcast_to(jnp.sum(line, axis=0, keepdims=True), (8, ZT))
            laid = line
            for t in range(1, T):
                laid = jnp.where(sub == t, roll(line, -MARKS * t, 1), laid)
            return laid

        high, low = marks_of(place.y + 1, 1), marks_of(place.y - 1, 0)
        slots = lax.broadcasted_iota(jnp.int32, (8, cells), 1).astype(F32)
        column = lax.broadcasted_iota(jnp.int32, table.shape, 1)
        spots = [jnp.where(column // BLK == q, roll(table, q * BLK, 1), 0.0) for q in range(ZT // BLK)]
        wanted = []
        for t in range(T):
            line = jnp.broadcast_to(returns[0:1, t * ZT : (t + 1) * ZT], (8, ZT))
            spread = line
            for y in range(1, CY):
                spread = jnp.where(sub == y, roll(line, -y * MARKS, 1), spread)
            wanted.append(spread.astype(F32))
        wanted += [high, low]
        for tile in range(NZ // ZT):
            laid = jnp.zeros((8 * len(wanted), ZT), F32)
            for q in range(ZT // BLK):
                block = tile * (ZT // BLK) + q
                match = jnp.concatenate([want[:, block : block + 1] == slots for want in wanted], axis=0)
                laid = laid + jnp.dot(
                    match.astype(F32), spots[q], precision=lax.Precision.HIGHEST, preferred_element_type=F32
                )
            at = slice(tile * ZT, (tile + 1) * ZT)
            for t in range(T):
                back[t, 0:8, at] = laid[8 * t : 8 * t + 8]
                back[t, 8:9, at] = laid[8 * T + t : 8 * T + t + 1]
                back[t, 15:16, at] = laid[8 * T + 8 + t : 8 * T + 9 + t]

    wait_for(copies[1:])


OWN, EDGE = slice(0, 8), slice(8, 16)


class Halves:
    def __init__(self, own, edge):
        self.own, self.edge = own, edge

    def __getitem__(self, at):
        t, p, rows = at
        return (self.own if rows is OWN else self.edge)[t, p]

    def __setitem__(self, at, value):
        t, p, rows = at
        (self.own if rows is OWN else self.edge)[t, p] = value


def steps(place, weights, sources, diagonal, inverse, x1, x2, ya, za, yb, zb, back, inflow, u0, u1, kept, put, partial=None, store=None):
    odd_x, odd_y, exit_side = place.odd_x, place.odd_y, place.exit_side
    even, even_z = even_mask(NZ), even_mask(ZT)
    sub, lane = iotas(NZ)
    own, edge = OWN, EDGE

    zero = jnp.zeros((8, NZ), F32)
    places = {(1, 0): 0, (2, 0): 1, "ring": 2}

    def beyond_ring(t):
        return jnp.where(even, u1[t, 0, edge], u1[t, 3, edge])

    def finished(unit, t, weight):
        beyond = beyond_ring(t) if unit == "ring" else u1[t, unit[0], edge]
        halo = around(zero, beyond)
        return partial[places[unit], t] + (halo if weight is None else weight * halo)

    def from_partial(colour, unit):
        return partial is not None and colour == 0 and unit in places

    def around(centre, beyond):
        up = roll(jnp.where(sub == 0, beyond, centre), -1, 0)
        down = roll(jnp.where(sub == 7, beyond, centre), 1, 0)
        return up + down

    def planes(colour, unit, t):
        old, new = (kept, u1) if colour == 0 else (u1, u0)
        if unit == "ring":
            centre = jnp.where(even, new[t, 0, own], new[t, 3, own])
            beyond = zero if store is not None else beyond_ring(t)
            x_sum = jnp.where(even, new[t, 3, own] + new[t, 2, own], new[t, 0, own] + new[t, 1, own])
            return centre, beyond, x_sum, jnp.where(even, old[t, 3, own], old[t, 0, own])
        p, rows = unit
        here, other = (own, edge) if rows == 0 else (edge, own)
        centre = new[t, p, here]
        beyond = zero if store is not None else new[t, p, other]
        below, above = new[t, p - 1, here], new[t, p + 1, here]
        x_sum = centre + (jnp.where(even, below, above) if colour == 0 else jnp.where(even, above, below))
        return centre, beyond, x_sum, old[t, p, here]

    def inflow_of(colour, unit):
        base = 64 * colour
        if unit == "ring":
            values = jnp.where(even_z, inflow[base + 48 : base + 56], inflow[base : base + 8])
        else:
            start = base + 16 * unit[0] + 8 * unit[1]
            values = inflow[pl.ds(pl.multiple_of(start, 8), 8)]
        return jnp.concatenate([values] * (NZ // ZT), axis=1)

    ring_mask = (sub + lane + odd_x) % 2 == 0
    edge_mask = jnp.where(sub == 7, 1, 0) == odd_y

    def of_ring(index):
        tile = VAL + index // 2
        if index % 2 == 0:
            return jnp.where(ring_mask, x1[tile], x2[tile])
        return roll(jnp.where(ring_mask, x2[tile], x1[tile]), -1, 0)

    def of_edge(first, second, tile, index, p):
        tile, row = tile + index // 4, 4 * (index % 2) + 2 * (p - 1) + index % 4 // 2
        return jnp.where(edge_mask, first[tile, row : row + 1], second[tile, row : row + 1])

    def taken(colour, unit, kind, index):
        if unit == "ring":
            return of_ring(T * T + index if kind == "source" else index)
        p, rows = unit
        if rows == 0:
            if kind == "inverse":
                raw = inverse.at[index // T, index % T]
            else:
                raw = (sources if kind == "source" else diagonal).at[index]
            return packed(raw[2 * p - 2], raw[2 * p - 1], even, colour)
        if kind == "inverse":
            return of_edge(yb, zb, 0, index, p)
        return of_edge(ya, za, YVAL, index if kind == "source" else T + index, p)

    def valid(unit):
        if unit == "ring":
            return jnp.where(even, place.rows_x - 1 - place.x, place.x) > 0
        if unit[1] == 0:
            return None
        return jnp.where(sub == 7, place.y, place.rows_y - 1 - place.y) > 0

    def turbine(colour, unit):
        driving = []
        for t in range(T):
            weight = jnp.concatenate([jnp.broadcast_to(weights[t : t + 1], (8, ZT))] * (NZ // ZT), axis=1)
            if from_partial(colour, unit):
                driving.append(finished(unit, t, weight))
                continue
            centre, beyond, x_sum, kept = planes(colour, unit, t)
            start = inflow_of(colour, unit) if t == 0 else kept
            ahead = jnp.where(lane == NZ - 1, 0.0, roll(centre, -1, 1))
            behind = jnp.where(lane == 0, start, roll(centre, 1, 1))
            total = x_sum + around(centre, beyond) + ahead + behind
            source = taken(colour, unit, "source", t)
            driving.append(source + weight * total)
            if store is not None:
                store[places[unit], t] = driving[t]
        if store is not None:
            return
        for s in range(T):
            value = taken(colour, unit, "inverse", T * s) * driving[0]
            for t in range(1, T):
                value = value + taken(colour, unit, "inverse", T * s + t) * driving[t]
            put(colour, unit, s, value)

    def combustor(colour, unit):
        before = None
        started = from_partial(colour, unit)
        current = None if started else planes(colour, unit, 0)
        flag = valid(unit)

        def finish(t, total):
            value = total / (6.0 + taken(colour, unit, "diagonal", t))
            if flag is not None:
                value = jnp.where(flag, value, 0.0)
            put(colour, unit, t, value)

        for t in range(T):
            if started:
                finish(t, finished(unit, t, None))
                continue
            after = planes(colour, unit, t + 1) if t + 1 < T else None
            centre, beyond, x_sum, _ = current
            edge_ahead = 0.0 if after is None else roll(after[0], -1, 1)
            edge_behind = 0.0 if before is None else roll(before, 1, 1)
            ahead = jnp.where(lane == NZ - 1, edge_ahead, roll(centre, -1, 1))
            behind = jnp.where(lane == 0, edge_behind, roll(centre, 1, 1))
            total = x_sum + around(centre, beyond) + ahead + behind
            total = taken(colour, unit, "source", t) + total
            if store is not None:
                store[places[unit], t] = total
            else:
                finish(t, total)
            before, current = centre, after

    return combustor, turbine


def by_section(place, two, units):
    def run(step):
        for colour, unit in units:
            step(colour, unit)

    pl.when(place.section == 0)(functools.partial(run, two[0]))
    pl.when(place.section != 0)(functools.partial(run, two[1]))


FIRST_COLOUR = [(0, unit) for unit in ((1, 0), (2, 0), (1, 1), (2, 1), "ring")]


def sweep_kernel(
    begins, ends, weights, sources, diagonal, inverse, x2, x1, za, ya, zb, yb, back, inflow, *rest
):
    place = Place()
    odd_x, odd_y, exit_side = place.odd_x, place.odd_y, place.exit_side
    even = even_mask(NZ)
    if begins:
        fields, outs = rest[0], rest[1:]
        r2, r1, y2, y1 = x2, x1, za, ya
    else:
        kept, near, partial, y2, y1, *outs = rest
    if ends:
        out, u0, u1, second = outs
    else:
        first_sent, second_sent, u0, u1 = outs
    if begins:
        kept, partial = u0, None
    else:
        u1 = Halves(near, u1)
    own, edge = OWN, EDGE
    own_rows, own_rows_z = (lax.broadcasted_iota(jnp.int32, (8, width), 0) for width in (NZ, ZT))

    def beside(tile, rows, at):
        first, second = y1[tile, rows, at], y2[tile, rows, at]
        low, high = jnp.where(odd_y == 1, first, second), jnp.where(odd_y == 1, second, first)
        return low, high

    whole = slice(0, NZ)
    for t in range(T):
        if begins:
            a, b = r1[t], r2[t]
            u1[t, 0, own] = jnp.where(odd_x == 1, a, b)
            u1[t, 3, own] = jnp.where(odd_x == 1, b, a)
            for k in (0, 1):
                u1[t, k + 1, own] = packed(fields[t, 2 * k], fields[t, 2 * k + 1], even, 1)
                u0[t, k + 1, own] = packed(fields[t, 2 * k], fields[t, 2 * k + 1], even, 0)
            tile, at = T + t // 4, slice(t % 4 * ZT, (t % 4 + 1) * ZT)
            a, b = r1[tile, :, at], r2[tile, :, at]
            u0[t, 0, own, :ZT] = jnp.where(odd_x == 1, a, b)
            u0[t, 3, own, :ZT] = jnp.where(odd_x == 1, b, a)
        low, high = beside(t // 2, slice(0, 8), whole)
        for k in (0, 1):
            base = 4 * (t % 2) + 2 * k
            u1[t, k + 1, edge] = jnp.where(own_rows < 2, roll(high, -base, 0), roll(low, 6 - base, 0))
            if begins:
                row, at = 4 + 2 * k + t // 4, slice(t % 4 * ZT, (t % 4 + 1) * ZT)
                above, below = beside(3, slice(row, row + 1), at)
                u0[t, k + 1, edge, :ZT] = jnp.where(own_rows_z < 4, below, above)
        above, below = beside(4, slice(t, t + 1), whole)
        corner = jnp.where(own_rows < 4, below, above)
        u1[t, 0, edge] = corner
        u1[t, 3, edge] = corner

    @pl.when(exit_side)
    def _():
        for t in range(T):
            u1[t, 3, edge] = back[t, edge]
            if begins:
                u1[t, 3, own] = back[t, own]

    pair_1, pair_2 = 2 - odd_x, 1 + odd_x

    def put(colour, unit, t, value):
        if unit == "ring":
            u0[t, 0, own] = value
            u0[t, 3, own] = jnp.where(exit_side, back[t, own], value)
        elif colour == 1 and ends:
            second[t, unit[0] - 1] = value
        elif colour == 1:
            (first_sent if unit[0] is pair_1 else second_sent)[t] = value
        else:
            (u0, u1)[colour][t, unit[0], own if unit[1] == 0 else edge] = value

    two = steps(place, weights, sources, diagonal, inverse, x1, x2, ya, za, yb, zb, back, inflow, u0, u1, kept, put, partial)
    by_section(place, two, FIRST_COLOUR)
    if not ends:
        by_section(place, two, [(1, (pair_2, 0)), (1, (pair_1, 0))])
        return
    by_section(place, two, [(1, (1, 0)), (1, (2, 0))])
    for t in range(T):
        for k in (0, 1):
            a, b = u0[t, k + 1, own], second[t, k]
            out[t, 2 * k] = jnp.where(even, a, b)
            out[t, 2 * k + 1] = jnp.where(even, b, a)


def sums_kernel(weights, sources, diagonal, inverse, x2, x1, back, inflow, m1, m2, kept, r2, r1, near, sums):
    place = Place()
    odd_x, exit_side = place.odd_x, place.exit_side
    for t in range(T):
        for low, high, below, above in ((r2[t], r1[t], 0, 3), (m2[t], m1[t], 1, 2)):
            near[t, below] = jnp.where(odd_x == 1, high, low)
            near[t, above] = jnp.where(odd_x == 1, low, high)

    @pl.when(exit_side)
    def _():
        for t in range(T):
            near[t, 3] = back[t, OWN]

    ones = Halves(near, None)
    none = [None] * 4
    two = steps(place, weights, sources, diagonal, inverse, x1, x2, *none, back, inflow, None, ones, kept, None, None, sums)
    by_section(place, two, [(0, (1, 0)), (0, (2, 0)), (0, "ring")])


def shape(*dims):
    return jax.ShapeDtypeStruct(dims, F32)


SMEM = pl.BlockSpec(memory_space=pltpu.SMEM)
VMEM = pl.BlockSpec(memory_space=pltpu.VMEM)
ANY = pl.BlockSpec(memory_space=pl.ANY)
HBM = pl.BlockSpec(memory_space=pltpu.HBM)


def call(kernel, outs, operands, out_specs=None, scratch=(), limit=24):
    return pl.pallas_call(
        kernel,
        out_shape=outs,
        in_specs=[spec for spec, _ in operands],
        out_specs=out_specs or [VMEM] * len(outs),
        scratch_shapes=list(scratch),
        compiler_params=pltpu.CompilerParams(vmem_limit_bytes=limit << 20),
    )(*[operand for _, operand in operands])


def far(array):
    return HBM, pltpu.with_memory_space_constraint(array, pltpu.HBM)


def swap(axis, pairs, array, turbine_only):
    if turbine_only:
        pairs = [(2 * i + 1, 2 * j + 1) for i, j in pairs]
        axis = (axis, "sa")
    return lax.ppermute(array, axis, pairs)


def inner_swap(axis, array, turbine_only=False):
    return swap(axis, [(i, i ^ 1) for i in range(lax.axis_size(axis))], array, turbine_only)


def outer_swap(axis, array, turbine_only=False):
    pairs = [(i, (i + 1 ^ 1) - 1) for i in range(1, lax.axis_size(axis) - 1)]
    return swap(axis, pairs, array, turbine_only)


def swaps(axis, first, second, turbine_only=False):
    second = outer_swap(axis, second, turbine_only)
    return inner_swap(axis, first, turbine_only), second


def chosen_places(tile):
    places = []
    for index in range(8 * tile, 8 * tile + 8):
        c, p, r = index // 64, index // 16 % 4, index % 16
        y = r if r < 12 else r - 16
        x = 2 * (p - 1) + (c if r % 2 == 0 else 1 - c)
        block = None
        if 0 <= x < CX and 0 <= y < CY:
            block = (0, x, y)
        elif x == -1 and 0 <= y < CY:
            block = (1, CX - 1, y)
        elif x == CX and 0 <= y < CY:
            block = (2, 0, y)
        elif 0 <= x < CX and y == -1:
            block = (3, x, CY - 1)
        elif 0 <= x < CX and y == CY:
            block = (4, x, 0)
        places.append(-1 if block is None else BLK * block[0] + CY * block[1] + block[2])
    return places


def shards(fields, sources, diagonal, block_inverse, coupling, donors, returns):
    values = fields[0]
    source = sources[0]
    rows_x, rows_y = lax.axis_size("gx"), lax.axis_size("gy")
    cells = rows_x * rows_y
    flat = [
        array.reshape(-1, CY, NZ // ZT, ZT).transpose(0, 2, 1, 3).reshape(-1, ZT)
        for array in (source, diagonal, block_inverse)
    ]
    near = (returns, values, *flat)
    messages = [(tiles, 8, NZ) for tiles in [VAL + XBULK] * 2 + [YBULK] * 2 + [4] * 2] + [(2 * CHUNK * cells, ZT)]
    m1, m2, yb, zb, s1, s2, payload = call(
        opening_kernel,
        [pltpu.HBM(dims, F32) for dims in messages],
        [far(array) for array in (donors.T, *near)],
        [HBM] * len(messages),
        [pltpu.SMEM(donors.T.shape, donors.dtype)]
        + [pltpu.VMEM(array.shape, array.dtype) for array in near]
        + [pltpu.VMEM(dims, F32) for dims in messages]
        + [pltpu.VMEM((cells, ZT), F32), pltpu.SemaphoreType.DMA((9,)), pltpu.SemaphoreType.DMA((21,))],
    )
    x1, x2 = swaps("gx", m1, m2)
    yb, zb = swaps("gy", yb, zb, turbine_only=True)
    arrived = lax.all_to_all(
        payload.reshape(2 * cells, 1, CHUNK * ZT), ("sa", "gx", "gy"), split_axis=0, concat_axis=0, tiled=True
    ).reshape(2 * CHUNK * cells, ZT)
    arrived, x1, x2 = lax.optimization_barrier((arrived, x1, x2))
    ya, za = call(
        first_corner_kernel,
        [shape(YHEAD, 8, NZ)] * 2,
        [far(m1), far(m2), (ANY, x2), (ANY, x1), far(s1), far(s2)],
        scratch=[pltpu.VMEM((4, VAL, 8, NZ), F32), pltpu.SemaphoreType.DMA((6,))],
    )
    ya, za = swaps("gy", ya, za)
    distant = (values, source, diagonal, block_inverse)
    made = call(
        interface_kernel,
        [shape(T, 16, NZ), shape(128, ZT), shape(8, ZT)] + [pltpu.VMEM(array.shape, array.dtype) for array in distant],
        [(VMEM, arrived), (SMEM, pltpu.with_memory_space_constraint(coupling, pltpu.HBM)), far(returns)]
        + [far(array) for array in distant],
        scratch=[pltpu.VMEM(returns.shape, returns.dtype), pltpu.SemaphoreType.DMA((len(distant) + 1,))],
    )
    back, inflow, weights, values, source, diagonal, block_inverse = made

    coefficients = [weights, source, diagonal, block_inverse]
    given = [*coefficients, x2, x1, za, ya, zb, yb, back, inflow]
    block, half = pltpu.VMEM((T, 4, 16, NZ), F32), pltpu.VMEM((T, 4, 8, NZ), F32)
    state = [values]
    for sweep in range(SWEEPS):
        begins, ends = sweep == 0, sweep == SWEEPS - 1
        results = call(
            functools.partial(sweep_kernel, begins, ends),
            [shape(T, CX, CY, NZ)] if ends else [shape(T, 8, NZ)] * 2 + [shape(*block.shape)],
            [(VMEM, array) for array in (*given, *state)],
            scratch=([block] if ends else [])
            + [block if begins else half]
            + ([pltpu.VMEM((T, 2, 8, NZ), F32)] if ends else []),
            limit=40,
        )
        if ends:
            break
        m1, m2, u0 = results
        r1, r2 = swaps("gx", m1, m2)
        y1, y2 = call(corner_kernel, [shape(YVAL, 8, NZ)] * 2, [(VMEM, array) for array in (m1, m2, r2, r1)])
        y1, y2 = swaps("gy", y1, y2)
        near, sums = call(
            sums_kernel,
            [shape(*half.shape), shape(3, T, 8, NZ)],
            [(VMEM, array) for array in (*coefficients, x2, x1, back, inflow, m1, m2, u0, r2, r1)],
            limit=40,
        )
        state = [u0, near, sums, y2, y1]
    return results[0][None]


def solution(mesh):
    return jax.shard_map(
        shards,
        mesh=mesh,
        in_specs=(
            P("sa", None, "gx", "gy", None),
            P("sa", None, "gx", "gy", None),
            P(None, "gx", "gy", None),
            P(None, None, "gx", "gy", None),
            P(),
            P(),
            P("gy", None),
        ),
        out_specs=P("sa", None, "gx", "gy", None),
        check_vma=False,
    )
```

```python
import functools
import jax
import jax.numpy as jnp
from jax import lax
from jax.experimental import pallas as pl
from jax.experimental.pallas import tpu as pltpu
from jax.sharding import PartitionSpec as P

SWEEPS = 4
BLK = 32
T = 7
CX = 4
CY = 8
NZ = 512
ZT = 128
VAL = T + 2
COEF = T * T + T
XBULK = COEF // 2
MARKS = NZ // BLK
CHUNK = 2
YVAL = 5
YHEAD = YVAL + 4
YBULK = T * T // 4 + 1
F32 = jnp.float32


def iotas(width):
    sub = lax.broadcasted_iota(jnp.int32, (8, width), 0)
    lane = lax.broadcasted_iota(jnp.int32, (8, width), 1)
    return sub, lane


def even_mask(width):
    sub, lane = iotas(width)
    return (sub + lane) % 2 == 0


def roll(array, shift, axis):
    size = array.shape[axis]
    shift = shift % size
    return array if shift == 0 else pltpu.roll(array, shift, axis)


def packed(pair_low, pair_high, even, colour):
    return jnp.where(even, pair_low, pair_high) if colour == 0 else jnp.where(even, pair_high, pair_low)


class Place:
    def __init__(self):
        self.rows_x = lax.axis_size("gx")
        self.section, self.x, self.y = (lax.axis_index(axis) for axis in ("sa", "gx", "gy"))
        self.rows_y = lax.axis_size("gy")
        self.odd_x, self.odd_y = lax.rem(self.x, 2), lax.rem(self.y, 2)
        self.exit_side = (self.section == 0) & (self.x == self.rows_x - 1)


def store_message(ref, ones, zeros_first):
    for t in range(T):
        ref[t] = ones(t)
        ref[T + t // 4, :, (t % 4) * ZT : (t % 4 + 1) * ZT] = zeros_first(t)
    ref[T + 1, :, 3 * ZT :] = jnp.zeros((8, ZT), F32)


def wait_for(copies):
    for copy in copies:
        copy.wait()


def lines(ref, index, row):
    found = [ref[pl.ds(128 * index + 8 * z + row, 8, stride=32), :] for z in range(NZ // ZT)]
    return jnp.concatenate(found, axis=1)


def second_half(array):
    return roll(array, 4, 0)


def row_of_colour_0(raw, row, lane):
    return jnp.where((lane + row) % 2 == 0, raw, roll(raw, -1, 0))


def interleaved(first, second, sub):
    return jnp.where(sub % 2 == 0, first, roll(second, 1, 0))


def fill_payload(place, donors, returns, fields, payload, blocks):
    sub, lane = iotas(ZT)
    payload[...] = jnp.zeros_like(payload)
    cells = blocks.shape[0]

    @pl.when(place.exit_side)
    def _():
        for entry in range(cells):
            gy, block, slot = donors[0, entry], donors[1, entry], donors[2, entry]
            piece, row, column = block // 128, block % 128 // 16, block % 16
            start = pl.multiple_of(column // 4 * ZT, ZT)
            found = fields[piece, CX - 1, :, pl.ds(start, ZT)]
            found = pltpu.roll(pltpu.roll(found, (8 - row) % 8, 0), (ZT - column % 4 * BLK) % ZT, 1)
            blocks[pl.ds(slot, 1), :] = jnp.where((lane < BLK) & (gy == place.y), found, 0.0)[:1]
        marks = [jnp.zeros((8, ZT), F32)] * 2
        for t in range(T):
            line = jnp.broadcast_to(returns[0:1, t * ZT : (t + 1) * ZT], (8, ZT)).astype(F32)
            for n, row in enumerate((CY - 1, 0)):
                turned = roll(line, MARKS * (t - row), 1)
                marks[n] = jnp.where(lane // MARKS == t, turned, marks[n])
        for tile in range(cells // 8):
            for n in (0, 1):
                payload[pl.ds(8 * CHUNK * tile + n, 8, stride=CHUNK), :] = marks[n]
        tiles = cells // 8
        zero = jnp.zeros((8, ZT), F32)
        for tile in range(tiles):
            here = blocks[8 * tile : 8 * tile + 8]
            below = blocks[8 * tile - 8 : 8 * tile] if tile > 0 else zero
            above = blocks[8 * tile + 8 : 8 * tile + 16] if tile + 1 < tiles else zero
            left = jnp.where(sub == 0, 0.0, roll(here, 1, 0))
            right = jnp.where(sub == 7, 0.0, roll(here, -1, 0))
            wide = here + roll(below, BLK, 1) + roll(above, 2 * BLK, 1) + roll(left, 3 * BLK, 1)
            payload[pl.ds(CHUNK * (cells + 8 * tile), 8, stride=CHUNK), :] = wide
            payload[pl.ds(CHUNK * (cells + 8 * tile) + 1, 8, stride=CHUNK), :] = right

    @pl.when(place.section == 1)
    def _():
        inlet = jnp.zeros((8, ZT), F32)
        for x in range(CX):
            column = jnp.broadcast_to(fields[0, x, :, 0:1], (8, ZT))
            inlet = inlet + jnp.where(lane == CY * x + sub, column, 0.0)
        inlet = jnp.broadcast_to(jnp.sum(inlet, axis=0, keepdims=True), (8, ZT))
        for tile in range(cells // 8):
            payload[pl.ds(8 * CHUNK * tile, 8, stride=CHUNK), :] = inlet


def lines(ref, index, row):
    found = [ref[pl.ds(128 * index + 8 * z + row, 8, stride=32), :] for z in range(NZ // ZT)]
    return jnp.concatenate(found, axis=1)


def second_half(array):
    return roll(array, 4, 0)


def row_of_colour_0(raw, row, lane):
    return jnp.where((lane + row) % 2 == 0, raw, roll(raw, -1, 0))


def interleaved(first, second, sub):
    return jnp.where(sub % 2 == 0, first, roll(second, 1, 0))


def opening_kernel(
    donors_far,
    returns_far,
    fields_far,
    sources_far,
    diagonal_far,
    inverse_far,
    m1_far,
    m2_far,
    b1_far,
    b2_far,
    s1_far,
    s2_far,
    payload_far,
    donors,
    returns,
    fields,
    sources,
    diagonal,
    inverse,
    m1,
    m2,
    b1,
    b2,
    s1,
    s2,
    payload,
    blocks,
    sems,
    out_sems,
):
    pairs = (
        (donors_far, donors),
        (returns_far, returns),
        (fields_far, fields),
        (sources_far, sources),
        (diagonal_far, diagonal),
    )
    bounds = [0, 12, 24, 36, T * T]
    pieces = [slice(CX * NZ // ZT * CY * a, CX * NZ // ZT * CY * b) for a, b in zip(bounds, bounds[1:])]
    pairs += tuple((inverse_far.at[piece], inverse.at[piece]) for piece in pieces)
    loads = [pltpu.make_async_copy(far, near, sems.at[n]) for n, (far, near) in enumerate(pairs)]
    for load in loads:
        load.start()
    place = Place()
    sends = []

    def send(*refs):
        for near, far, at in refs:
            copy = pltpu.make_async_copy(near.at[at], far.at[at], out_sems.at[len(sends)])
            copy.start()
            sends.append(copy)

    wait_for(loads[:3])
    section, odd, odd_y = place.section, place.odd_x, place.odd_y == 1
    even, even_z = even_mask(NZ), even_mask(ZT)
    for ref, pair in ((m1, 1 - odd), (m2, odd)):
        store_message(
            ref,
            lambda t: packed(fields[t, 2 * pair], fields[t, 2 * pair + 1], even, 1),
            lambda t: packed(fields[t, 2 * pair, :, :ZT], fields[t, 2 * pair + 1, :, :ZT], even_z, 0),
        )
    send((m1, m1_far, slice(0, VAL)), (m2, m2_far, slice(0, VAL)))
    fill_payload(place, donors, returns, fields, payload, blocks)
    send((payload, payload_far, slice(None)))
    wait_for(loads[3:5])
    sub, lane = iotas(NZ)

    def plane_of(ref, index, plane):
        at = [pl.multiple_of(8 * (4 * (CX * index + plane) + z), 8) for z in range(NZ // ZT)]
        return jnp.concatenate([ref[pl.ds(start, 8), :] for start in at], axis=1)

    def coefficient(index, plane):
        if index >= T * T:
            return plane_of(sources, index - T * T, plane)
        raw = plane_of(inverse, index, plane)
        return jnp.where(section == 0, plane_of(diagonal, index, plane), raw) if index < T else raw

    def x_tiles(begin, end):
        for ref, far in ((m1, 1 - odd), (m2, odd)):
            wanted = (sub + lane + far) % 2 == 0
            plane = far * (CX - 1)
            for tile in range(begin, end):
                first, second = coefficient(2 * tile, plane), coefficient(2 * tile + 1, plane)
                ref[VAL + tile] = jnp.where(wanted, first, roll(second, 1, 0))
        at = slice(VAL + begin, VAL + end)
        send((m1, m1_far, at), (m2, m2_far, at))

    def inverse_rows(tile, row):
        if tile + 1 == YBULK:
            return row_of_colour_0(second_half(lines(inverse, T * T - 2, row)), row, lane)
        first, second = (row_of_colour_0(lines(inverse, 4 * tile + 2 * n, row), row, lane) for n in (0, 1))
        return interleaved(first, second, sub)

    def pair(index, row):
        if index + 1 < T:
            return lines(sources, index, row)
        if index + 1 == T:
            halves = second_half(lines(sources, index - 1, row)), second_half(lines(diagonal, 0, row))
            return jnp.where(sub < 4, halves[0], halves[1])
        return lines(diagonal, index - T, row)

    def other_rows(tile, row):
        first = row_of_colour_0(pair(4 * tile, row), row, lane)
        if tile == 3:
            return first
        return interleaved(first, row_of_colour_0(pair(4 * tile + 2, row), row, lane), sub)

    def y_tiles(refs, rows_of, begin, end):
        first, second, first_far, second_far = refs
        for tile in range(begin, end):
            down, up = rows_of(tile, 0), rows_of(tile, CY - 1)
            first[tile] = jnp.where(odd_y, down, up)
            second[tile] = jnp.where(odd_y, up, down)
        at = slice(begin, end)
        send((first, first_far, at), (second, second_far, at))

    y_tiles((s1, s2, s1_far, s2_far), other_rows, 0, 4)
    for n, (begin, end) in enumerate(zip(bounds, bounds[1:])):
        loads[5 + n].wait()
        last = end == T * T
        x_tiles(begin // 2, XBULK if last else end // 2)
        y_tiles((b1, b2, b1_far, b2_far), inverse_rows, begin // 4, YBULK if last else end // 4)
    wait_for(sends)


def corner_values(m1, m2, r1, r2, y1, y2):
    place = Place()
    odd_x, odd_y = place.odd_x == 1, place.odd_y == 1
    sub, lane = iotas(NZ)
    even = even_mask(NZ)
    tiles = {}
    for t in range(m1.shape[0]):
        a, b = m1[t], m2[t]
        own = jnp.where(odd_x, a, b), jnp.where(odd_x, b, a)
        for start in (0, 6):
            if t < T:
                base = 4 * (t % 2)
                rows = [roll(own[k], base + 2 * k - start, 0) for k in (0, 1)]
                both = jnp.where(sub < base + 2, rows[0], rows[1])
                tiles[start, t] = both
                c, d = r1[t], r2[t]
                from_low, from_high = jnp.where(odd_x, c, d), jnp.where(odd_x, d, c)
                ring = jnp.where(even, from_low, from_high)
                tiles[start, "ring", t] = roll(ring, t - (0 if start == 0 else CY - 1), 0)
            else:
                row = 0 if start == 0 else CY - 1
                rows = [roll(own[k], 4 + 2 * k + t - T - row, 0) for k in (0, 1)]
                tiles[start, t] = jnp.where(sub < 6, rows[0], rows[1])
    for tile in range(YVAL):
        sides = []
        for start in (0, 6):
            if tile < 3:
                sides.append(jnp.where(sub < 4, tiles[start, 2 * tile], tiles[start, 2 * tile + 1]))
            elif tile == 3:
                laid = tiles[start, T - 1]
                if m1.shape[0] > T:
                    firsts = jnp.where(sub % 2 == 0, tiles[start, T], tiles[start, T + 1])
                    laid = jnp.where(sub < 4, laid, firsts)
                sides.append(laid)
            else:
                laid = tiles[start, "ring", 0]
                for t in range(1, T):
                    laid = jnp.where(sub == t, tiles[start, "ring", t], laid)
                sides.append(laid)
        down, up = sides
        y1[tile] = jnp.where(odd_y, down, up)
        y2[tile] = jnp.where(odd_y, up, down)


def corner_kernel(m1, m2, r2, r1, y1, y2):
    corner_values(m1, m2, r1, r2, y1, y2)


def first_corner_kernel(m1, m2, r2, r1, s1, s2, y1, y2, heads, sems):
    pairs = [(ref.at[:VAL], heads.at[n]) for n, ref in enumerate((m1, m2, r1, r2))]
    pairs += [(s1, y1.at[YVAL:YHEAD]), (s2, y2.at[YVAL:YHEAD])]
    copies = [pltpu.make_async_copy(far, near, sems.at[n]) for n, (far, near) in enumerate(pairs)]
    for copy in copies:
        copy.start()
    wait_for(copies)
    corner_values(*[heads.at[n] for n in range(4)], y1, y2)


def interface_kernel(
    blocks,
    coupling,
    x2,
    x1,
    returns_far,
    fields_far,
    sources_far,
    diagonal_far,
    inverse_far,
    back,
    inflow,
    weights,
    fields,
    sources,
    diagonal,
    chosen,
    ring,
    returns,
    inverse,
    sems,
):
    pairs = [
        (returns_far, returns),
        (inverse_far, inverse),
        (fields_far, fields),
        (sources_far, sources),
        (diagonal_far, diagonal),
    ]
    copies = [pltpu.make_async_copy(far, near, sems.at[n]) for n, (far, near) in enumerate(pairs)]
    for copy in copies:
        copy.start()
    place = Place()
    back[...] = jnp.zeros_like(back)
    cells = blocks.shape[0] // (2 * CHUNK)

    def summed(n):
        total = jnp.zeros((8, ZT), F32)
        for tile in range(cells // 8):
            total = total + blocks[pl.ds(8 * CHUNK * tile + n, 8, stride=CHUNK), :]
        return jnp.broadcast_to(jnp.sum(total, axis=0, keepdims=True), (8, ZT))

    first, second = summed(0), summed(1)
    sub, lane = iotas(ZT)
    weight = jnp.zeros((8, ZT), F32)
    for t in range(T):
        weight = jnp.where(sub == t, coupling[t], weight)
    weights[...] = weight
    for row in range(16):
        found = jnp.full((8, ZT), -1, jnp.int32)
        for r, target in enumerate(chosen_places(row)):
            found = jnp.where(sub == r, target, found)
        parts = jnp.where(lane == found, first, 0.0) + jnp.where(lane + ZT == found, second, 0.0)
        inflow[8 * row : 8 * row + 8, :] = jnp.broadcast_to(jnp.sum(parts, axis=1, keepdims=True), (8, ZT))

    copies[0].wait()

    @pl.when(place.exit_side)
    def _():
        table = blocks[pl.ds(CHUNK * cells, cells, stride=CHUNK), :]
        sub, lane = iotas(ZT)

        def marks_of(y, n):
            line = jnp.zeros((8, ZT), F32)
            for tile in range(place.rows_y // 8):
                at = CHUNK * (cells - place.rows_y + 8 * tile) + n
                line = line + jnp.where(sub + 8 * tile == y, blocks[pl.ds(at, 8, stride=CHUNK), :], 0.0)
            line = jnp.broadcast_to(jnp.sum(line, axis=0, keepdims=True), (8, ZT))
            laid = line
            for t in range(1, T):
                laid = jnp.where(sub == t, roll(line, -MARKS * t, 1), laid)
            return laid

        high, low = marks_of(place.y + 1, 1), marks_of(place.y - 1, 0)
        slots = lax.broadcasted_iota(jnp.int32, (8, cells), 1).astype(F32)
        column = lax.broadcasted_iota(jnp.int32, table.shape, 1)
        spots = [jnp.where(column // BLK == q, roll(table, q * BLK, 1), 0.0) for q in range(ZT // BLK)]
        wanted = []
        for t in range(T):
            line = jnp.broadcast_to(returns[0:1, t * ZT : (t + 1) * ZT], (8, ZT))
            spread = line
            for y in range(1, CY):
                spread = jnp.where(sub == y, roll(line, -y * MARKS, 1), spread)
            wanted.append(spread.astype(F32))
        wanted += [high, low]
        for tile in range(NZ // ZT):
            laid = jnp.zeros((8 * len(wanted), ZT), F32)
            for q in range(ZT // BLK):
                block = tile * (ZT // BLK) + q
                match = jnp.concatenate([want[:, block : block + 1] == slots for want in wanted], axis=0)
                laid = laid + jnp.dot(
                    match.astype(F32), spots[q], precision=lax.Precision.HIGHEST, preferred_element_type=F32
                )
            at = slice(tile * ZT, (tile + 1) * ZT)
            for t in range(T):
                back[t, 0:8, at] = laid[8 * t : 8 * t + 8]
                back[t, 8:9, at] = laid[8 * T + t : 8 * T + t + 1]
                back[t, 15:16, at] = laid[8 * T + 8 + t : 8 * T + 9 + t]

    even = even_mask(NZ)
    wide, long = iotas(NZ)
    ring_mask = (wide + long + place.odd_x) % 2 == 0
    for index in range(COEF):
        tile = VAL + index // 2
        if index % 2 == 0:
            ring[index] = jnp.where(ring_mask, x1[tile], x2[tile])
        else:
            ring[index] = roll(jnp.where(ring_mask, x2[tile], x1[tile]), -1, 0)
    copies[1].wait()
    for index in range(T * T):
        for k in (0, 1):
            a, b = (inverse[index // T, index % T, 2 * k + n] for n in (0, 1))
            chosen[0, index, k] = packed(a, b, even, 0)
            chosen[1, index, k] = packed(a, b, even, 1)
    wait_for(copies[2:])


OWN, EDGE = slice(0, 8), slice(8, 16)


class Halves:
    def __init__(self, own, edge):
        self.own, self.edge = own, edge

    def __getitem__(self, at):
        t, p, rows = at
        return (self.own if rows is OWN else self.edge)[t, p]

    def __setitem__(self, at, value):
        t, p, rows = at
        (self.own if rows is OWN else self.edge)[t, p] = value


def steps(place, weights, sources, diagonal, inverse, ring, ya, za, yb, zb, back, inflow, u0, u1, kept, put, partial=None, store=None):
    odd_x, odd_y, exit_side = place.odd_x, place.odd_y, place.exit_side
    even, even_z = even_mask(NZ), even_mask(ZT)
    sub, lane = iotas(NZ)
    own, edge = OWN, EDGE

    zero = jnp.zeros((8, NZ), F32)
    places = {(1, 0): 0, (2, 0): 1, "ring": 2}

    def beyond_ring(t):
        return jnp.where(even, u1[t, 0, edge], u1[t, 3, edge])

    def finished(unit, t, weight):
        beyond = beyond_ring(t) if unit == "ring" else u1[t, unit[0], edge]
        halo = around(zero, beyond)
        return partial[places[unit], t] + (halo if weight is None else weight * halo)

    def from_partial(colour, unit):
        return partial is not None and colour == 0 and unit in places

    def around(centre, beyond):
        up = roll(jnp.where(sub == 0, beyond, centre), -1, 0)
        down = roll(jnp.where(sub == 7, beyond, centre), 1, 0)
        return up + down

    def planes(colour, unit, t):
        old, new = (kept, u1) if colour == 0 else (u1, u0)
        if unit == "ring":
            centre = jnp.where(even, new[t, 0, own], new[t, 3, own])
            beyond = zero if store is not None else beyond_ring(t)
            x_sum = jnp.where(even, new[t, 3, own] + new[t, 2, own], new[t, 0, own] + new[t, 1, own])
            return centre, beyond, x_sum, jnp.where(even, old[t, 3, own], old[t, 0, own])
        p, rows = unit
        here, other = (own, edge) if rows == 0 else (edge, own)
        centre = new[t, p, here]
        beyond = zero if store is not None else new[t, p, other]
        below, above = new[t, p - 1, here], new[t, p + 1, here]
        x_sum = centre + (jnp.where(even, below, above) if colour == 0 else jnp.where(even, above, below))
        return centre, beyond, x_sum, old[t, p, here]

    def inflow_of(colour, unit):
        base = 64 * colour
        if unit == "ring":
            values = jnp.where(even_z, inflow[base + 48 : base + 56], inflow[base : base + 8])
        else:
            start = base + 16 * unit[0] + 8 * unit[1]
            values = inflow[pl.ds(pl.multiple_of(start, 8), 8)]
        return jnp.concatenate([values] * (NZ // ZT), axis=1)

    edge_mask = jnp.where(sub == 7, 1, 0) == odd_y

    def of_edge(first, second, tile, index, p):
        tile, row = tile + index // 4, 4 * (index % 2) + 2 * (p - 1) + index % 4 // 2
        return jnp.where(edge_mask, first[tile, row : row + 1], second[tile, row : row + 1])

    def taken(colour, unit, kind, index):
        if unit == "ring":
            return ring[T * T + index if kind == "source" else index]
        p, rows = unit
        if rows == 0:
            if kind == "inverse":
                return inverse[colour, index, p - 1]
            raw = (sources if kind == "source" else diagonal).at[index]
            return packed(raw[2 * p - 2], raw[2 * p - 1], even, colour)
        if kind == "inverse":
            return of_edge(yb, zb, 0, index, p)
        return of_edge(ya, za, YVAL, index if kind == "source" else T + index, p)

    def valid(unit):
        if unit == "ring":
            return jnp.where(even, place.rows_x - 1 - place.x, place.x) > 0
        if unit[1] == 0:
            return None
        return jnp.where(sub == 7, place.y, place.rows_y - 1 - place.y) > 0

    def turbine(colour, unit):
        driving = []
        for t in range(T):
            weight = jnp.concatenate([jnp.broadcast_to(weights[t : t + 1], (8, ZT))] * (NZ // ZT), axis=1)
            if from_partial(colour, unit):
                driving.append(finished(unit, t, weight))
                continue
            centre, beyond, x_sum, kept = planes(colour, unit, t)
            start = inflow_of(colour, unit) if t == 0 else kept
            ahead = jnp.where(lane == NZ - 1, 0.0, roll(centre, -1, 1))
            behind = jnp.where(lane == 0, start, roll(centre, 1, 1))
            total = x_sum + around(centre, beyond) + ahead + behind
            source = taken(colour, unit, "source", t)
            driving.append(source + weight * total)
            if store is not None:
                store[places[unit], t] = driving[t]
        if store is not None:
            return
        for s in range(T):
            value = taken(colour, unit, "inverse", T * s) * driving[0]
            for t in range(1, T):
                value = value + taken(colour, unit, "inverse", T * s + t) * driving[t]
            put(colour, unit, s, value)

    def combustor(colour, unit):
        before = None
        started = from_partial(colour, unit)
        current = None if started else planes(colour, unit, 0)
        flag = valid(unit)

        def finish(t, total):
            value = total / (6.0 + taken(colour, unit, "diagonal", t))
            if flag is not None:
                value = jnp.where(flag, value, 0.0)
            put(colour, unit, t, value)

        for t in range(T):
            if started:
                finish(t, finished(unit, t, None))
                continue
            after = planes(colour, unit, t + 1) if t + 1 < T else None
            centre, beyond, x_sum, _ = current
            edge_ahead = 0.0 if after is None else roll(after[0], -1, 1)
            edge_behind = 0.0 if before is None else roll(before, 1, 1)
            ahead = jnp.where(lane == NZ - 1, edge_ahead, roll(centre, -1, 1))
            behind = jnp.where(lane == 0, edge_behind, roll(centre, 1, 1))
            total = x_sum + around(centre, beyond) + ahead + behind
            total = taken(colour, unit, "source", t) + total
            if store is not None:
                store[places[unit], t] = total
            else:
                finish(t, total)
            before, current = centre, after

    return combustor, turbine


def by_section(place, two, units):
    def run(step):
        for colour, unit in units:
            step(colour, unit)

    pl.when(place.section == 0)(functools.partial(run, two[0]))
    pl.when(place.section != 0)(functools.partial(run, two[1]))


FIRST_COLOUR = [(0, unit) for unit in ((1, 0), (2, 0), (1, 1), (2, 1), "ring")]


def sweep_kernel(
    begins, ends, weights, sources, diagonal, inverse, ring, za, ya, zb, yb, back, inflow, *rest
):
    place = Place()
    odd_x, odd_y, exit_side = place.odd_x, place.odd_y, place.exit_side
    even = even_mask(NZ)
    if begins:
        fields, r2, r1, *outs = rest
        y2, y1 = za, ya
    else:
        kept, near, partial, y2, y1, *outs = rest
    if ends:
        out, u0, u1, second = outs
    else:
        first_sent, second_sent, u0, u1 = outs
    if begins:
        kept, partial = u0, None
    else:
        u1 = Halves(near, u1)
    own, edge = OWN, EDGE
    own_rows, own_rows_z = (lax.broadcasted_iota(jnp.int32, (8, width), 0) for width in (NZ, ZT))

    def beside(tile, rows, at):
        first, second = y1[tile, rows, at], y2[tile, rows, at]
        low, high = jnp.where(odd_y == 1, first, second), jnp.where(odd_y == 1, second, first)
        return low, high

    whole = slice(0, NZ)
    for t in range(T):
        if begins:
            a, b = r1[t], r2[t]
            u1[t, 0, own] = jnp.where(odd_x == 1, a, b)
            u1[t, 3, own] = jnp.where(odd_x == 1, b, a)
            for k in (0, 1):
                u1[t, k + 1, own] = packed(fields[t, 2 * k], fields[t, 2 * k + 1], even, 1)
                u0[t, k + 1, own] = packed(fields[t, 2 * k], fields[t, 2 * k + 1], even, 0)
            tile, at = T + t // 4, slice(t % 4 * ZT, (t % 4 + 1) * ZT)
            a, b = r1[tile, :, at], r2[tile, :, at]
            u0[t, 0, own, :ZT] = jnp.where(odd_x == 1, a, b)
            u0[t, 3, own, :ZT] = jnp.where(odd_x == 1, b, a)
        low, high = beside(t // 2, slice(0, 8), whole)
        for k in (0, 1):
            base = 4 * (t % 2) + 2 * k
            u1[t, k + 1, edge] = jnp.where(own_rows < 2, roll(high, -base, 0), roll(low, 6 - base, 0))
            if begins:
                row, at = 4 + 2 * k + t // 4, slice(t % 4 * ZT, (t % 4 + 1) * ZT)
                above, below = beside(3, slice(row, row + 1), at)
                u0[t, k + 1, edge, :ZT] = jnp.where(own_rows_z < 4, below, above)
        above, below = beside(4, slice(t, t + 1), whole)
        corner = jnp.where(own_rows < 4, below, above)
        u1[t, 0, edge] = corner
        u1[t, 3, edge] = corner

    @pl.when(exit_side)
    def _():
        for t in range(T):
            u1[t, 3, edge] = back[t, edge]
            if begins:
                u1[t, 3, own] = back[t, own]

    pair_1, pair_2 = 2 - odd_x, 1 + odd_x

    def put(colour, unit, t, value):
        if unit == "ring":
            u0[t, 0, own] = value
            u0[t, 3, own] = jnp.where(exit_side, back[t, own], value)
        elif colour == 1 and ends:
            second[t, unit[0] - 1] = value
        elif colour == 1:
            (first_sent if unit[0] is pair_1 else second_sent)[t] = value
        else:
            (u0, u1)[colour][t, unit[0], own if unit[1] == 0 else edge] = value

    two = steps(place, weights, sources, diagonal, inverse, ring, ya, za, yb, zb, back, inflow, u0, u1, kept, put, partial)
    by_section(place, two, FIRST_COLOUR)
    if not ends:
        by_section(place, two, [(1, (pair_2, 0)), (1, (pair_1, 0))])
        return
    by_section(place, two, [(1, (1, 0)), (1, (2, 0))])
    for t in range(T):
        for k in (0, 1):
            a, b = u0[t, k + 1, own], second[t, k]
            out[t, 2 * k] = jnp.where(even, a, b)
            out[t, 2 * k + 1] = jnp.where(even, b, a)


def sums_kernel(weights, sources, diagonal, inverse, ring, back, inflow, m1, m2, kept, r2, r1, near, sums):
    place = Place()
    odd_x, exit_side = place.odd_x, place.exit_side
    for t in range(T):
        for low, high, below, above in ((r2[t], r1[t], 0, 3), (m2[t], m1[t], 1, 2)):
            near[t, below] = jnp.where(odd_x == 1, high, low)
            near[t, above] = jnp.where(odd_x == 1, low, high)

    @pl.when(exit_side)
    def _():
        for t in range(T):
            near[t, 3] = back[t, OWN]

    ones = Halves(near, None)
    none = [None] * 4
    two = steps(place, weights, sources, diagonal, inverse, ring, *none, back, inflow, None, ones, kept, None, None, sums)
    by_section(place, two, [(0, (1, 0)), (0, (2, 0)), (0, "ring")])


def shape(*dims):
    return jax.ShapeDtypeStruct(dims, F32)


SMEM = pl.BlockSpec(memory_space=pltpu.SMEM)
VMEM = pl.BlockSpec(memory_space=pltpu.VMEM)
ANY = pl.BlockSpec(memory_space=pl.ANY)
HBM = pl.BlockSpec(memory_space=pltpu.HBM)


def call(kernel, outs, operands, out_specs=None, scratch=(), limit=24):
    return pl.pallas_call(
        kernel,
        out_shape=outs,
        in_specs=[spec for spec, _ in operands],
        out_specs=out_specs or [VMEM] * len(outs),
        scratch_shapes=list(scratch),
        compiler_params=pltpu.CompilerParams(vmem_limit_bytes=limit << 20),
    )(*[operand for _, operand in operands])


def far(array):
    return HBM, pltpu.with_memory_space_constraint(array, pltpu.HBM)


def swap(axis, pairs, array, turbine_only):
    if turbine_only:
        pairs = [(2 * i + 1, 2 * j + 1) for i, j in pairs]
        axis = (axis, "sa")
    return lax.ppermute(array, axis, pairs)


def inner_swap(axis, array, turbine_only=False):
    return swap(axis, [(i, i ^ 1) for i in range(lax.axis_size(axis))], array, turbine_only)


def outer_swap(axis, array, turbine_only=False):
    pairs = [(i, (i + 1 ^ 1) - 1) for i in range(1, lax.axis_size(axis) - 1)]
    return swap(axis, pairs, array, turbine_only)


def swaps(axis, first, second, turbine_only=False):
    second = outer_swap(axis, second, turbine_only)
    return inner_swap(axis, first, turbine_only), second


def chosen_places(tile):
    places = []
    for index in range(8 * tile, 8 * tile + 8):
        c, p, r = index // 64, index // 16 % 4, index % 16
        y = r if r < 12 else r - 16
        x = 2 * (p - 1) + (c if r % 2 == 0 else 1 - c)
        block = None
        if 0 <= x < CX and 0 <= y < CY:
            block = (0, x, y)
        elif x == -1 and 0 <= y < CY:
            block = (1, CX - 1, y)
        elif x == CX and 0 <= y < CY:
            block = (2, 0, y)
        elif 0 <= x < CX and y == -1:
            block = (3, x, CY - 1)
        elif 0 <= x < CX and y == CY:
            block = (4, x, 0)
        places.append(-1 if block is None else BLK * block[0] + CY * block[1] + block[2])
    return places


def shards(fields, sources, diagonal, block_inverse, coupling, donors, returns):
    values = fields[0]
    source = sources[0]
    rows_x, rows_y = lax.axis_size("gx"), lax.axis_size("gy")
    cells = rows_x * rows_y
    flat = [
        array.reshape(-1, CY, NZ // ZT, ZT).transpose(0, 2, 1, 3).reshape(-1, ZT)
        for array in (source, diagonal, block_inverse)
    ]
    near = (returns, values, *flat)
    messages = [(tiles, 8, NZ) for tiles in [VAL + XBULK] * 2 + [YBULK] * 2 + [4] * 2] + [(2 * CHUNK * cells, ZT)]
    m1, m2, yb, zb, s1, s2, payload = call(
        opening_kernel,
        [pltpu.HBM(dims, F32) for dims in messages],
        [far(array) for array in (donors.T, *near)],
        [HBM] * len(messages),
        [pltpu.SMEM(donors.T.shape, donors.dtype)]
        + [pltpu.VMEM(array.shape, array.dtype) for array in near]
        + [pltpu.VMEM(dims, F32) for dims in messages]
        + [pltpu.VMEM((cells, ZT), F32), pltpu.SemaphoreType.DMA((9,)), pltpu.SemaphoreType.DMA((21,))],
    )
    x1, x2 = swaps("gx", m1, m2)
    yb, zb = swaps("gy", yb, zb, turbine_only=True)
    arrived = lax.all_to_all(
        payload.reshape(2 * cells, 1, CHUNK * ZT), ("sa", "gx", "gy"), split_axis=0, concat_axis=0, tiled=True
    ).reshape(2 * CHUNK * cells, ZT)
    arrived, x1, x2 = lax.optimization_barrier((arrived, x1, x2))
    ya, za = call(
        first_corner_kernel,
        [shape(YHEAD, 8, NZ)] * 2,
        [far(m1), far(m2), (ANY, x2), (ANY, x1), far(s1), far(s2)],
        scratch=[pltpu.VMEM((4, VAL, 8, NZ), F32), pltpu.SemaphoreType.DMA((6,))],
    )
    ya, za = swaps("gy", ya, za)
    distant = (values, source, diagonal, block_inverse)
    made = call(
        interface_kernel,
        [shape(T, 16, NZ), shape(128, ZT), shape(8, ZT)]
        + [pltpu.VMEM(array.shape, F32) for array in distant[:3]]
        + [pltpu.VMEM((2, T * T, 2, 8, NZ), F32), pltpu.VMEM((COEF, 8, NZ), F32)],
        [(VMEM, arrived), (SMEM, pltpu.with_memory_space_constraint(coupling, pltpu.HBM)), (VMEM, x2), (VMEM, x1)]
        + [far(array) for array in (returns, *distant)],
        scratch=[
            pltpu.VMEM(returns.shape, returns.dtype),
            pltpu.VMEM(block_inverse.shape, F32),
            pltpu.SemaphoreType.DMA((5,)),
        ],
    )
    back, inflow, weights, values, source, diagonal, inverse, ring = made

    coefficients = [weights, source, diagonal, inverse, ring]
    given = [*coefficients, za, ya, zb, yb, back, inflow]
    block, half = pltpu.VMEM((T, 4, 16, NZ), F32), pltpu.VMEM((T, 4, 8, NZ), F32)
    state = [values, x2, x1]
    for sweep in range(SWEEPS):
        begins, ends = sweep == 0, sweep == SWEEPS - 1
        results = call(
            functools.partial(sweep_kernel, begins, ends),
            [shape(T, CX, CY, NZ)] if ends else [shape(T, 8, NZ)] * 2 + [shape(*block.shape)],
            [(VMEM, array) for array in (*given, *state)],
            scratch=([block] if ends else [])
            + [block if begins else half]
            + ([pltpu.VMEM((T, 2, 8, NZ), F32)] if ends else []),
            limit=40,
        )
        if ends:
            break
        m1, m2, u0 = results
        r1, r2 = swaps("gx", m1, m2)
        y1, y2 = call(corner_kernel, [shape(YVAL, 8, NZ)] * 2, [(VMEM, array) for array in (m1, m2, r2, r1)])
        y1, y2 = swaps("gy", y1, y2)
        near, sums = call(
            sums_kernel,
            [shape(*half.shape), shape(3, T, 8, NZ)],
            [(VMEM, array) for array in (*coefficients, back, inflow, m1, m2, u0, r2, r1)],
            limit=40,
        )
        state = [u0, near, sums, y2, y1]
    return results[0][None]


def solution(mesh):
    return jax.shard_map(
        shards,
        mesh=mesh,
        in_specs=(
            P("sa", None, "gx", "gy", None),
            P("sa", None, "gx", "gy", None),
            P(None, "gx", "gy", None),
            P(None, None, "gx", "gy", None),
            P(),
            P(),
            P("gy", None),
        ),
        out_specs=P("sa", None, "gx", "gy", None),
        check_vma=False,
    )
```

```python
import functools
import jax
import jax.numpy as jnp
from jax import lax
from jax.experimental import pallas as pl
from jax.experimental.pallas import tpu as pltpu
from jax.sharding import PartitionSpec as P

SWEEPS = 4
BLK = 32
T = 7
CX = 4
CY = 8
NZ = 512
ZT = 128
VAL = T + 2
COEF = T * T + T
XBULK = COEF // 2
MARKS = NZ // BLK
CHUNK = 2
YVAL = 5
YHEAD = YVAL + 4
YBULK = T * T // 4 + 1
F32 = jnp.float32


def iotas(width):
    sub = lax.broadcasted_iota(jnp.int32, (8, width), 0)
    lane = lax.broadcasted_iota(jnp.int32, (8, width), 1)
    return sub, lane


def even_mask(width):
    sub, lane = iotas(width)
    return (sub + lane) % 2 == 0


def roll(array, shift, axis):
    size = array.shape[axis]
    shift = shift % size
    return array if shift == 0 else pltpu.roll(array, shift, axis)


def packed(pair_low, pair_high, even, colour):
    return jnp.where(even, pair_low, pair_high) if colour == 0 else jnp.where(even, pair_high, pair_low)


class Place:
    def __init__(self):
        self.rows_x = lax.axis_size("gx")
        self.section, self.x, self.y = (lax.axis_index(axis) for axis in ("sa", "gx", "gy"))
        self.rows_y = lax.axis_size("gy")
        self.odd_x, self.odd_y = lax.rem(self.x, 2), lax.rem(self.y, 2)
        self.exit_side = (self.section == 0) & (self.x == self.rows_x - 1)


def store_message(ref, ones, zeros_first):
    for t in range(T):
        ref[t] = ones(t)
        ref[T + t // 4, :, (t % 4) * ZT : (t % 4 + 1) * ZT] = zeros_first(t)
    ref[T + 1, :, 3 * ZT :] = jnp.zeros((8, ZT), F32)


def wait_for(copies):
    for copy in copies:
        copy.wait()


def lines(ref, index, row):
    found = [ref[pl.ds(128 * index + 8 * z + row, 8, stride=32), :] for z in range(NZ // ZT)]
    return jnp.concatenate(found, axis=1)


def second_half(array):
    return roll(array, 4, 0)


def row_of_colour_0(raw, row, lane):
    return jnp.where((lane + row) % 2 == 0, raw, roll(raw, -1, 0))


def interleaved(first, second, sub):
    return jnp.where(sub % 2 == 0, first, roll(second, 1, 0))


def fill_payload(place, donors, returns, fields, payload, blocks):
    sub, lane = iotas(ZT)
    payload[...] = jnp.zeros_like(payload)
    cells = blocks.shape[0]

    @pl.when(place.exit_side)
    def _():
        for entry in range(cells):
            gy, block, slot = donors[0, entry], donors[1, entry], donors[2, entry]
            piece, row, column = block // 128, block % 128 // 16, block % 16
            start = pl.multiple_of(column // 4 * ZT, ZT)
            found = fields[piece, CX - 1, :, pl.ds(start, ZT)]
            found = pltpu.roll(pltpu.roll(found, (8 - row) % 8, 0), (ZT - column % 4 * BLK) % ZT, 1)
            blocks[pl.ds(slot, 1), :] = jnp.where((lane < BLK) & (gy == place.y), found, 0.0)[:1]
        marks = [jnp.zeros((8, ZT), F32)] * 2
        for t in range(T):
            line = jnp.broadcast_to(returns[0:1, t * ZT : (t + 1) * ZT], (8, ZT)).astype(F32)
            for n, row in enumerate((CY - 1, 0)):
                turned = roll(line, MARKS * (t - row), 1)
                marks[n] = jnp.where(lane // MARKS == t, turned, marks[n])
        for tile in range(cells // 8):
            for n in (0, 1):
                payload[pl.ds(8 * CHUNK * tile + n, 8, stride=CHUNK), :] = marks[n]
        tiles = cells // 8
        zero = jnp.zeros((8, ZT), F32)
        for tile in range(tiles):
            here = blocks[8 * tile : 8 * tile + 8]
            below = blocks[8 * tile - 8 : 8 * tile] if tile > 0 else zero
            above = blocks[8 * tile + 8 : 8 * tile + 16] if tile + 1 < tiles else zero
            left = jnp.where(sub == 0, 0.0, roll(here, 1, 0))
            right = jnp.where(sub == 7, 0.0, roll(here, -1, 0))
            wide = here + roll(below, BLK, 1) + roll(above, 2 * BLK, 1) + roll(left, 3 * BLK, 1)
            payload[pl.ds(CHUNK * (cells + 8 * tile), 8, stride=CHUNK), :] = wide
            payload[pl.ds(CHUNK * (cells + 8 * tile) + 1, 8, stride=CHUNK), :] = right

    @pl.when(place.section == 1)
    def _():
        inlet = jnp.zeros((8, ZT), F32)
        for x in range(CX):
            column = jnp.broadcast_to(fields[0, x, :, 0:1], (8, ZT))
            inlet = inlet + jnp.where(lane == CY * x + sub, column, 0.0)
        inlet = jnp.broadcast_to(jnp.sum(inlet, axis=0, keepdims=True), (8, ZT))
        for tile in range(cells // 8):
            payload[pl.ds(8 * CHUNK * tile, 8, stride=CHUNK), :] = inlet


def lines(ref, index, row):
    found = [ref[pl.ds(128 * index + 8 * z + row, 8, stride=32), :] for z in range(NZ // ZT)]
    return jnp.concatenate(found, axis=1)


def second_half(array):
    return roll(array, 4, 0)


def row_of_colour_0(raw, row, lane):
    return jnp.where((lane + row) % 2 == 0, raw, roll(raw, -1, 0))


def interleaved(first, second, sub):
    return jnp.where(sub % 2 == 0, first, roll(second, 1, 0))


def opening_kernel(
    donors_far,
    returns_far,
    fields_far,
    sources_far,
    diagonal_far,
    inverse_far,
    m1_far,
    m2_far,
    b1_far,
    b2_far,
    s1_far,
    s2_far,
    payload_far,
    donors,
    returns,
    fields,
    sources,
    diagonal,
    inverse,
    m1,
    m2,
    b1,
    b2,
    s1,
    s2,
    payload,
    blocks,
    sems,
    out_sems,
):
    pairs = (
        (donors_far, donors),
        (returns_far, returns),
        (fields_far, fields),
        (sources_far, sources),
        (diagonal_far, diagonal),
    )
    bounds = [0, 12, 24, 36, T * T]
    pieces = [slice(CX * NZ // ZT * CY * a, CX * NZ // ZT * CY * b) for a, b in zip(bounds, bounds[1:])]
    pairs += tuple((inverse_far.at[piece], inverse.at[piece]) for piece in pieces)
    loads = [pltpu.make_async_copy(far, near, sems.at[n]) for n, (far, near) in enumerate(pairs)]
    for load in loads:
        load.start()
    place = Place()
    sends = []

    def send(*refs):
        for near, far, at in refs:
            copy = pltpu.make_async_copy(near.at[at], far.at[at], out_sems.at[len(sends)])
            copy.start()
            sends.append(copy)

    wait_for(loads[:3])
    section, odd, odd_y = place.section, place.odd_x, place.odd_y == 1
    even, even_z = even_mask(NZ), even_mask(ZT)
    for ref, pair in ((m1, 1 - odd), (m2, odd)):
        store_message(
            ref,
            lambda t: packed(fields[t, 2 * pair], fields[t, 2 * pair + 1], even, 1),
            lambda t: packed(fields[t, 2 * pair, :, :ZT], fields[t, 2 * pair + 1, :, :ZT], even_z, 0),
        )
    send((m1, m1_far, slice(0, VAL)), (m2, m2_far, slice(0, VAL)))
    fill_payload(place, donors, returns, fields, payload, blocks)
    send((payload, payload_far, slice(None)))
    wait_for(loads[3:5])
    sub, lane = iotas(NZ)

    def plane_of(ref, index, plane):
        at = [pl.multiple_of(8 * (4 * (CX * index + plane) + z), 8) for z in range(NZ // ZT)]
        return jnp.concatenate([ref[pl.ds(start, 8), :] for start in at], axis=1)

    def coefficient(index, plane):
        if index >= T * T:
            return plane_of(sources, index - T * T, plane)
        raw = plane_of(inverse, index, plane)
        return jnp.where(section == 0, plane_of(diagonal, index, plane), raw) if index < T else raw

    def x_tiles(begin, end):
        for ref, far in ((m1, 1 - odd), (m2, odd)):
            wanted = (sub + lane + far) % 2 == 0
            plane = far * (CX - 1)
            for tile in range(begin, end):
                first, second = coefficient(2 * tile, plane), coefficient(2 * tile + 1, plane)
                ref[VAL + tile] = jnp.where(wanted, first, roll(second, 1, 0))
        at = slice(VAL + begin, VAL + end)
        send((m1, m1_far, at), (m2, m2_far, at))

    def inverse_rows(tile, row):
        if tile + 1 == YBULK:
            return row_of_colour_0(second_half(lines(inverse, T * T - 2, row)), row, lane)
        first, second = (row_of_colour_0(lines(inverse, 4 * tile + 2 * n, row), row, lane) for n in (0, 1))
        return interleaved(first, second, sub)

    def pair(index, row):
        if index + 1 < T:
            return lines(sources, index, row)
        if index + 1 == T:
            halves = second_half(lines(sources, index - 1, row)), second_half(lines(diagonal, 0, row))
            return jnp.where(sub < 4, halves[0], halves[1])
        return lines(diagonal, index - T, row)

    def other_rows(tile, row):
        first = row_of_colour_0(pair(4 * tile, row), row, lane)
        if tile == 3:
            return first
        return interleaved(first, row_of_colour_0(pair(4 * tile + 2, row), row, lane), sub)

    def y_tiles(refs, rows_of, begin, end):
        first, second, first_far, second_far = refs
        for tile in range(begin, end):
            down, up = rows_of(tile, 0), rows_of(tile, CY - 1)
            first[tile] = jnp.where(odd_y, down, up)
            second[tile] = jnp.where(odd_y, up, down)
        at = slice(begin, end)
        send((first, first_far, at), (second, second_far, at))

    y_tiles((s1, s2, s1_far, s2_far), other_rows, 0, 4)
    for n, (begin, end) in enumerate(zip(bounds, bounds[1:])):
        loads[5 + n].wait()
        last = end == T * T
        x_tiles(begin // 2, XBULK if last else end // 2)
        y_tiles((b1, b2, b1_far, b2_far), inverse_rows, begin // 4, YBULK if last else end // 4)
    wait_for(sends)


def corner_values(m1, m2, r1, r2, y1, y2):
    place = Place()
    odd_x, odd_y = place.odd_x == 1, place.odd_y == 1
    sub, lane = iotas(NZ)
    even = even_mask(NZ)
    tiles = {}
    for t in range(m1.shape[0]):
        a, b = m1[t], m2[t]
        own = jnp.where(odd_x, a, b), jnp.where(odd_x, b, a)
        for start in (0, 6):
            if t < T:
                base = 4 * (t % 2)
                rows = [roll(own[k], base + 2 * k - start, 0) for k in (0, 1)]
                both = jnp.where(sub < base + 2, rows[0], rows[1])
                tiles[start, t] = both
                c, d = r1[t], r2[t]
                from_low, from_high = jnp.where(odd_x, c, d), jnp.where(odd_x, d, c)
                ring = jnp.where(even, from_low, from_high)
                tiles[start, "ring", t] = roll(ring, t - (0 if start == 0 else CY - 1), 0)
            else:
                row = 0 if start == 0 else CY - 1
                rows = [roll(own[k], 4 + 2 * k + t - T - row, 0) for k in (0, 1)]
                tiles[start, t] = jnp.where(sub < 6, rows[0], rows[1])
    for tile in range(YVAL):
        sides = []
        for start in (0, 6):
            if tile < 3:
                sides.append(jnp.where(sub < 4, tiles[start, 2 * tile], tiles[start, 2 * tile + 1]))
            elif tile == 3:
                laid = tiles[start, T - 1]
                if m1.shape[0] > T:
                    firsts = jnp.where(sub % 2 == 0, tiles[start, T], tiles[start, T + 1])
                    laid = jnp.where(sub < 4, laid, firsts)
                sides.append(laid)
            else:
                laid = tiles[start, "ring", 0]
                for t in range(1, T):
                    laid = jnp.where(sub == t, tiles[start, "ring", t], laid)
                sides.append(laid)
        down, up = sides
        y1[tile] = jnp.where(odd_y, down, up)
        y2[tile] = jnp.where(odd_y, up, down)


def corner_kernel(m1, m2, r2, r1, y1, y2):
    corner_values(m1, m2, r1, r2, y1, y2)


def first_corner_kernel(m1, m2, r2, r1, s1, s2, y1, y2, heads, sems):
    pairs = [(ref.at[:VAL], heads.at[n]) for n, ref in enumerate((m1, m2, r1, r2))]
    pairs += [(s1, y1.at[YVAL:YHEAD]), (s2, y2.at[YVAL:YHEAD])]
    copies = [pltpu.make_async_copy(far, near, sems.at[n]) for n, (far, near) in enumerate(pairs)]
    for copy in copies:
        copy.start()
    wait_for(copies)
    corner_values(*[heads.at[n] for n in range(4)], y1, y2)


def interface_kernel(
    blocks,
    coupling,
    x2,
    x1,
    returns_far,
    fields_far,
    sources_far,
    diagonal_far,
    inverse_far,
    back,
    inflow,
    weights,
    fields,
    sources,
    diagonal,
    chosen,
    ring,
    returns,
    inverse,
    sems,
):
    pairs = [
        (returns_far, returns),
        (inverse_far, inverse),
        (fields_far, fields),
        (sources_far, sources),
        (diagonal_far, diagonal),
    ]
    copies = [pltpu.make_async_copy(far, near, sems.at[n]) for n, (far, near) in enumerate(pairs)]
    for copy in copies:
        copy.start()
    place = Place()
    back[...] = jnp.zeros_like(back)
    cells = blocks.shape[0] // (2 * CHUNK)

    def summed(n):
        total = jnp.zeros((8, ZT), F32)
        for tile in range(cells // 8):
            total = total + blocks[pl.ds(8 * CHUNK * tile + n, 8, stride=CHUNK), :]
        return jnp.broadcast_to(jnp.sum(total, axis=0, keepdims=True), (8, ZT))

    first, second = summed(0), summed(1)
    sub, lane = iotas(ZT)
    weight = jnp.zeros((8, ZT), F32)
    for t in range(T):
        weight = jnp.where(sub == t, coupling[t], weight)
    weights[...] = weight
    for row in range(16):
        found = jnp.full((8, ZT), -1, jnp.int32)
        for r, target in enumerate(chosen_places(row)):
            found = jnp.where(sub == r, target, found)
        parts = jnp.where(lane == found, first, 0.0) + jnp.where(lane + ZT == found, second, 0.0)
        inflow[8 * row : 8 * row + 8, :] = jnp.broadcast_to(jnp.sum(parts, axis=1, keepdims=True), (8, ZT))

    copies[0].wait()

    @pl.when(place.exit_side)
    def _():
        table = blocks[pl.ds(CHUNK * cells, cells, stride=CHUNK), :]
        sub, lane = iotas(ZT)

        def marks_of(y, n):
            line = jnp.zeros((8, ZT), F32)
            for tile in range(place.rows_y // 8):
                at = CHUNK * (cells - place.rows_y + 8 * tile) + n
                line = line + jnp.where(sub + 8 * tile == y, blocks[pl.ds(at, 8, stride=CHUNK), :], 0.0)
            line = jnp.broadcast_to(jnp.sum(line, axis=0, keepdims=True), (8, ZT))
            laid = line
            for t in range(1, T):
                laid = jnp.where(sub == t, roll(line, -MARKS * t, 1), laid)
            return laid

        high, low = marks_of(place.y + 1, 1), marks_of(place.y - 1, 0)
        slots = lax.broadcasted_iota(jnp.int32, (8, cells), 1).astype(F32)
        column = lax.broadcasted_iota(jnp.int32, table.shape, 1)
        spots = [jnp.where(column // BLK == q, roll(table, q * BLK, 1), 0.0) for q in range(ZT // BLK)]
        wanted = []
        for t in range(T):
            line = jnp.broadcast_to(returns[0:1, t * ZT : (t + 1) * ZT], (8, ZT))
            spread = line
            for y in range(1, CY):
                spread = jnp.where(sub == y, roll(line, -y * MARKS, 1), spread)
            wanted.append(spread.astype(F32))
        wanted += [high, low]
        for tile in range(NZ // ZT):
            laid = jnp.zeros((8 * len(wanted), ZT), F32)
            for q in range(ZT // BLK):
                block = tile * (ZT // BLK) + q
                match = jnp.concatenate([want[:, block : block + 1] == slots for want in wanted], axis=0)
                laid = laid + jnp.dot(
                    match.astype(F32), spots[q], precision=lax.Precision.HIGHEST, preferred_element_type=F32
                )
            at = slice(tile * ZT, (tile + 1) * ZT)
            for t in range(T):
                back[t, 0:8, at] = laid[8 * t : 8 * t + 8]
                back[t, 8:9, at] = laid[8 * T + t : 8 * T + t + 1]
                back[t, 15:16, at] = laid[8 * T + 8 + t : 8 * T + 9 + t]

    even = even_mask(NZ)
    wide, long = iotas(NZ)
    ring_mask = (wide + long + place.odd_x) % 2 == 0
    for index in range(COEF):
        tile = VAL + index // 2
        if index % 2 == 0:
            ring[index] = jnp.where(ring_mask, x1[tile], x2[tile])
        else:
            ring[index] = roll(jnp.where(ring_mask, x2[tile], x1[tile]), -1, 0)
    copies[1].wait()
    for index in range(T * T):
        for k in (0, 1):
            a, b = (inverse[index // T, index % T, 2 * k + n] for n in (0, 1))
            chosen[0, index, k] = packed(a, b, even, 0)
            chosen[1, index, k] = packed(a, b, even, 1)
    wait_for(copies[2:])


OWN, EDGE = slice(0, 8), slice(8, 16)


class Halves:
    def __init__(self, own, edge):
        self.own, self.edge = own, edge

    def __getitem__(self, at):
        t, p, rows = at
        return (self.own if rows is OWN else self.edge)[t, p]

    def __setitem__(self, at, value):
        t, p, rows = at
        (self.own if rows is OWN else self.edge)[t, p] = value


def steps(place, weights, sources, diagonal, inverse, ring, ya, za, yb, zb, back, inflow, u0, u1, kept, put, partial=None, store=None):
    odd_x, odd_y, exit_side = place.odd_x, place.odd_y, place.exit_side
    even, even_z = even_mask(NZ), even_mask(ZT)
    sub, lane = iotas(NZ)
    own, edge = OWN, EDGE

    zero = jnp.zeros((8, NZ), F32)
    places = {(1, 0): 0, (2, 0): 1, "ring": 2}

    def beyond_ring(t):
        return jnp.where(even, u1[t, 0, edge], u1[t, 3, edge])

    def finished(unit, t, weight):
        beyond = beyond_ring(t) if unit == "ring" else u1[t, unit[0], edge]
        halo = around(zero, beyond)
        return partial[places[unit], t] + (halo if weight is None else weight * halo)

    def from_partial(colour, unit):
        return partial is not None and colour == 0 and unit in places

    def around(centre, beyond):
        up = roll(jnp.where(sub == 0, beyond, centre), -1, 0)
        down = roll(jnp.where(sub == 7, beyond, centre), 1, 0)
        return up + down

    def planes(colour, unit, t):
        old, new = (kept, u1) if colour == 0 else (u1, u0)
        if unit == "ring":
            centre = jnp.where(even, new[t, 0, own], new[t, 3, own])
            beyond = zero if store is not None else beyond_ring(t)
            x_sum = jnp.where(even, new[t, 3, own] + new[t, 2, own], new[t, 0, own] + new[t, 1, own])
            return centre, beyond, x_sum, jnp.where(even, old[t, 3, own], old[t, 0, own])
        p, rows = unit
        here, other = (own, edge) if rows == 0 else (edge, own)
        centre = new[t, p, here]
        beyond = zero if store is not None else new[t, p, other]
        below, above = new[t, p - 1, here], new[t, p + 1, here]
        x_sum = centre + (jnp.where(even, below, above) if colour == 0 else jnp.where(even, above, below))
        return centre, beyond, x_sum, old[t, p, here]

    def inflow_of(colour, unit):
        base = 64 * colour
        if unit == "ring":
            values = jnp.where(even_z, inflow[base + 48 : base + 56], inflow[base : base + 8])
        else:
            start = base + 16 * unit[0] + 8 * unit[1]
            values = inflow[pl.ds(pl.multiple_of(start, 8), 8)]
        return jnp.concatenate([values] * (NZ // ZT), axis=1)

    edge_mask = jnp.where(sub == 7, 1, 0) == odd_y

    def of_edge(first, second, tile, index, p):
        tile, row = tile + index // 4, 4 * (index % 2) + 2 * (p - 1) + index % 4 // 2
        return jnp.where(edge_mask, first[tile, row : row + 1], second[tile, row : row + 1])

    def taken(colour, unit, kind, index):
        if unit == "ring":
            return ring[T * T + index if kind == "source" else index]
        p, rows = unit
        if rows == 0:
            if kind == "inverse":
                return inverse[colour, index, p - 1]
            raw = (sources if kind == "source" else diagonal).at[index]
            return packed(raw[2 * p - 2], raw[2 * p - 1], even, colour)
        if kind == "inverse":
            return of_edge(yb, zb, 0, index, p)
        return of_edge(ya, za, YVAL, index if kind == "source" else T + index, p)

    def valid(unit):
        if unit == "ring":
            return jnp.where(even, place.rows_x - 1 - place.x, place.x) > 0
        if unit[1] == 0:
            return None
        return jnp.where(sub == 7, place.y, place.rows_y - 1 - place.y) > 0

    def turbine(colour, unit):
        driving = []
        for t in range(T):
            weight = jnp.concatenate([jnp.broadcast_to(weights[t : t + 1], (8, ZT))] * (NZ // ZT), axis=1)
            if from_partial(colour, unit):
                driving.append(finished(unit, t, weight))
                continue
            centre, beyond, x_sum, kept = planes(colour, unit, t)
            start = inflow_of(colour, unit) if t == 0 else kept
            ahead = jnp.where(lane == NZ - 1, 0.0, roll(centre, -1, 1))
            behind = jnp.where(lane == 0, start, roll(centre, 1, 1))
            total = x_sum + around(centre, beyond) + ahead + behind
            source = taken(colour, unit, "source", t)
            driving.append(source + weight * total)
            if store is not None:
                store[places[unit], t] = driving[t]
        if store is not None:
            return
        for s in range(T):
            value = taken(colour, unit, "inverse", T * s) * driving[0]
            for t in range(1, T):
                value = value + taken(colour, unit, "inverse", T * s + t) * driving[t]
            put(colour, unit, s, value)

    def combustor(colour, unit):
        before = None
        started = from_partial(colour, unit)
        current = None if started else planes(colour, unit, 0)
        flag = valid(unit)

        def finish(t, total):
            value = total / (6.0 + taken(colour, unit, "diagonal", t))
            if flag is not None:
                value = jnp.where(flag, value, 0.0)
            put(colour, unit, t, value)

        for t in range(T):
            if started:
                finish(t, finished(unit, t, None))
                continue
            after = planes(colour, unit, t + 1) if t + 1 < T else None
            centre, beyond, x_sum, _ = current
            edge_ahead = 0.0 if after is None else roll(after[0], -1, 1)
            edge_behind = 0.0 if before is None else roll(before, 1, 1)
            ahead = jnp.where(lane == NZ - 1, edge_ahead, roll(centre, -1, 1))
            behind = jnp.where(lane == 0, edge_behind, roll(centre, 1, 1))
            total = x_sum + around(centre, beyond) + ahead + behind
            total = taken(colour, unit, "source", t) + total
            if store is not None:
                store[places[unit], t] = total
            else:
                finish(t, total)
            before, current = centre, after

    return combustor, turbine


def by_section(place, two, units):
    def run(step):
        for colour, unit in units:
            step(colour, unit)

    pl.when(place.section == 0)(functools.partial(run, two[0]))
    pl.when(place.section != 0)(functools.partial(run, two[1]))


FIRST_COLOUR = [(0, unit) for unit in ((1, 0), (2, 0), (1, 1), (2, 1), "ring")]


def sweep_kernel(
    begins, ends, weights, sources, diagonal, inverse, ring, za, ya, yb, zb, back, inflow, *rest
):
    place = Place()
    odd_x, odd_y, exit_side = place.odd_x, place.odd_y, place.exit_side
    even = even_mask(NZ)
    if begins:
        fields, r2, r1, *outs = rest
        y2, y1 = za, ya
    else:
        kept, near, partial, y2, y1, *outs = rest
    if ends:
        out, u0, u1, second = outs
    else:
        first_sent, second_sent, u0, u1 = outs
    if begins:
        kept, partial = u0, None
    else:
        u1 = Halves(near, u1)
    own, edge = OWN, EDGE
    own_rows, own_rows_z = (lax.broadcasted_iota(jnp.int32, (8, width), 0) for width in (NZ, ZT))

    def beside(tile, rows, at):
        first, second = y1[tile, rows, at], y2[tile, rows, at]
        low, high = jnp.where(odd_y == 1, first, second), jnp.where(odd_y == 1, second, first)
        return low, high

    whole = slice(0, NZ)
    for t in range(T):
        if begins:
            a, b = r1[t], r2[t]
            u1[t, 0, own] = jnp.where(odd_x == 1, a, b)
            u1[t, 3, own] = jnp.where(odd_x == 1, b, a)
            for k in (0, 1):
                u1[t, k + 1, own] = packed(fields[t, 2 * k], fields[t, 2 * k + 1], even, 1)
                u0[t, k + 1, own] = packed(fields[t, 2 * k], fields[t, 2 * k + 1], even, 0)
            tile, at = T + t // 4, slice(t % 4 * ZT, (t % 4 + 1) * ZT)
            a, b = r1[tile, :, at], r2[tile, :, at]
            u0[t, 0, own, :ZT] = jnp.where(odd_x == 1, a, b)
            u0[t, 3, own, :ZT] = jnp.where(odd_x == 1, b, a)
        low, high = beside(t // 2, slice(0, 8), whole)
        for k in (0, 1):
            base = 4 * (t % 2) + 2 * k
            u1[t, k + 1, edge] = jnp.where(own_rows < 2, roll(high, -base, 0), roll(low, 6 - base, 0))
            if begins:
                row, at = 4 + 2 * k + t // 4, slice(t % 4 * ZT, (t % 4 + 1) * ZT)
                above, below = beside(3, slice(row, row + 1), at)
                u0[t, k + 1, edge, :ZT] = jnp.where(own_rows_z < 4, below, above)
        above, below = beside(4, slice(t, t + 1), whole)
        corner = jnp.where(own_rows < 4, below, above)
        u1[t, 0, edge] = corner
        u1[t, 3, edge] = corner

    @pl.when(exit_side)
    def _():
        for t in range(T):
            u1[t, 3, edge] = back[t, edge]
            if begins:
                u1[t, 3, own] = back[t, own]

    pair_1, pair_2 = 2 - odd_x, 1 + odd_x

    def put(colour, unit, t, value):
        if unit == "ring":
            u0[t, 0, own] = value
            u0[t, 3, own] = jnp.where(exit_side, back[t, own], value)
        elif colour == 1 and ends:
            second[t, unit[0] - 1] = value
        elif colour == 1:
            (first_sent if unit[0] is pair_1 else second_sent)[t] = value
        else:
            (u0, u1)[colour][t, unit[0], own if unit[1] == 0 else edge] = value

    two = steps(place, weights, sources, diagonal, inverse, ring, ya, za, yb, zb, back, inflow, u0, u1, kept, put, partial)
    by_section(place, two, FIRST_COLOUR)
    if not ends:
        by_section(place, two, [(1, (pair_2, 0)), (1, (pair_1, 0))])
        return
    by_section(place, two, [(1, (1, 0)), (1, (2, 0))])
    for t in range(T):
        for k in (0, 1):
            a, b = u0[t, k + 1, own], second[t, k]
            out[t, 2 * k] = jnp.where(even, a, b)
            out[t, 2 * k + 1] = jnp.where(even, b, a)


def sums_kernel(weights, sources, diagonal, inverse, ring, back, inflow, m1, m2, kept, r2, r1, near, sums):
    place = Place()
    odd_x, exit_side = place.odd_x, place.exit_side
    for t in range(T):
        for low, high, below, above in ((r2[t], r1[t], 0, 3), (m2[t], m1[t], 1, 2)):
            near[t, below] = jnp.where(odd_x == 1, high, low)
            near[t, above] = jnp.where(odd_x == 1, low, high)

    @pl.when(exit_side)
    def _():
        for t in range(T):
            near[t, 3] = back[t, OWN]

    ones = Halves(near, None)
    none = [None] * 4
    two = steps(place, weights, sources, diagonal, inverse, ring, *none, back, inflow, None, ones, kept, None, None, sums)
    by_section(place, two, [(0, (1, 0)), (0, (2, 0)), (0, "ring")])


def shape(*dims):
    return jax.ShapeDtypeStruct(dims, F32)


SMEM = pl.BlockSpec(memory_space=pltpu.SMEM)
VMEM = pl.BlockSpec(memory_space=pltpu.VMEM)
ANY = pl.BlockSpec(memory_space=pl.ANY)
HBM = pl.BlockSpec(memory_space=pltpu.HBM)


def call(kernel, outs, operands, out_specs=None, scratch=(), limit=24):
    return pl.pallas_call(
        kernel,
        out_shape=outs,
        in_specs=[spec for spec, _ in operands],
        out_specs=out_specs or [VMEM] * len(outs),
        scratch_shapes=list(scratch),
        compiler_params=pltpu.CompilerParams(vmem_limit_bytes=limit << 20),
    )(*[operand for _, operand in operands])


def far(array):
    return HBM, pltpu.with_memory_space_constraint(array, pltpu.HBM)


def swap(axis, pairs, array, turbine_only):
    if turbine_only:
        pairs = [(2 * i + 1, 2 * j + 1) for i, j in pairs]
        axis = (axis, "sa")
    return lax.ppermute(array, axis, pairs)


def inner_swap(axis, array, turbine_only=False):
    return swap(axis, [(i, i ^ 1) for i in range(lax.axis_size(axis))], array, turbine_only)


def outer_swap(axis, array, turbine_only=False):
    pairs = [(i, (i + 1 ^ 1) - 1) for i in range(1, lax.axis_size(axis) - 1)]
    return swap(axis, pairs, array, turbine_only)


def swaps(axis, first, second, turbine_only=False):
    second = outer_swap(axis, second, turbine_only)
    return inner_swap(axis, first, turbine_only), second


def chosen_places(tile):
    places = []
    for index in range(8 * tile, 8 * tile + 8):
        c, p, r = index // 64, index // 16 % 4, index % 16
        y = r if r < 12 else r - 16
        x = 2 * (p - 1) + (c if r % 2 == 0 else 1 - c)
        block = None
        if 0 <= x < CX and 0 <= y < CY:
            block = (0, x, y)
        elif x == -1 and 0 <= y < CY:
            block = (1, CX - 1, y)
        elif x == CX and 0 <= y < CY:
            block = (2, 0, y)
        elif 0 <= x < CX and y == -1:
            block = (3, x, CY - 1)
        elif 0 <= x < CX and y == CY:
            block = (4, x, 0)
        places.append(-1 if block is None else BLK * block[0] + CY * block[1] + block[2])
    return places


def shards(fields, sources, diagonal, block_inverse, coupling, donors, returns):
    values = fields[0]
    source = sources[0]
    rows_x, rows_y = lax.axis_size("gx"), lax.axis_size("gy")
    cells = rows_x * rows_y
    flat = [
        array.reshape(-1, CY, NZ // ZT, ZT).transpose(0, 2, 1, 3).reshape(-1, ZT)
        for array in (source, diagonal, block_inverse)
    ]
    near = (returns, values, *flat)
    messages = [(tiles, 8, NZ) for tiles in [VAL + XBULK] * 2 + [YBULK] * 2 + [4] * 2] + [(2 * CHUNK * cells, ZT)]
    m1, m2, yb, zb, s1, s2, payload = call(
        opening_kernel,
        [pltpu.HBM(dims, F32) for dims in messages],
        [far(array) for array in (donors.T, *near)],
        [HBM] * len(messages),
        [pltpu.SMEM(donors.T.shape, donors.dtype)]
        + [pltpu.VMEM(array.shape, array.dtype) for array in near]
        + [pltpu.VMEM(dims, F32) for dims in messages]
        + [pltpu.VMEM((cells, ZT), F32), pltpu.SemaphoreType.DMA((9,)), pltpu.SemaphoreType.DMA((21,))],
    )
    x1, x2 = swaps("gx", m1, m2)
    yb, zb = swaps("gy", yb, zb, turbine_only=True)
    arrived = lax.all_to_all(
        payload.reshape(2 * cells, 1, CHUNK * ZT), ("sa", "gx", "gy"), split_axis=0, concat_axis=0, tiled=True
    ).reshape(2 * CHUNK * cells, ZT)
    arrived, x1, x2 = lax.optimization_barrier((arrived, x1, x2))
    ya, za = call(
        first_corner_kernel,
        [shape(YHEAD, 8, NZ)] * 2,
        [far(m1), far(m2), (ANY, x2), (ANY, x1), far(s1), far(s2)],
        scratch=[pltpu.VMEM((4, VAL, 8, NZ), F32), pltpu.SemaphoreType.DMA((6,))],
    )
    ya, za = swaps("gy", ya, za)
    distant = (values, source, diagonal, block_inverse)
    made = call(
        interface_kernel,
        [shape(T, 16, NZ), shape(128, ZT), shape(8, ZT)]
        + [pltpu.VMEM(array.shape, F32) for array in distant[:3]]
        + [pltpu.VMEM((2, T * T, 2, 8, NZ), F32), pltpu.VMEM((COEF, 8, NZ), F32)],
        [(VMEM, arrived), (SMEM, pltpu.with_memory_space_constraint(coupling, pltpu.HBM)), (VMEM, x2), (VMEM, x1)]
        + [far(array) for array in (returns, *distant)],
        scratch=[
            pltpu.VMEM(returns.shape, returns.dtype),
            pltpu.VMEM(block_inverse.shape, F32),
            pltpu.SemaphoreType.DMA((5,)),
        ],
    )
    back, inflow, weights, values, source, diagonal, inverse, ring = made

    coefficients = [weights, source, diagonal, inverse, ring]
    given = [*coefficients, za, ya, yb, zb, back, inflow]
    block, half = pltpu.VMEM((T, 4, 16, NZ), F32), pltpu.VMEM((T, 4, 8, NZ), F32)
    state = [values, x2, x1]
    for sweep in range(SWEEPS):
        begins, ends = sweep == 0, sweep == SWEEPS - 1
        results = call(
            functools.partial(sweep_kernel, begins, ends),
            [shape(T, CX, CY, NZ)] if ends else [shape(T, 8, NZ)] * 2 + [shape(*block.shape)],
            [(VMEM, array) for array in (*given, *state)],
            scratch=([block] if ends else [])
            + [block if begins else half]
            + ([pltpu.VMEM((T, 2, 8, NZ), F32)] if ends else []),
            limit=40,
        )
        if ends:
            break
        m1, m2, u0 = results
        r1, r2 = swaps("gx", m1, m2)
        y1, y2 = call(corner_kernel, [shape(YVAL, 8, NZ)] * 2, [(VMEM, array) for array in (m1, m2, r2, r1)])
        y1, y2 = swaps("gy", y1, y2)
        near, sums = call(
            sums_kernel,
            [shape(*half.shape), shape(3, T, 8, NZ)],
            [(VMEM, array) for array in (*coefficients, back, inflow, m1, m2, u0, r2, r1)],
            limit=40,
        )
        state = [u0, near, sums, y2, y1]
    return results[0][None]


def solution(mesh):
    return jax.shard_map(
        shards,
        mesh=mesh,
        in_specs=(
            P("sa", None, "gx", "gy", None),
            P("sa", None, "gx", "gy", None),
            P(None, "gx", "gy", None),
            P(None, None, "gx", "gy", None),
            P(),
            P(),
            P("gy", None),
        ),
        out_specs=P("sa", None, "gx", "gy", None),
        check_vma=False,
    )
```
